128 devices in a mesh: group: 4 (over z), front: 32 (over y, x, core).
Axes of the slice: x: 4, y: 4, z: 4, core: 2. Of those that a mesh axis runs over, the one named last changes fastest.
Arguments:
- front_matrix: float32 [4, 8192, 8192], P('group', 'front'), as said below
- child_tiles: bfloat16 [4, 4096, 128, 128], P('group', 'front'), may hold values from -4 to 4
- tile_route: int32 [4, 4096, 1], P('group', 'front'), may hold values from 0 to 103; in each aligned block of 128 rows (0 to 127, 128 to 255, ..., all dimensions but the last counted through in order) at most 2 rows name the same one
- tile_row: int32 [4, 4096], P('group', 'front'), may hold values from 0 to 1
- tile_col: int32 [4, 4096], P('group', 'front'), may hold values from 0 to 63
Outputs:
- factor: float32 [4, 8192, 1536], P('group', 'front')
- schur: float32 [4, 8192, 6656], P('group', 'front')
The draws below stay inside these ranges and needn't reach their ends.
Inputs may be any that keep to these rules, and one draw needn't show every extreme that they name: Each front_matrix block is symmetric and positive definite. `tile_route`: among the 128 tiles of one device no value appears more than 2 times.
All inputs are finite; a program needn't handle non-finite values.
Results may differ from the reference program's by a relative error of at most 0.022.
Values may be sent and summed in bfloat16 or wider, within the bound.
A program may use at most 192 MiB of HBM per device.

```python
import math
import jax
import jax.numpy as jnp
import numpy as np
from jax import lax

PW = 256
TB = 128
PANELS = 6
CT = 128
NF = 8192
DEST = 104
CAP = 2
N_GROUP = 4
N_FRONT = 32


def draw_front_matrix(key, part):
    key = jax.random.fold_in(key, 11)
    key_spots, key_weights, key_ridge = jax.random.split(key, 3)
    spots = jax.random.uniform(key_spots, (N_GROUP, 3, NF), jnp.float32)
    weights = jnp.exp(jax.random.uniform(key_weights, (N_GROUP, NF), jnp.float32, jnp.log(0.5), jnp.log(2.0)))
    ridge = jax.random.uniform(key_ridge, (N_GROUP, NF), jnp.float32, 0.5, 2.0)
    distance = jnp.zeros((N_GROUP, NF, NF), jnp.float32)
    for c in range(3):
        coord = spots[:, c, :]
        distance = distance + (coord[:, :, None] - coord[:, None, :]) ** 2
    kernel = jnp.exp(distance * (-1.0 / (2.0 * 0.15 * 0.15))) * weights[:, :, None] * weights[:, None, :]
    places = jnp.arange(NF)
    diagonal = places[:, None] == places[None, :]
    return kernel + jnp.where(diagonal[None, :, :], ridge[:, :, None], 0.0)


def plant(array, key, low, high):
    shape = array.shape
    index_at = [jax.random.randint(jax.random.fold_in(key, axis), (), 0, shape[axis]) for axis in range(len(shape))]
    array = array.at[tuple(index_at)].set(low)
    longest = shape.index(max(shape))
    index_at[longest] = (index_at[longest] + 1) % shape[longest]
    return array.at[tuple(index_at)].set(high)


def block_levels(stream_key, dims, pieces, smallest, largest):
    factor_of, own = 1.0, jax.random.fold_in(stream_key, 6)
    for position, shards_of in pieces:
        steps = jnp.exp(jax.random.uniform(jax.random.fold_in(own, position), (shards_of,), jnp.float32, smallest / len(pieces), largest / len(pieces)))
        factor_of = factor_of * jnp.repeat(steps, dims[position] // shards_of).reshape([-1 if axis == position else 1 for axis in range(len(dims))])
    return factor_of


def deal_out(stream_key, own, number, rows, amount, top, reach, skew):
    ranking = jax.random.permutation(stream_key, amount)
    packed, common = shares(amount, rows * top, reach, skew, True), shares(amount, rows * top, reach, skew, False)
    places = jnp.arange(amount)

    def named(tallies, rotation):
        used = int((tallies > 0).sum())
        fixed = max(1, used // 4)
        moved = fixed + (places - fixed + rotation * (used - fixed)) % max(1, amount - fixed)
        return jnp.zeros((amount,), jnp.int32).at[ranking[jnp.where(places < fixed, places, moved)]].set(jnp.asarray(tallies, jnp.int32))

    tallies = jnp.where(number % 4 == 0, named(packed, number // 4), named(common, number - number // 4 - 1))
    mixed = jax.random.permutation(jax.random.fold_in(own, 3), amount)
    donor, taker = mixed[0:amount // 2 * 2:2], mixed[1:amount // 2 * 2:2]
    slack = jnp.minimum(tallies[donor] - 1, reach - tallies[taker]) // 2
    slack = jnp.where((donor == ranking[0]) | (taker == ranking[0]) | (tallies[taker] == 0), 0, jnp.maximum(slack, 0))
    moved = jax.random.randint(jax.random.fold_in(own, 4), (amount // 2,), 0, 1 << 20) % (slack + 1)
    tallies = tallies.at[donor].add(-moved).at[taker].add(moved)
    labels = jnp.searchsorted(jnp.cumsum(tallies), jnp.arange(rows * top), side="right").astype(jnp.int32)
    grid = labels.reshape(top, rows).T
    grid = grid[jax.random.permutation(jax.random.fold_in(own, 1), rows)]
    rotation = jax.random.randint(jax.random.fold_in(own, 2), (rows, 1), 0, top)
    return jnp.take_along_axis(grid, (jnp.arange(top)[None, :] + rotation) % top, axis=1)


def shares(count, total, limit, slope, full):
    portions = [(1 << 20) // math.isqrt(rank ** slope) + 1 for rank in range(1, count + 1)]
    largest = limit if full else min(limit, max(-(-total // count), total * portions[0] // sum(portions)))
    least = 1 if total - largest >= count - 1 else 0
    given, surplus = [largest] + [least] * (count - 1), total - largest - least * (count - 1)
    while surplus > 0:
        movable = [i for i in range(1, count) if given[i] < largest] or [i for i in range(1, count) if given[i] < limit]
        mass, budget = sum([portions[i] for i in movable]), surplus
        for i in movable:
            addition = min(limit - given[i], max(1, budget * portions[i] // mass), surplus)
            given[i] = given[i] + addition
            surplus = surplus - addition
    return np.array(given)


def scatter_about(own_key, dims, deviation, bound, pieces=(), held_as=jnp.bfloat16):
    array = deviation * jax.random.normal(own_key, dims, jnp.float32)
    if pieces:
        array = array * block_levels(own_key, dims, pieces, -0.22, 0.18)
    return jnp.clip(array, -bound, bound).astype(held_as)


def setup_inputs(seed: int = 0) -> dict:
    key_of = jax.random.split(jax.random.key(seed), 6)
    front_matrix = draw_front_matrix(jax.random.fold_in(key_of[5], 71), 0)
    child_tiles = scatter_about(key_of[1], (N_GROUP, N_FRONT * CT, TB, TB), 0.5, 4.0, ((0, 4), (1, 32)))
    tile_route_keys = jax.random.split(jax.random.fold_in(key_of[2], 1), N_GROUP * (N_FRONT * CT) // CT)
    tile_route_turns = jax.random.permutation(jax.random.fold_in(key_of[2], 3), N_GROUP * (N_FRONT * CT) // CT)
    tile_route = jax.vmap(lambda own, number: deal_out(jax.random.fold_in(key_of[2], 2), own, number, CT, DEST, 1, CAP, 2))(tile_route_keys, tile_route_turns).reshape((N_GROUP, N_FRONT * CT, 1))
    tile_row = plant(jax.random.randint(key_of[3], (N_GROUP, N_FRONT * CT), 0, PW // TB), jax.random.fold_in(key_of[3], 1), 0, (PW // TB) - 1).astype(jnp.int32)
    tile_col = plant(jax.random.randint(key_of[4], (N_GROUP, N_FRONT * CT), 0, NF // TB), jax.random.fold_in(key_of[4], 1), 0, (NF // TB) - 1).astype(jnp.int32)
    return {"front_matrix": front_matrix, "child_tiles": child_tiles, "tile_route": tile_route, "tile_row": tile_row, "tile_col": tile_col}


def factor_front(assembled):
    pivots = PANELS * PW
    factor = jnp.zeros((NF, pivots), jnp.float32)
    lowbits = jnp.zeros((NF, pivots), jnp.bfloat16)
    for k in range(PANELS):
        first = k * PW
        last = first + PW
        row_bits = lowbits[first:last].astype(jnp.float32)
        pivot = assembled[first:last, first:last] - jnp.dot(row_bits, row_bits.T, precision=lax.Precision.HIGHEST)
        lower_block = jnp.linalg.cholesky(pivot)
        current = assembled[last:, first:last] - jnp.dot(lowbits[last:].astype(jnp.float32), row_bits.T, precision=lax.Precision.HIGHEST)
        solved = lax.linalg.triangular_solve(lower_block, current, left_side=False, lower=True, transpose_a=True)
        factor = factor.at[first:last, first:last].set(lower_block).at[last:, first:last].set(solved)
        lowbits = factor.astype(jnp.bfloat16)
    trailing = lowbits[pivots:].astype(jnp.float32)
    lower_part = assembled[pivots:, pivots:] - jnp.dot(trailing, trailing.T, precision=lax.Precision.HIGHEST)
    schur = jnp.concatenate([jnp.zeros((pivots, NF - pivots), jnp.float32), lower_part], axis=0)
    return (factor, schur)

def reference(front_matrix, child_tiles, tile_route, tile_row, tile_col):
    groups = front_matrix.shape[0]
    tail = N_FRONT - PANELS
    target = tile_route.reshape(-1).astype(jnp.int32)
    dest_group = target // tail
    dest_tile = (PANELS + target % tail) * (PW // TB) + tile_row.reshape(-1)
    columns = tile_col.reshape(-1)
    blocks = front_matrix.reshape(groups, NF // TB, TB, NF // TB, TB)
    blocks = blocks.at[dest_group, dest_tile, :, columns, :].add(child_tiles.reshape(-1, TB, TB).astype(jnp.float32))
    assembled = blocks.reshape(groups, NF, NF)
    factors = []
    schurs = []
    for g in range(groups):
        one_factor, one_schur = factor_front(assembled[g])
        factors.append(one_factor)
        schurs.append(one_schur)
    return (jnp.stack(factors), jnp.stack(schurs))
```

```python
import functools

import jax
import jax.numpy as jnp
from jax import lax
from jax.experimental import pallas as pl
from jax.experimental.pallas import tpu as pltpu
from jax.sharding import PartitionSpec as P

PANELS = 6
PW = 256
TB = 128
SUB = 16
SLOTS = 2
MIB = 1 << 20


def dot_nt(a, b, precision=None):
    return lax.dot_general(
        a, b, (((1,), (1,)), ((), ())), precision=precision, preferred_element_type=jnp.float32
    )


def dot_nn(a, b, precision=None):
    return lax.dot_general(
        a, b, (((1,), (0,)), ((), ())), precision=precision, preferred_element_type=jnp.float32
    )


def halves(a):
    high = a.astype(jnp.bfloat16)
    low = (a - high.astype(jnp.float32)).astype(jnp.bfloat16)
    return high, low


def dot_tn_split(a, b):
    ah, al = halves(a)
    bh, bl = halves(b)
    left = jnp.concatenate([ah, ah, al], axis=0)
    right = jnp.concatenate([bh, bl, bh], axis=0)
    return lax.dot_general(
        left, right, (((0,), (0,)), ((), ())), preferred_element_type=jnp.float32
    )


def dot_nt_split(a, b):
    ah, al = halves(a)
    bh, bl = halves(b)
    left = jnp.concatenate([ah, ah, al], axis=1)
    right = jnp.concatenate([bh, bl, bh], axis=1)
    return dot_nt(left, right)


def dot_nn_split(a, b):
    ah, al = halves(a)
    bh, bl = halves(b)
    left = jnp.concatenate([ah, ah, al], axis=1)
    right = jnp.concatenate([bh, bl, bh], axis=0)
    return dot_nn(left, right)


def chol_inv(block):
    n = TB
    parts = SUB // 8
    lane = lax.broadcasted_iota(jnp.int32, (8, n), 1)
    sub = lax.broadcasted_iota(jnp.int32, (8, n), 0)
    rows = [block[8 * i : 8 * i + 8] for i in range(n // 8)]
    upper = []
    inverse = []
    for p in range(n // SUB):
        first = p * parts
        left = p * SUB
        panel = rows[first : first + parts]
        unit = [jnp.where(lane == sub + (left + 8 * h), 1.0, 0.0) for h in range(parts)]
        spread = [
            [jnp.broadcast_to(panel[h][:, left + j : left + j + 1], (8, n)) for h in range(parts)]
            for j in range(SUB)
        ]
        scale = [jnp.zeros((8, n), jnp.float32) for _ in range(parts)]
        for j in range(SUB):
            at, s = divmod(j, 8)
            inv = lax.rsqrt(jnp.broadcast_to(spread[j][at][s : s + 1], (8, n)))
            mult = [None] * parts
            for h in range(at, parts):
                mult[h] = spread[j][h] * inv
                if h == at:
                    mult[h] = jnp.where(sub > s, mult[h], 0.0)
            for target in [panel, unit] + spread[j + 1 :]:
                row = jnp.broadcast_to(target[at][s : s + 1], (8, n)) * inv
                for h in range(at, parts):
                    target[h] = target[h] - mult[h] * row
            scale[at] = jnp.where(sub == s, inv, scale[at])
        inside = (lane >= left) & (lane < left + SUB)
        ups = []
        full = []
        for h in range(parts):
            up = panel[h] * scale[h]
            mixed = jnp.where(inside, unit[h] * scale[h], up)
            inverse.append(jnp.where(lane < left + SUB, mixed, 0.0))
            upper.append(jnp.where(lane >= left, up, 0.0))
            ups.append(up)
            full.append(mixed)
        if left + SUB < n:
            ups = jnp.concatenate(ups, axis=0)
            full = jnp.concatenate(full, axis=0)
            change = dot_tn_split(ups[:, left + SUB :], full)
            for k, i in enumerate(range(first + parts, n // 8)):
                rows[i] = jnp.where(inside, 0.0, rows[i]) - change[8 * k : 8 * k + 8]
    return jnp.concatenate(upper, axis=0), jnp.concatenate(inverse, axis=0)


def pivot_kernel(me_ref, lead_ref, bits_ref, inverse_ref, own_ref, work, sem):
    copy = pltpu.make_async_copy(lead_ref, work, sem)
    copy.start()
    copy.wait()
    high = lax.Precision.HIGHEST

    def at(i):
        return pl.ds(pl.multiple_of(i * PW, PW), PW)

    def panel(k, carry):
        low = pl.ds(pl.multiple_of(k * PW, TB), TB)
        top = pl.ds(pl.multiple_of(k * PW + TB, TB), TB)
        u1, w1 = chol_inv(work[low, low])
        l21 = dot_nt(work[top, low], w1, high)
        u2, w2 = chol_inv(work[top, top] - dot_nt(l21, l21, high))
        w21 = -dot_nn(w2, dot_nn(l21, w1, high), high)
        work[low, low] = u1.T
        work[low, top] = jnp.zeros((TB, TB), jnp.float32)
        work[top, low] = l21
        work[top, top] = u2.T
        inverse_ref[k, :TB, :TB] = w1
        inverse_ref[k, :TB, TB:] = jnp.zeros((TB, TB), jnp.float32)
        inverse_ref[k, TB:, :TB] = w21
        inverse_ref[k, TB:, TB:] = w2

        def below(i, c):
            solved = dot_nt_split(work[at(i), at(k)], inverse_ref[k])
            work[at(i), at(k)] = solved
            bits_ref[at(i), at(k)] = solved.astype(jnp.bfloat16)
            return c

        lax.fori_loop(k + 1, PANELS, below, 0)

        def column(j, c):
            def row(i, c2):
                work[at(i), at(j)] -= dot_nt(bits_ref[at(i), at(k)], bits_ref[at(j), at(k)])
                return c2

            return lax.fori_loop(j, PANELS, row, c)

        lax.fori_loop(k + 1, PANELS, column, 0)
        return carry

    lax.fori_loop(0, PANELS, panel, 0)
    me = jnp.minimum(me_ref[0], PANELS - 1)

    def out(j, c):
        own_ref[:, at(j)] = jnp.where(j <= me, work[at(me), at(j)], 0.0)
        return c

    lax.fori_loop(0, PANELS, out, 0)


def factor_pivots(me, lead):
    order = PANELS * PW
    return pl.pallas_call(
        pivot_kernel,
        grid_spec=pltpu.PrefetchScalarGridSpec(
            num_scalar_prefetch=1,
            grid=(1,),
            in_specs=[pl.BlockSpec(memory_space=pl.ANY)],
            out_specs=[
                pl.BlockSpec((order, order), lambda i, m: (0, 0)),
                pl.BlockSpec((PANELS, PW, PW), lambda i, m: (0, 0, 0)),
                pl.BlockSpec((PW, order), lambda i, m: (0, 0)),
            ],
            scratch_shapes=[pltpu.VMEM((order, order), jnp.float32), pltpu.SemaphoreType.DMA],
        ),
        out_shape=[
            jax.ShapeDtypeStruct((order, order), jnp.bfloat16),
            jax.ShapeDtypeStruct((PANELS, PW, PW), jnp.float32),
            jax.ShapeDtypeStruct((PW, order), jnp.float32),
        ],
        compiler_params=pltpu.CompilerParams(vmem_limit_bytes=48 * MIB),
        cost_estimate=pl.CostEstimate(
            flops=80_000_000_000, bytes_accessed=20_000_000, transcendentals=0
        ),
        name="factor_pivots",
    )(me, lead)


def pack_kernel(pick_ref, tiles_ref, outbox_ref, sem):
    count = outbox_ref.shape[0]

    def send(i, c):
        pltpu.make_async_copy(tiles_ref.at[pick_ref[i]], outbox_ref.at[i], sem).start()
        return c

    lax.fori_loop(0, count, send, 0)
    pltpu.make_async_copy(outbox_ref, outbox_ref, sem).wait()


def pack_tiles(pick, tiles):
    count = pick.shape[0]
    return pl.pallas_call(
        pack_kernel,
        grid_spec=pltpu.PrefetchScalarGridSpec(
            num_scalar_prefetch=1,
            grid=(1,),
            in_specs=[pl.BlockSpec(tiles.shape, lambda i, p: (0, 0, 0))],
            out_specs=pl.BlockSpec(memory_space=pl.ANY),
            scratch_shapes=[pltpu.SemaphoreType.DMA],
        ),
        out_shape=jax.ShapeDtypeStruct((count, TB, TB), jnp.bfloat16),
        compiler_params=pltpu.CompilerParams(vmem_limit_bytes=32 * MIB),
        name="pack_tiles",
    )(pick, tiles)


CHUNK = 32


def solve_kernel(
    tags_ref, me_ref, front_ref, inbox_ref, bits_ref, inverse_ref, own_ref,
    factor_ref, rows_ref, rest_ref, work, landed, sems, rest_sem,
):
    pivots = PANELS * PW
    count = inbox_ref.shape[0]
    chunks = count // CHUNK
    fill = pltpu.make_async_copy(front_ref, work, sems.at[chunks])
    fill.start()

    def fetch(c):
        part = pl.ds(c * CHUNK, CHUNK)
        return pltpu.make_async_copy(inbox_ref.at[part], landed.at[part], sems.at[c])

    for c in range(chunks):
        fetch(c).start()
    fill.wait()

    for c in range(chunks):
        fetch(c).wait()

        def add(i, carry):
            code = tags_ref[i]

            @pl.when(code >= 0)
            def _():
                place = (
                    pl.ds(pl.multiple_of((code // 64) * TB, TB), TB),
                    pl.ds(pl.multiple_of((code % 64) * TB, TB), TB),
                )
                work[place] += landed[i].astype(jnp.float32)

            return carry

        lax.fori_loop(c * CHUNK, (c + 1) * CHUNK, add, 0)
    leave = pltpu.make_async_copy(work.at[:, pl.ds(pivots, rest_ref.shape[1])], rest_ref, rest_sem)
    leave.start()
    below = me_ref[0] >= PANELS
    for k in range(PANELS):
        at = slice(k * PW, (k + 1) * PW)
        current = work[:, at]
        if k:
            current = current - dot_nt(rows_ref[:, : k * PW], bits_ref[at, : k * PW])
        solved = dot_nt_split(current, inverse_ref[k])
        rows_ref[:, at] = solved.astype(jnp.bfloat16)
        factor_ref[:, at] = jnp.where(below, solved, own_ref[:, at])
    leave.wait()


def solve_rows(tags, me, front, inbox, bits, inverse, own):
    order = front.shape[1]
    pivots = PANELS * PW
    whole = lambda shape: pl.BlockSpec(shape, lambda i, t, m: (0,) * len(shape))
    count = inbox.shape[0]
    return pl.pallas_call(
        solve_kernel,
        grid_spec=pltpu.PrefetchScalarGridSpec(
            num_scalar_prefetch=2,
            grid=(1,),
            in_specs=[
                pl.BlockSpec(memory_space=pl.ANY),
                pl.BlockSpec(memory_space=pl.ANY),
                whole(bits.shape),
                whole(inverse.shape),
                whole(own.shape),
            ],
            out_specs=[
                whole((PW, pivots)),
                whole((PW, pivots)),
                pl.BlockSpec(memory_space=pl.ANY),
            ],
            scratch_shapes=[
                pltpu.VMEM((PW, order), jnp.float32),
                pltpu.VMEM(inbox.shape, jnp.bfloat16),
                pltpu.SemaphoreType.DMA((count // CHUNK + 1,)),
                pltpu.SemaphoreType.DMA,
            ],
        ),
        out_shape=[
            jax.ShapeDtypeStruct((PW, pivots), jnp.float32),
            jax.ShapeDtypeStruct((PW, pivots), jnp.bfloat16),
            jax.ShapeDtypeStruct((PW, order - pivots), jnp.float32),
        ],
        compiler_params=pltpu.CompilerParams(vmem_limit_bytes=56 * MIB),
        name="solve_rows",
    )(tags, me, front, inbox, bits, inverse, own)


def schur_kernel(me_ref, rest_ref, rows_ref, others_ref, out_ref):
    term = dot_nt(rows_ref[...], others_ref[...])
    out_ref[...] = jnp.where(me_ref[0] >= PANELS, rest_ref[...] - term, 0.0)


def schur_rows(me, rest, rows, gathered):
    width = rest.shape[1]
    return pl.pallas_call(
        schur_kernel,
        grid_spec=pltpu.PrefetchScalarGridSpec(
            num_scalar_prefetch=1,
            grid=(width // PW,),
            in_specs=[
                pl.BlockSpec((PW, PW), lambda j, m: (0, j)),
                pl.BlockSpec(rows.shape, lambda j, m: (0, 0)),
                pl.BlockSpec((PW, rows.shape[1]), lambda j, m: (j + PANELS, 0)),
            ],
            out_specs=pl.BlockSpec((PW, PW), lambda j, m: (0, j)),
        ),
        out_shape=jax.ShapeDtypeStruct(rest.shape, jnp.float32),
        compiler_params=pltpu.CompilerParams(vmem_limit_bytes=32 * MIB),
        name="schur_rows",
    )(me, rest, rows, gathered)


def lead_everywhere(work, fronts):
    pivots = PANELS * PW
    share = PW // fronts
    pieces = lax.all_to_all(
        work[:, :pivots].reshape(fronts, share, pivots), "front", 0, 0, tiled=True
    )
    packed = jnp.concatenate(
        [
            jnp.concatenate(
                [pieces[i, :, : (i + 1) * PW], pieces[PANELS - 1 - i, :, : (PANELS - i) * PW]],
                axis=1,
            )
            for i in range(PANELS // 2)
        ],
        axis=0,
    )
    everyone = lax.all_gather(packed, "front", axis=0).reshape(fronts, PANELS // 2, share, -1)
    lead = [None] * PANELS
    for i in range(PANELS // 2):
        both = everyone[:, i].reshape(fronts * share, -1)
        for at, block in ((i, both[:, : (i + 1) * PW]), (PANELS - 1 - i, both[:, (i + 1) * PW :])):
            lead[at] = jnp.pad(block, ((0, 0), (0, pivots - block.shape[1])))
    return jnp.concatenate(lead, axis=0)


def on_device(front_matrix, child_tiles, tile_route, tile_row, tile_col):
    work = front_matrix[0]
    tiles = child_tiles[0]
    count = tiles.shape[0]
    groups = lax.axis_size("group")
    fronts = lax.axis_size("front")
    devices = groups * fronts
    tail = fronts - PANELS
    me = lax.axis_index("front")
    mine = lax.axis_index("group") * fronts + me
    lead = lead_everywhere(work, fronts)

    target = tile_route[0, :, 0]
    destination = target // tail * fronts + PANELS + target % tail
    code = (destination * 2 + tile_row[0]) * 64 + tile_col[0]
    positions = jnp.arange(count, dtype=jnp.int32)
    meets = destination[None, :] == jnp.arange(devices, dtype=jnp.int32)[:, None]
    first = jnp.min(jnp.where(meets, positions[None, :], count), axis=1)
    last = jnp.max(jnp.where(meets, positions[None, :], -1), axis=1)
    pick = jnp.stack([jnp.where(first < count, first, 0), jnp.maximum(last, 0)], axis=1)
    codes = lax.all_gather(code, ("group", "front"), axis=0).reshape(devices, count)
    here = codes // 128 == mine
    from_first = jnp.min(jnp.where(here, positions[None, :], count), axis=1)
    from_last = jnp.max(jnp.where(here, positions[None, :], -1), axis=1)
    label = codes % 128
    tag_first = jnp.max(
        jnp.where(positions[None, :] == from_first[:, None], label, -1), axis=1
    )
    tag_last = jnp.max(
        jnp.where(
            (positions[None, :] == from_last[:, None]) & (from_last != from_first)[:, None],
            label,
            -1,
        ),
        axis=1,
    )
    tags = jnp.stack([tag_first, tag_last], axis=1).reshape(devices * SLOTS)

    outbox = pack_tiles(pick.reshape(devices * SLOTS), tiles)
    inbox = lax.all_to_all(
        outbox.reshape(devices, SLOTS, TB, TB), ("group", "front"), 0, 0, tiled=True
    ).reshape(devices * SLOTS, TB, TB)

    self = me.astype(jnp.int32).reshape(1)
    bits, inverse, own = factor_pivots(self, lead)
    factor, rows, rest = solve_rows(tags, self, work, inbox, bits, inverse, own)
    gathered = lax.all_gather(rows, "front", axis=0, tiled=True)
    schur = schur_rows(self, rest, rows, gathered)
    return (factor[None], schur[None])


def solution(mesh):
    return jax.shard_map(
        on_device,
        mesh=mesh,
        in_specs=(
            P("group", "front", None),
            P("group", "front", None, None),
            P("group", "front", None),
            P("group", "front"),
            P("group", "front"),
        ),
        out_specs=(P("group", "front", None), P("group", "front", None)),
        check_vma=False,
    )
```

```python
import functools

import jax
import jax.numpy as jnp
from jax import lax
from jax.experimental import pallas as pl
from jax.experimental.pallas import tpu as pltpu
from jax.sharding import PartitionSpec as P

PANELS = 6
PW = 256
TB = 128
SUB = 16
SLOTS = 2
MIB = 1 << 20


def dot_nt(a, b, precision=None):
    return lax.dot_general(
        a, b, (((1,), (1,)), ((), ())), precision=precision, preferred_element_type=jnp.float32
    )


def dot_nn(a, b, precision=None):
    return lax.dot_general(
        a, b, (((1,), (0,)), ((), ())), precision=precision, preferred_element_type=jnp.float32
    )


def halves(a):
    high = a.astype(jnp.bfloat16)
    low = (a - high.astype(jnp.float32)).astype(jnp.bfloat16)
    return high, low


def dot_tn_split(a, b):
    ah, al = halves(a)
    bh, bl = halves(b)
    left = jnp.concatenate([ah, ah, al], axis=0)
    right = jnp.concatenate([bh, bl, bh], axis=0)
    return lax.dot_general(
        left, right, (((0,), (0,)), ((), ())), preferred_element_type=jnp.float32
    )


def dot_nt_split(a, b):
    ah, al = halves(a)
    bh, bl = halves(b)
    left = jnp.concatenate([ah, ah, al], axis=1)
    right = jnp.concatenate([bh, bl, bh], axis=1)
    return dot_nt(left, right)


def dot_nn_split(a, b):
    ah, al = halves(a)
    bh, bl = halves(b)
    left = jnp.concatenate([ah, ah, al], axis=1)
    right = jnp.concatenate([bh, bl, bh], axis=0)
    return dot_nn(left, right)


def chol_inv(block):
    n = TB
    parts = SUB // 8
    lane = lax.broadcasted_iota(jnp.int32, (8, n), 1)
    sub = lax.broadcasted_iota(jnp.int32, (8, n), 0)
    rows = [block[8 * i : 8 * i + 8] for i in range(n // 8)]
    upper = []
    inverse = []
    for p in range(n // SUB):
        first = p * parts
        left = p * SUB
        panel = rows[first : first + parts]
        unit = [jnp.where(lane == sub + (left + 8 * h), 1.0, 0.0) for h in range(parts)]
        spread = [
            [jnp.broadcast_to(panel[h][:, left + j : left + j + 1], (8, n)) for h in range(parts)]
            for j in range(SUB)
        ]
        scale = [jnp.zeros((8, n), jnp.float32) for _ in range(parts)]
        for j in range(SUB):
            at, s = divmod(j, 8)
            inv = lax.rsqrt(jnp.broadcast_to(spread[j][at][s : s + 1], (8, n)))
            mult = [None] * parts
            for h in range(at, parts):
                mult[h] = spread[j][h] * inv
                if h == at:
                    mult[h] = jnp.where(sub > s, mult[h], 0.0)
            for target in [panel, unit] + spread[j + 1 :]:
                row = jnp.broadcast_to(target[at][s : s + 1], (8, n)) * inv
                for h in range(at, parts):
                    target[h] = target[h] - mult[h] * row
            scale[at] = jnp.where(sub == s, inv, scale[at])
        inside = (lane >= left) & (lane < left + SUB)
        ups = []
        full = []
        for h in range(parts):
            up = panel[h] * scale[h]
            mixed = jnp.where(inside, unit[h] * scale[h], up)
            inverse.append(jnp.where(lane < left + SUB, mixed, 0.0))
            upper.append(jnp.where(lane >= left, up, 0.0))
            ups.append(up)
            full.append(mixed)
        if left + SUB < n:
            ups = jnp.concatenate(ups, axis=0)
            full = jnp.concatenate(full, axis=0)
            change = dot_tn_split(ups[:, left + SUB :], full)
            for k, i in enumerate(range(first + parts, n // 8)):
                rows[i] = jnp.where(inside, 0.0, rows[i]) - change[8 * k : 8 * k + 8]
    return jnp.concatenate(upper, axis=0), jnp.concatenate(inverse, axis=0)


def share_segments(i):
    half_width = (PANELS + 1) * PW // 2
    group = min(i, PANELS - 1 - i)
    begin = 0 if i < PANELS // 2 else (group + 1) * PW
    end = begin + (i + 1) * PW
    found = []
    for half in range(2):
        low, high = max(begin, half * half_width), min(end, (half + 1) * half_width)
        if low < high:
            found.append((half, group, low - half * half_width, low - begin, high - low))
    return found


MESH = pl.DeviceIdType.MESH
SIDE = 4
SENDS = 64
MOVES = {"b+": (0, 3), "b-": (0, 1), "a+": (3, 0), "a-": (1, 0)}


def when(condition, action):
    if condition is None:
        action()
    else:
        pl.when(condition)(action)


class Ring:
    def __init__(self, skip):
        me = lax.axis_index("front")
        self.me = me
        self.core = me % 2
        x, y = (me // 2) % SIDE, me // (2 * SIDE)
        self.a = jnp.where(self.core == 0, y, x)
        self.b = jnp.where(self.core == 0, x, y)
        self.skip = skip
        self.sends = 0
        self.late = []
        self.peer = {"s": me + 1 - 2 * self.core}
        for name, (da, db) in MOVES.items():
            self.peer[name] = 2 * self.chip(SIDE - da, SIDE - db) + self.core

    def chip(self, da, db, other=False):
        core = 1 - self.core if other else self.core
        a, b = (self.b, self.a) if other else (self.a, self.b)
        a, b = (a + da) % SIDE, (b + db) % SIDE
        return jnp.where(core == 0, a * SIDE + b, b * SIDE + a)

    def live(self, da, db, other=False):
        return self.chip(da, db, other) * 2 >= self.skip if self.skip else None

    def greet(self):
        barrier = pltpu.get_barrier_semaphore()
        for peer in self.peer.values():
            pl.semaphore_signal(barrier, inc=1, device_id={"front": peer}, device_id_type=MESH)
        return barrier

    def gather(self, own, out, ring_recv, side_recv, own_recv, local_sem, send_sem):
        core = self.core

        def piece(da, db, s, other=False):
            half = 1 - core if other else core
            chip = self.chip(da, db, other)
            if s is None:
                return out.at[pl.ds(2 * chip, 2), half]
            return out.at[2 * chip + s, half]

        def remote(source, target, recv, to, condition):
            k = self.sends
            self.sends += 1

            def make():
                return pltpu.make_async_remote_copy(
                    src_ref=source,
                    dst_ref=target,
                    send_sem=send_sem.at[k],
                    recv_sem=recv,
                    device_id={"front": self.peer[to]},
                    device_id_type=MESH,
                )

            when(condition, lambda: make().start())
            self.late.append((condition, lambda: make().wait_send()))

        def arrive(ref, sem, condition):
            def wait():
                pltpu.make_async_remote_copy(
                    src_ref=ref,
                    dst_ref=ref,
                    send_sem=send_sem.at[0],
                    recv_sem=sem,
                    device_id={"front": self.peer["s"]},
                    device_id_type=MESH,
                ).wait_recv()

            when(condition, wait)

        def give(da, db, s, to):
            ref = piece(da, db, s)
            at = 0 if s is None else s
            if to == "s":
                recv = side_recv.at[da, db, at]
            else:
                recv = ring_recv.at[(da + MOVES[to][0]) % SIDE, (db + MOVES[to][1]) % SIDE, at]
            remote(ref, ref, recv, to, self.live(da, db))

        here = self.live(0, 0)
        mine = pltpu.make_async_copy(own(core), piece(0, 0, core), local_sem.at[0])
        rest = pltpu.make_async_copy(own(1 - core), piece(0, 0, core, True), local_sem.at[1])
        when(here, mine.start)
        when(here, rest.start)
        remote(own(1 - core), piece(0, 0, core, True), own_recv.at[0], "s", here)
        remote(own(core), piece(0, 0, core), own_recv.at[1], "s", here)
        when(here, mine.wait)
        arrive(piece(0, 0, 1 - core), own_recv.at[0], here)
        for to in MOVES:
            give(0, 0, None, to)
        steps = [
            (0, 3, None, [(0, "b+"), (None, "a+"), (None, "a-")]),
            (0, 1, None, [(1, "b-"), (None, "a+"), (None, "a-")]),
            (3, 0, None, [(0, "a+")]),
            (1, 0, None, [(1, "a-")]),
            (0, 2, 0, [(0, "a+"), (0, "a-")]),
            (0, 2, 1, [(1, "a+"), (1, "a-")]),
            (3, 3, None, [(0, "a+")]),
            (1, 3, None, [(1, "a-")]),
            (3, 1, None, [(0, "a+")]),
            (1, 1, None, [(1, "a-")]),
            (2, 0, 0, []),
            (2, 0, 1, []),
            (3, 2, 0, [(0, "a+")]),
            (1, 2, 1, [(1, "a-")]),
            (3, 2, 1, []),
            (1, 2, 0, []),
            (2, 3, 0, []),
            (2, 3, 1, []),
            (2, 1, 0, []),
            (2, 1, 1, []),
            (2, 2, 0, []),
            (2, 2, 1, []),
        ]
        for da, db, s, onward in steps:
            arrive(piece(da, db, s), ring_recv.at[da, db, s or 0], self.live(da, db))
            for part, to in onward:
                give(da, db, part, to)
            give(da, db, s, "s")
        arrive(piece(0, 0, 1 - core, True), own_recv.at[1], here)
        when(here, rest.wait)
        for da, db, s, _ in steps:
            arrive(piece(da, db, s, True), side_recv.at[da, db, s or 0], self.live(da, db, True))
        for condition, wait in self.late:
            when(condition, wait)


RING_SEMS = [
    pltpu.SemaphoreType.DMA((SIDE, SIDE, 2)),
    pltpu.SemaphoreType.DMA((SIDE, SIDE, 2)),
    pltpu.SemaphoreType.DMA((2,)),
    pltpu.SemaphoreType.DMA((2,)),
    pltpu.SemaphoreType.DMA((SENDS,)),
]


def gather_kernel(rows_ref, out_ref, *sems):
    ring = Ring(PANELS)
    pl.semaphore_wait(ring.greet(), len(ring.peer))
    ring.gather(lambda h: rows_ref.at[h], out_ref, *sems)


def gather_rows(rows):
    fronts = lax.axis_size("front")
    halved = rows.reshape(2, rows.shape[0] // 2, rows.shape[1])
    out = pl.pallas_call(
        gather_kernel,
        in_specs=[pl.BlockSpec(memory_space=pl.ANY)],
        out_specs=pl.BlockSpec(memory_space=pl.ANY),
        out_shape=jax.ShapeDtypeStruct((fronts,) + halved.shape, rows.dtype),
        scratch_shapes=RING_SEMS,
        compiler_params=pltpu.CompilerParams(collective_id=1, has_side_effects=True),
        name="gather_rows",
    )(halved)
    return out.reshape(fronts * rows.shape[0], rows.shape[1])


def spread_kernel(front_ref, out_ref, share, deal_recv, deal_send, *sems):
    fronts = out_ref.shape[0]
    ring = Ring(0)
    me = ring.me
    barrier = ring.greet()
    for i in range(PANELS):

        @pl.when(me != i)
        def _():
            pl.semaphore_signal(barrier, inc=1, device_id={"front": i}, device_id_type=MESH)

    @pl.when(me < PANELS)
    def _():
        pl.semaphore_wait(barrier, len(ring.peer) + fronts - 1)

    @pl.when(me >= PANELS)
    def _():
        pl.semaphore_wait(barrier, len(ring.peer))

    pieces = []
    for i in range(PANELS):
        for segment in share_segments(i):
            pieces.append((i, len(pieces)) + segment)

    def source(f, piece):
        i, _, _, _, _, column, width = piece
        return front_ref.at[pl.ds(pl.multiple_of(f * 8, 8), 8), pl.ds(column, width)]

    def target(piece):
        _, _, half, group, column, _, width = piece
        return share.at[half, pl.ds(group * 8, 8), pl.ds(column, width)]

    def far(f, piece):
        return pltpu.make_async_remote_copy(
            src_ref=source(f, piece),
            dst_ref=target(piece),
            send_sem=deal_send.at[piece[2], f],
            recv_sem=deal_recv.at[piece[1]],
            device_id={"front": f},
            device_id_type=MESH,
        )

    def near(piece):
        return pltpu.make_async_copy(source(me, piece), target(piece), deal_recv.at[piece[1]])

    for i in range(PANELS):
        mine = [piece for piece in pieces if piece[0] == i]

        @pl.when(me == i)
        def _():
            def deal(f, c):
                @pl.when(f != me)
                def _():
                    for piece in mine:
                        far(f, piece).start()

                return c

            lax.fori_loop(0, fronts, deal, 0)
            for piece in mine:
                near(piece).start()

    for piece in pieces:

        @pl.when(me == piece[0])
        def _():
            near(piece).wait()

        @pl.when(me != piece[0])
        def _():
            far(0, piece).wait_recv()

    ring.gather(lambda h: share.at[h], out_ref, *sems)
    for i in range(PANELS):
        mine = [piece for piece in pieces if piece[0] == i]

        @pl.when(me == i)
        def _():
            def done(f, c):
                @pl.when(f != me)
                def _():
                    for piece in mine:
                        far(f, piece).wait_send()

                return c

            lax.fori_loop(0, fronts, done, 0)


def spread_pivots(front):
    fronts = lax.axis_size("front")
    share = (2, PANELS // 2 * (PW // fronts), (PANELS + 1) * PW // 2)
    return pl.pallas_call(
        spread_kernel,
        in_specs=[pl.BlockSpec(memory_space=pl.ANY)],
        out_specs=pl.BlockSpec(memory_space=pl.ANY),
        out_shape=jax.ShapeDtypeStruct((fronts,) + share, jnp.float32),
        scratch_shapes=[
            pltpu.VMEM(share, jnp.float32),
            pltpu.SemaphoreType.DMA((9,)),
            pltpu.SemaphoreType.DMA((2, fronts)),
        ]
        + RING_SEMS,
        compiler_params=pltpu.CompilerParams(collective_id=2, has_side_effects=True),
        name="spread_pivots",
    )(front)


def pivot_kernel(me_ref, shares_ref, bits_ref, inverse_ref, own_ref, work, sem):
    high = lax.Precision.HIGHEST
    fronts = shares_ref.shape[0]
    for i in range(PANELS):
        for half, group, source, target, width in share_segments(i):
            pltpu.make_async_copy(
                shares_ref.at[:, half, pl.ds(group * 8, 8), pl.ds(source, width)],
                work.at[pl.ds(i * fronts, fronts), :, pl.ds(target, width)],
                sem,
            ).start()
    pltpu.make_async_copy(shares_ref, shares_ref, sem).wait()

    def cols(i):
        return pl.ds(pl.multiple_of(i * PW, PW), PW)

    def load(i, j):
        return work[pl.ds(i * 32, 32), :, cols(j)].reshape(PW, PW)

    def panel(k, carry):
        top = pl.ds(k * 32, 16)
        low = pl.ds(k * 32 + 16, 16)
        left = pl.ds(pl.multiple_of(k * PW, TB), TB)
        right = pl.ds(pl.multiple_of(k * PW + TB, TB), TB)
        u1, w1 = chol_inv(work[top, :, left].reshape(TB, TB))
        l21 = dot_nt(work[low, :, left].reshape(TB, TB), w1, high)
        u2, w2 = chol_inv(work[low, :, right].reshape(TB, TB) - dot_nt(l21, l21, high))
        w21 = -dot_nn(w2, dot_nn(l21, w1, high), high)
        work[top, :, left] = u1.T.reshape(16, 8, TB)
        work[top, :, right] = jnp.zeros((16, 8, TB), jnp.float32)
        work[low, :, left] = l21.reshape(16, 8, TB)
        work[low, :, right] = u2.T.reshape(16, 8, TB)
        inverse_ref[k, :TB, :TB] = w1
        inverse_ref[k, :TB, TB:] = jnp.zeros((TB, TB), jnp.float32)
        inverse_ref[k, TB:, :TB] = w21
        inverse_ref[k, TB:, TB:] = w2

        def below(i, c):
            solved = dot_nt_split(load(i, k), inverse_ref[k])
            work[pl.ds(i * 32, 32), :, cols(k)] = solved.reshape(32, 8, PW)
            bits_ref[cols(i), cols(k)] = solved.astype(jnp.bfloat16)
            return c

        lax.fori_loop(k + 1, PANELS, below, 0)

        def column(j, c):
            def row(i, c2):
                term = dot_nt(bits_ref[cols(i), cols(k)], bits_ref[cols(j), cols(k)])
                work[pl.ds(i * 32, 32), :, cols(j)] -= term.reshape(32, 8, PW)
                return c2

            return lax.fori_loop(j, PANELS, row, c)

        lax.fori_loop(k + 1, PANELS, column, 0)
        return carry

    lax.fori_loop(0, PANELS, panel, 0)
    me = jnp.minimum(me_ref[0], PANELS - 1)

    def out(j, c):
        own_ref[:, cols(j)] = jnp.where(j <= me, load(me, j), 0.0)
        return c

    lax.fori_loop(0, PANELS, out, 0)


def factor_pivots(me, shares):
    order = PANELS * PW
    return pl.pallas_call(
        pivot_kernel,
        grid_spec=pltpu.PrefetchScalarGridSpec(
            num_scalar_prefetch=1,
            grid=(1,),
            in_specs=[pl.BlockSpec(memory_space=pl.ANY)],
            out_specs=[
                pl.BlockSpec((order, order), lambda i, m: (0, 0)),
                pl.BlockSpec((PANELS, PW, PW), lambda i, m: (0, 0, 0)),
                pl.BlockSpec((PW, order), lambda i, m: (0, 0)),
            ],
            scratch_shapes=[
                pltpu.VMEM((order // 8, 8, order), jnp.float32),
                pltpu.SemaphoreType.DMA,
            ],
        ),
        out_shape=[
            jax.ShapeDtypeStruct((order, order), jnp.bfloat16),
            jax.ShapeDtypeStruct((PANELS, PW, PW), jnp.float32),
            jax.ShapeDtypeStruct((PW, order), jnp.float32),
        ],
        compiler_params=pltpu.CompilerParams(vmem_limit_bytes=48 * MIB),
        cost_estimate=pl.CostEstimate(
            flops=80_000_000_000, bytes_accessed=20_000_000, transcendentals=0
        ),
        name="factor_pivots",
    )(me, shares)


def pack_kernel(pick_ref, tiles_ref, outbox_ref, sem):
    count = outbox_ref.shape[0]

    def send(i, c):
        pltpu.make_async_copy(tiles_ref.at[pick_ref[i]], outbox_ref.at[i], sem).start()
        return c

    lax.fori_loop(0, count, send, 0, unroll=8)
    pltpu.make_async_copy(outbox_ref, outbox_ref, sem).wait()


def pack_tiles(pick, tiles):
    count = pick.shape[0]
    return pl.pallas_call(
        pack_kernel,
        grid_spec=pltpu.PrefetchScalarGridSpec(
            num_scalar_prefetch=1,
            grid=(1,),
            in_specs=[pl.BlockSpec(tiles.shape, lambda i, p: (0, 0, 0))],
            out_specs=pl.BlockSpec(memory_space=pl.ANY),
            scratch_shapes=[pltpu.SemaphoreType.DMA],
        ),
        out_shape=jax.ShapeDtypeStruct((count, TB, TB), jnp.bfloat16),
        compiler_params=pltpu.CompilerParams(vmem_limit_bytes=32 * MIB),
        name="pack_tiles",
    )(pick, tiles)


CHUNK = 32


def solve_kernel(
    tags_ref, me_ref, front_ref, inbox_ref, bits_ref, inverse_ref, own_ref,
    factor_ref, rows_ref, rest_ref, work, landed, sems, rest_sem,
):
    pivots = PANELS * PW
    count = inbox_ref.shape[0]
    chunks = count // CHUNK
    fill = pltpu.make_async_copy(front_ref, work, sems.at[chunks])
    fill.start()

    def fetch(c):
        part = pl.ds(c * CHUNK, CHUNK)
        return pltpu.make_async_copy(inbox_ref.at[part], landed.at[part], sems.at[c])

    for c in range(chunks):
        fetch(c).start()
    fill.wait()

    for c in range(chunks):
        fetch(c).wait()

        def add(i, carry):
            code = tags_ref[i]

            @pl.when(code >= 0)
            def _():
                place = (
                    pl.ds(pl.multiple_of((code // 64) * TB, TB), TB),
                    pl.ds(pl.multiple_of((code % 64) * TB, TB), TB),
                )
                work[place] += landed[i].astype(jnp.float32)

            return carry

        lax.fori_loop(c * CHUNK, (c + 1) * CHUNK, add, 0)
    leave = pltpu.make_async_copy(work.at[:, pl.ds(pivots, rest_ref.shape[1])], rest_ref, rest_sem)
    leave.start()
    below = me_ref[0] >= PANELS
    for k in range(PANELS):
        at = slice(k * PW, (k + 1) * PW)
        current = work[:, at]
        if k:
            current = current - dot_nt(rows_ref[:, : k * PW], bits_ref[at, : k * PW])
        solved = dot_nt_split(current, inverse_ref[k])
        rows_ref[:, at] = solved.astype(jnp.bfloat16)
        factor_ref[:, at] = jnp.where(below, solved, own_ref[:, at])
    leave.wait()


def solve_rows(tags, me, front, inbox, bits, inverse, own):
    order = front.shape[1]
    pivots = PANELS * PW
    whole = lambda shape: pl.BlockSpec(shape, lambda i, t, m: (0,) * len(shape))
    count = inbox.shape[0]
    return pl.pallas_call(
        solve_kernel,
        grid_spec=pltpu.PrefetchScalarGridSpec(
            num_scalar_prefetch=2,
            grid=(1,),
            in_specs=[
                pl.BlockSpec(memory_space=pl.ANY),
                pl.BlockSpec(memory_space=pl.ANY),
                whole(bits.shape),
                whole(inverse.shape),
                whole(own.shape),
            ],
            out_specs=[
                whole((PW, pivots)),
                whole((PW, pivots)),
                pl.BlockSpec(memory_space=pl.ANY),
            ],
            scratch_shapes=[
                pltpu.VMEM((PW, order), jnp.float32),
                pltpu.VMEM(inbox.shape, jnp.bfloat16),
                pltpu.SemaphoreType.DMA((count // CHUNK + 1,)),
                pltpu.SemaphoreType.DMA,
            ],
        ),
        out_shape=[
            jax.ShapeDtypeStruct((PW, pivots), jnp.float32),
            jax.ShapeDtypeStruct((PW, pivots), jnp.bfloat16),
            jax.ShapeDtypeStruct((PW, order - pivots), jnp.float32),
        ],
        compiler_params=pltpu.CompilerParams(vmem_limit_bytes=56 * MIB),
        name="solve_rows",
    )(tags, me, front, inbox, bits, inverse, own)


def schur_kernel(me_ref, rest_ref, rows_ref, others_ref, out_ref):
    term = dot_nt(rows_ref[...], others_ref[...])
    out_ref[...] = jnp.where(me_ref[0] >= PANELS, rest_ref[...] - term, 0.0)


def schur_rows(me, rest, rows, gathered):
    width = rest.shape[1]
    return pl.pallas_call(
        schur_kernel,
        grid_spec=pltpu.PrefetchScalarGridSpec(
            num_scalar_prefetch=1,
            grid=(width // PW,),
            in_specs=[
                pl.BlockSpec((PW, PW), lambda j, m: (0, j)),
                pl.BlockSpec(rows.shape, lambda j, m: (0, 0)),
                pl.BlockSpec((PW, rows.shape[1]), lambda j, m: (j + PANELS, 0)),
            ],
            out_specs=pl.BlockSpec((PW, PW), lambda j, m: (0, j)),
        ),
        out_shape=jax.ShapeDtypeStruct(rest.shape, jnp.float32),
        compiler_params=pltpu.CompilerParams(vmem_limit_bytes=32 * MIB),
        name="schur_rows",
    )(me, rest, rows, gathered)


def on_device(front_matrix, child_tiles, tile_route, tile_row, tile_col):
    work = front_matrix[0]
    tiles = child_tiles[0]
    count = tiles.shape[0]
    groups = lax.axis_size("group")
    fronts = lax.axis_size("front")
    devices = groups * fronts
    tail = fronts - PANELS
    me = lax.axis_index("front")
    mine = lax.axis_index("group") * fronts + me
    shares = spread_pivots(work)

    target = tile_route[0, :, 0]
    destination = target // tail * fronts + PANELS + target % tail
    code = (destination * 2 + tile_row[0]) * 64 + tile_col[0]
    positions = jnp.arange(count, dtype=jnp.int32)
    meets = destination[None, :] == jnp.arange(devices, dtype=jnp.int32)[:, None]
    first = jnp.min(jnp.where(meets, positions[None, :], count), axis=1)
    last = jnp.max(jnp.where(meets, positions[None, :], -1), axis=1)
    pick = jnp.stack([jnp.where(first < count, first, 0), jnp.maximum(last, 0)], axis=1)
    codes = lax.all_gather(code, ("group", "front"), axis=0).reshape(devices, count)
    here = codes // 128 == mine
    from_first = jnp.min(jnp.where(here, positions[None, :], count), axis=1)
    from_last = jnp.max(jnp.where(here, positions[None, :], -1), axis=1)
    label = codes % 128
    tag_first = jnp.max(
        jnp.where(positions[None, :] == from_first[:, None], label, -1), axis=1
    )
    tag_last = jnp.max(
        jnp.where(
            (positions[None, :] == from_last[:, None]) & (from_last != from_first)[:, None],
            label,
            -1,
        ),
        axis=1,
    )
    tags = jnp.stack([tag_first, tag_last], axis=1).reshape(devices * SLOTS)

    outbox = pack_tiles(pick.reshape(devices * SLOTS), tiles)
    inbox = lax.all_to_all(
        outbox.reshape(devices, SLOTS, TB, TB), ("group", "front"), 0, 0, tiled=True
    ).reshape(devices * SLOTS, TB, TB)

    self = me.astype(jnp.int32).reshape(1)
    bits, inverse, own = factor_pivots(self, shares)
    factor, rows, rest = solve_rows(tags, self, work, inbox, bits, inverse, own)
    gathered = gather_rows(rows)
    schur = schur_rows(self, rest, rows, gathered)
    return (factor[None], schur[None])


def solution(mesh):
    return jax.shard_map(
        on_device,
        mesh=mesh,
        in_specs=(
            P("group", "front", None),
            P("group", "front", None, None),
            P("group", "front", None),
            P("group", "front"),
            P("group", "front"),
        ),
        out_specs=(P("group", "front", None), P("group", "front", None)),
        check_vma=False,
    )
```

```python
import functools

import jax
import jax.numpy as jnp
from jax import lax
from jax.experimental import pallas as pl
from jax.experimental.pallas import tpu as pltpu
from jax.sharding import PartitionSpec as P

PANELS = 6
PW = 256
TB = 128
SUB = 16
SLOTS = 2
GROUPS = 4
LABEL_ROWS = 16
MIB = 1 << 20


def dot_nt(a, b, precision=None):
    return lax.dot_general(
        a, b, (((1,), (1,)), ((), ())), precision=precision, preferred_element_type=jnp.float32
    )


def dot_nn(a, b, precision=None):
    return lax.dot_general(
        a, b, (((1,), (0,)), ((), ())), precision=precision, preferred_element_type=jnp.float32
    )


def halves(a):
    high = a.astype(jnp.bfloat16)
    low = (a - high.astype(jnp.float32)).astype(jnp.bfloat16)
    return high, low


def dot_tn_split(a, b):
    ah, al = halves(a)
    bh, bl = halves(b)
    left = jnp.concatenate([ah, ah, al], axis=0)
    right = jnp.concatenate([bh, bl, bh], axis=0)
    return lax.dot_general(
        left, right, (((0,), (0,)), ((), ())), preferred_element_type=jnp.float32
    )


def dot_nt_split(a, b):
    ah, al = halves(a)
    bh, bl = halves(b)
    left = jnp.concatenate([ah, ah, al], axis=1)
    right = jnp.concatenate([bh, bl, bh], axis=1)
    return dot_nt(left, right)


def dot_nn_split(a, b):
    ah, al = halves(a)
    bh, bl = halves(b)
    left = jnp.concatenate([ah, ah, al], axis=1)
    right = jnp.concatenate([bh, bl, bh], axis=0)
    return dot_nn(left, right)


def chol_inv(block):
    n = TB
    parts = SUB // 8
    lane = lax.broadcasted_iota(jnp.int32, (8, n), 1)
    sub = lax.broadcasted_iota(jnp.int32, (8, n), 0)
    rows = [block[8 * i : 8 * i + 8] for i in range(n // 8)]
    upper = []
    inverse = []
    for p in range(n // SUB):
        first = p * parts
        left = p * SUB
        panel = rows[first : first + parts]
        unit = [jnp.where(lane == sub + (left + 8 * h), 1.0, 0.0) for h in range(parts)]
        spread = [
            [jnp.broadcast_to(panel[h][:, left + j : left + j + 1], (8, n)) for h in range(parts)]
            for j in range(SUB)
        ]
        scale = [jnp.zeros((8, n), jnp.float32) for _ in range(parts)]
        for j in range(SUB):
            at, s = divmod(j, 8)
            inv = lax.rsqrt(jnp.broadcast_to(spread[j][at][s : s + 1], (8, n)))
            mult = [None] * parts
            for h in range(at, parts):
                mult[h] = spread[j][h] * inv
                if h == at:
                    mult[h] = jnp.where(sub > s, mult[h], 0.0)
            for target in [panel, unit] + spread[j + 1 :]:
                row = jnp.broadcast_to(target[at][s : s + 1], (8, n)) * inv
                for h in range(at, parts):
                    target[h] = target[h] - mult[h] * row
            scale[at] = jnp.where(sub == s, inv, scale[at])
        inside = (lane >= left) & (lane < left + SUB)
        ups = []
        full = []
        for h in range(parts):
            up = panel[h] * scale[h]
            mixed = jnp.where(inside, unit[h] * scale[h], up)
            inverse.append(jnp.where(lane < left + SUB, mixed, 0.0))
            upper.append(jnp.where(lane >= left, up, 0.0))
            ups.append(up)
            full.append(mixed)
        if left + SUB < n:
            ups = jnp.concatenate(ups, axis=0)
            full = jnp.concatenate(full, axis=0)
            change = dot_tn_split(ups[:, left + SUB :], full)
            for k, i in enumerate(range(first + parts, n // 8)):
                rows[i] = jnp.where(inside, 0.0, rows[i]) - change[8 * k : 8 * k + 8]
    return jnp.concatenate(upper, axis=0), jnp.concatenate(inverse, axis=0)


def share_segments(i):
    half_width = (PANELS + 1) * PW // 2
    group = min(i, PANELS - 1 - i)
    begin = 0 if i < PANELS // 2 else (group + 1) * PW
    end = begin + (i + 1) * PW
    found = []
    for half in range(2):
        low, high = max(begin, half * half_width), min(end, (half + 1) * half_width)
        if low < high:
            found.append((half, group, low - half * half_width, low - begin, high - low))
    return found


MESH = pl.DeviceIdType.MESH
SIDE = 4
SENDS = 64
MOVES = {"b+": (0, 3), "b-": (0, 1), "a+": (3, 0), "a-": (1, 0)}


def when(condition, action):
    if condition is None:
        action()
    else:
        pl.when(condition)(action)


class Ring:
    def __init__(self, skip):
        me = lax.axis_index("front")
        self.me = me
        self.core = me % 2
        x, y = (me // 2) % SIDE, me // (2 * SIDE)
        self.a = jnp.where(self.core == 0, y, x)
        self.b = jnp.where(self.core == 0, x, y)
        self.skip = skip
        self.sends = 0
        self.late = []
        self.peer = {"s": me + 1 - 2 * self.core}
        for name, (da, db) in MOVES.items():
            self.peer[name] = 2 * self.chip(SIDE - da, SIDE - db) + self.core

    def chip(self, da, db, other=False):
        core = 1 - self.core if other else self.core
        a, b = (self.b, self.a) if other else (self.a, self.b)
        a, b = (a + da) % SIDE, (b + db) % SIDE
        return jnp.where(core == 0, a * SIDE + b, b * SIDE + a)

    def live(self, da, db, other=False):
        return self.chip(da, db, other) * 2 >= self.skip if self.skip else None

    def greet(self):
        barrier = pltpu.get_barrier_semaphore()
        for peer in self.peer.values():
            pl.semaphore_signal(barrier, inc=1, device_id={"front": peer}, device_id_type=MESH)
        return barrier

    def gather(self, own, out, sems, after=None):
        ring_recv, side_recv, own_recv, local_sem, send_sem = sems
        core = self.core

        def piece(da, db, s, other=False):
            half = 1 - core if other else core
            chip = self.chip(da, db, other)
            if s is None:
                return out.at[pl.ds(2 * chip, 2), half]
            return out.at[2 * chip + s, half]

        def remote(source, target, recv, to, condition):
            k = self.sends
            self.sends += 1

            def make():
                return pltpu.make_async_remote_copy(
                    src_ref=source,
                    dst_ref=target,
                    send_sem=send_sem.at[k],
                    recv_sem=recv,
                    device_id={"front": self.peer[to]},
                    device_id_type=MESH,
                )

            when(condition, lambda: make().start())
            self.late.append((condition, lambda: make().wait_send()))

        def arrive(ref, sem, condition):
            def wait():
                pltpu.make_async_remote_copy(
                    src_ref=ref,
                    dst_ref=ref,
                    send_sem=send_sem.at[0],
                    recv_sem=sem,
                    device_id={"front": self.peer["s"]},
                    device_id_type=MESH,
                ).wait_recv()

            when(condition, wait)

        def give(da, db, s, to):
            ref = piece(da, db, s)
            at = 0 if s is None else s
            if to == "s":
                recv = side_recv.at[da, db, at]
            else:
                recv = ring_recv.at[(da + MOVES[to][0]) % SIDE, (db + MOVES[to][1]) % SIDE, at]
            remote(ref, ref, recv, to, self.live(da, db))

        here = self.live(0, 0)
        mine = pltpu.make_async_copy(own(core), piece(0, 0, core), local_sem.at[0])
        rest = pltpu.make_async_copy(own(1 - core), piece(0, 0, core, True), local_sem.at[1])
        when(here, mine.start)
        when(here, rest.start)
        remote(own(1 - core), piece(0, 0, core, True), own_recv.at[0], "s", here)
        remote(own(core), piece(0, 0, core), own_recv.at[1], "s", here)
        when(here, mine.wait)
        arrive(piece(0, 0, 1 - core), own_recv.at[0], here)
        for to in MOVES:
            give(0, 0, None, to)
        steps = [
            (0, 3, None, [(0, "b+"), (None, "a+"), (None, "a-")]),
            (0, 1, None, [(1, "b-"), (None, "a+"), (None, "a-")]),
            (3, 0, None, [(0, "a+")]),
            (1, 0, None, [(1, "a-")]),
            (0, 2, 0, [(0, "a+"), (0, "a-")]),
            (0, 2, 1, [(1, "a+"), (1, "a-")]),
            (3, 3, None, [(0, "a+")]),
            (1, 3, None, [(1, "a-")]),
            (3, 1, None, [(0, "a+")]),
            (1, 1, None, [(1, "a-")]),
            (2, 0, 0, []),
            (2, 0, 1, []),
            (3, 2, 0, [(0, "a+")]),
            (1, 2, 1, [(1, "a-")]),
            (3, 2, 1, []),
            (1, 2, 0, []),
            (2, 3, 0, []),
            (2, 3, 1, []),
            (2, 1, 0, []),
            (2, 1, 1, []),
            (2, 2, 0, []),
            (2, 2, 1, []),
        ]
        def take_own():
            arrive(piece(0, 0, 1 - core, True), own_recv.at[1], here)
            when(here, rest.wait)

        def take_side(da, db):
            parts = [s for at_a, at_b, s, _ in steps if (at_a, at_b) == (da, db)]
            for s in parts:
                arrive(
                    piece(da, db, s, True), side_recv.at[da, db, s or 0], self.live(da, db, True)
                )

        for number, (da, db, s, onward) in enumerate(steps):
            arrive(piece(da, db, s), ring_recv.at[da, db, s or 0], self.live(da, db))
            for part, to in onward:
                give(da, db, part, to)
            give(da, db, s, "s")
            if after is not None:
                after(number, take_own, take_side)
        if after is None:
            take_own()
            for da, db in UNITS[1:]:
                take_side(da, db)
        for condition, wait in self.late:
            when(condition, wait)


UNITS = [
    (0, 0), (0, 3), (0, 1), (3, 0), (1, 0), (0, 2), (3, 3), (1, 3),
    (3, 1), (1, 1), (2, 0), (3, 2), (1, 2), (2, 3), (2, 1), (2, 2),
]
BATCHES = {5: (0, 6, 0, 5), 9: (6, 10, 5, 8), 11: (10, 11, 8, 10), 15: (11, 13, 10, 11), 21: (13, 16, 11, 16)}


RING_SEMS = [
    pltpu.SemaphoreType.DMA((SIDE, SIDE, 2)),
    pltpu.SemaphoreType.DMA((SIDE, SIDE, 2)),
    pltpu.SemaphoreType.DMA((2,)),
    pltpu.SemaphoreType.DMA((2,)),
    pltpu.SemaphoreType.DMA((SENDS,)),
]


def schur_kernel(rows_ref, rest_ref, out_ref, gathered, rest_sem, *sems):
    ring = Ring(PANELS)
    pl.semaphore_wait(ring.greet(), len(ring.peer))
    below = ring.me >= PANELS
    fill = pltpu.make_async_copy(rest_ref, out_ref, rest_sem)

    @pl.when(below)
    def _():
        fill.start()

    @pl.when(jnp.logical_not(below))
    def _():
        out_ref[...] = jnp.zeros_like(out_ref)

    def after(step, take_own, take_side):
        if step not in BATCHES:
            return
        own_from, own_to, side_from, side_to = BATCHES[step]
        if own_from == 0:
            take_own()

            @pl.when(below)
            def _():
                fill.wait()

        for da, db in UNITS[max(side_from, 1) : side_to]:
            take_side(da, db)

        def use(n, c):
            side = n >= own_to - own_from
            at = jnp.where(side, n - (own_to - own_from) + side_from, n + own_from)
            da = sum(jnp.where(at == i, unit[0], 0) for i, unit in enumerate(UNITS))
            db = sum(jnp.where(at == i, unit[1], 0) for i, unit in enumerate(UNITS))
            chip = jnp.where(side, ring.chip(da, db, True), ring.chip(da, db))
            half = jnp.where(side, 1 - ring.core, ring.core)

            @pl.when(below & (chip * 2 >= PANELS))
            def _():
                unit = gathered[pl.ds(chip * 2, 2), half].reshape(PW, rows_ref.shape[1])
                term = dot_nt(rows_ref[...], unit)
                for core in range(2):
                    start = (chip * 2 + core - PANELS) * PW + half * TB
                    at_columns = pl.ds(pl.multiple_of(start, TB), TB)
                    out_ref[:, at_columns] -= term[:, core * TB : (core + 1) * TB]

            return c

        lax.fori_loop(0, own_to - own_from + side_to - side_from, use, 0)

    ring.gather(lambda h: rows_ref.at[pl.ds(h * TB, TB)], gathered, sems, after)


def gather_schur(rows, rest):
    fronts = lax.axis_size("front")
    return pl.pallas_call(
        schur_kernel,
        in_specs=[
            pl.BlockSpec(memory_space=pltpu.VMEM),
            pl.BlockSpec(memory_space=pl.ANY),
        ],
        out_specs=pl.BlockSpec(memory_space=pltpu.VMEM),
        out_shape=jax.ShapeDtypeStruct(rest.shape, jnp.float32),
        scratch_shapes=[
            pltpu.VMEM((fronts, 2, TB, rows.shape[1]), jnp.bfloat16),
            pltpu.SemaphoreType.DMA,
        ]
        + RING_SEMS,
        compiler_params=pltpu.CompilerParams(
            collective_id=1, has_side_effects=True, vmem_limit_bytes=60 * MIB
        ),
        name="gather_schur",
    )(rows, rest)


def spread_kernel(front_ref, out_ref, share, deal_recv, deal_send, *sems):
    fronts = out_ref.shape[0]
    ring = Ring(0)
    me = ring.me
    barrier = ring.greet()
    for i in range(PANELS):

        @pl.when(me != i)
        def _():
            pl.semaphore_signal(barrier, inc=1, device_id={"front": i}, device_id_type=MESH)

    @pl.when(me < PANELS)
    def _():
        pl.semaphore_wait(barrier, len(ring.peer) + fronts - 1)

    @pl.when(me >= PANELS)
    def _():
        pl.semaphore_wait(barrier, len(ring.peer))

    pieces = []
    for i in range(PANELS):
        for segment in share_segments(i):
            pieces.append((i, len(pieces)) + segment)

    def source(f, piece):
        i, _, _, _, _, column, width = piece
        return front_ref.at[pl.ds(pl.multiple_of(f * 8, 8), 8), pl.ds(column, width)]

    def target(piece):
        _, _, half, group, column, _, width = piece
        return share.at[half, pl.ds(group * 8, 8), pl.ds(column, width)]

    def far(f, piece):
        return pltpu.make_async_remote_copy(
            src_ref=source(f, piece),
            dst_ref=target(piece),
            send_sem=deal_send.at[piece[2], f],
            recv_sem=deal_recv.at[piece[1]],
            device_id={"front": f},
            device_id_type=MESH,
        )

    def near(piece):
        return pltpu.make_async_copy(source(me, piece), target(piece), deal_recv.at[piece[1]])

    for i in range(PANELS):
        mine = [piece for piece in pieces if piece[0] == i]

        @pl.when(me == i)
        def _():
            def deal(f, c):
                @pl.when(f != me)
                def _():
                    for piece in mine:
                        far(f, piece).start()

                return c

            lax.fori_loop(0, fronts, deal, 0)
            for piece in mine:
                near(piece).start()

    for piece in pieces:

        @pl.when(me == piece[0])
        def _():
            near(piece).wait()

        @pl.when(me != piece[0])
        def _():
            far(0, piece).wait_recv()

    ring.gather(lambda h: share.at[h], out_ref, sems)
    for i in range(PANELS):
        mine = [piece for piece in pieces if piece[0] == i]

        @pl.when(me == i)
        def _():
            def done(f, c):
                @pl.when(f != me)
                def _():
                    for piece in mine:
                        far(f, piece).wait_send()

                return c

            lax.fori_loop(0, fronts, done, 0)


def spread_pivots(front):
    fronts = lax.axis_size("front")
    share = (2, PANELS // 2 * (PW // fronts), (PANELS + 1) * PW // 2)
    return pl.pallas_call(
        spread_kernel,
        in_specs=[pl.BlockSpec(memory_space=pl.ANY)],
        out_specs=pl.BlockSpec(memory_space=pl.ANY),
        out_shape=jax.ShapeDtypeStruct((fronts,) + share, jnp.float32),
        scratch_shapes=[
            pltpu.VMEM(share, jnp.float32),
            pltpu.SemaphoreType.DMA((9,)),
            pltpu.SemaphoreType.DMA((2, fronts)),
        ]
        + RING_SEMS,
        compiler_params=pltpu.CompilerParams(
            collective_id=2, has_side_effects=True, vmem_limit_bytes=60 * MIB
        ),
        name="spread_pivots",
    )(front)


def pivot_kernel(me_ref, shares_ref, bits_ref, inverse_ref, own_ref, work, sem):
    high = lax.Precision.HIGHEST
    fronts = shares_ref.shape[0]
    for i in range(PANELS):
        for half, group, source, target, width in share_segments(i):
            pltpu.make_async_copy(
                shares_ref.at[:, half, pl.ds(group * 8, 8), pl.ds(source, width)],
                work.at[pl.ds(i * fronts, fronts), :, pl.ds(target, width)],
                sem,
            ).start()
    pltpu.make_async_copy(shares_ref, shares_ref, sem).wait()

    def cols(i):
        return pl.ds(pl.multiple_of(i * PW, PW), PW)

    def load(i, j):
        return work[pl.ds(i * 32, 32), :, cols(j)].reshape(PW, PW)

    def panel(k, carry):
        top = pl.ds(k * 32, 16)
        low = pl.ds(k * 32 + 16, 16)
        left = pl.ds(pl.multiple_of(k * PW, TB), TB)
        right = pl.ds(pl.multiple_of(k * PW + TB, TB), TB)
        u1, w1 = chol_inv(work[top, :, left].reshape(TB, TB))
        l21 = dot_nt(work[low, :, left].reshape(TB, TB), w1, high)
        u2, w2 = chol_inv(work[low, :, right].reshape(TB, TB) - dot_nt(l21, l21, high))
        w21 = -dot_nn(w2, dot_nn(l21, w1, high), high)
        work[top, :, left] = u1.T.reshape(16, 8, TB)
        work[top, :, right] = jnp.zeros((16, 8, TB), jnp.float32)
        work[low, :, left] = l21.reshape(16, 8, TB)
        work[low, :, right] = u2.T.reshape(16, 8, TB)
        inverse_ref[k, :TB, :TB] = w1
        inverse_ref[k, :TB, TB:] = jnp.zeros((TB, TB), jnp.float32)
        inverse_ref[k, TB:, :TB] = w21
        inverse_ref[k, TB:, TB:] = w2

        def below(i, c):
            solved = dot_nt_split(load(i, k), inverse_ref[k])
            work[pl.ds(i * 32, 32), :, cols(k)] = solved.reshape(32, 8, PW)
            bits_ref[cols(i), cols(k)] = solved.astype(jnp.bfloat16)
            return c

        lax.fori_loop(k + 1, PANELS, below, 0)

        def column(j, c):
            def row(i, c2):
                term = dot_nt(bits_ref[cols(i), cols(k)], bits_ref[cols(j), cols(k)])
                work[pl.ds(i * 32, 32), :, cols(j)] -= term.reshape(32, 8, PW)
                return c2

            return lax.fori_loop(j, PANELS, row, c)

        lax.fori_loop(k + 1, PANELS, column, 0)
        return carry

    lax.fori_loop(0, PANELS, panel, 0)
    me = jnp.minimum(me_ref[0], PANELS - 1)

    def out(j, c):
        own_ref[:, cols(j)] = jnp.where(j <= me, load(me, j), 0.0)
        return c

    lax.fori_loop(0, PANELS, out, 0)


def factor_pivots(me, shares):
    order = PANELS * PW
    return pl.pallas_call(
        pivot_kernel,
        grid_spec=pltpu.PrefetchScalarGridSpec(
            num_scalar_prefetch=1,
            grid=(1,),
            in_specs=[pl.BlockSpec(memory_space=pl.ANY)],
            out_specs=[
                pl.BlockSpec((order, order), lambda i, m: (0, 0)),
                pl.BlockSpec((PANELS, PW, PW), lambda i, m: (0, 0, 0)),
                pl.BlockSpec((PW, order), lambda i, m: (0, 0)),
            ],
            scratch_shapes=[
                pltpu.VMEM((order // 8, 8, order), jnp.float32),
                pltpu.SemaphoreType.DMA,
            ],
        ),
        out_shape=[
            jax.ShapeDtypeStruct((order, order), jnp.bfloat16),
            jax.ShapeDtypeStruct((PANELS, PW, PW), jnp.float32),
            jax.ShapeDtypeStruct((PW, order), jnp.float32),
        ],
        compiler_params=pltpu.CompilerParams(vmem_limit_bytes=60 * MIB),
        cost_estimate=pl.CostEstimate(
            flops=80_000_000_000, bytes_accessed=20_000_000, transcendentals=0
        ),
        name="factor_pivots",
    )(me, shares)


def pack_kernel(pick_ref, tiles_ref, labels_ref, outbox_ref, sem, label_sem):
    tail = outbox_ref.shape[0] // GROUPS - PANELS
    labels = pltpu.make_async_copy(
        labels_ref, outbox_ref.at[:, pl.ds(SLOTS * TB, LABEL_ROWS)], label_sem
    )
    labels.start()

    def send(i, c):
        device = i // tail * (tail + PANELS) + PANELS + i % tail
        for s in range(SLOTS):
            pltpu.make_async_copy(
                tiles_ref.at[pick_ref[device * SLOTS + s]],
                outbox_ref.at[device, pl.ds(s * TB, TB)],
                sem,
            ).start()
        return c

    lax.fori_loop(0, GROUPS * tail, send, 0, unroll=4)
    filled = outbox_ref.at[pl.ds(0, GROUPS * tail), pl.ds(0, SLOTS * TB)]
    pltpu.make_async_copy(filled, filled, sem).wait()
    labels.wait()


def pack_tiles(pick, tiles, labels):
    devices = labels.shape[0]
    return pl.pallas_call(
        pack_kernel,
        grid_spec=pltpu.PrefetchScalarGridSpec(
            num_scalar_prefetch=1,
            grid=(1,),
            in_specs=[
                pl.BlockSpec(tiles.shape, lambda i, p: (0, 0, 0)),
                pl.BlockSpec(labels.shape, lambda i, p: (0, 0, 0)),
            ],
            out_specs=pl.BlockSpec(memory_space=pl.ANY),
            scratch_shapes=[pltpu.SemaphoreType.DMA, pltpu.SemaphoreType.DMA],
        ),
        out_shape=jax.ShapeDtypeStruct((devices, SLOTS * TB + LABEL_ROWS, TB), jnp.bfloat16),
        compiler_params=pltpu.CompilerParams(vmem_limit_bytes=60 * MIB),
        name="pack_tiles",
    )(pick, tiles, labels)


CHUNK = 16


def solve_kernel(
    tags_ref, me_ref, front_ref, inbox_ref, bits_ref, inverse_ref, own_ref,
    factor_ref, rows_ref, rest_ref, work, landed, sems, rest_sem,
):
    pivots = PANELS * PW
    count = inbox_ref.shape[0]
    chunks = count // CHUNK
    fill = pltpu.make_async_copy(front_ref, work, sems.at[chunks])
    fill.start()

    def fetch(c):
        part = pl.ds(c * CHUNK, CHUNK)
        return pltpu.make_async_copy(
            inbox_ref.at[part, pl.ds(0, SLOTS * TB)], landed.at[part], sems.at[c]
        )

    for c in range(chunks):
        fetch(c).start()
    fill.wait()

    for c in range(chunks):
        fetch(c).wait()

        def add(i, carry):
            for s in range(SLOTS):
                code = tags_ref[i * SLOTS + s]

                @pl.when(code >= 0)
                def _():
                    place = (
                        pl.ds(pl.multiple_of((code // 64) * TB, TB), TB),
                        pl.ds(pl.multiple_of((code % 64) * TB, TB), TB),
                    )
                    work[place] += landed[i, s * TB : (s + 1) * TB].astype(jnp.float32)

            return carry

        lax.fori_loop(c * CHUNK, (c + 1) * CHUNK, add, 0)
    leave = pltpu.make_async_copy(work.at[:, pl.ds(pivots, rest_ref.shape[1])], rest_ref, rest_sem)
    leave.start()
    below = me_ref[0] >= PANELS
    for k in range(PANELS):
        at = slice(k * PW, (k + 1) * PW)
        current = work[:, at]
        if k:
            current = current - dot_nt(rows_ref[:, : k * PW], bits_ref[at, : k * PW])
        solved = dot_nt_split(current, inverse_ref[k])
        rows_ref[:, at] = solved.astype(jnp.bfloat16)
        factor_ref[:, at] = jnp.where(below, solved, own_ref[:, at])
    leave.wait()


def solve_rows(tags, me, front, inbox, bits, inverse, own):
    order = front.shape[1]
    pivots = PANELS * PW
    whole = lambda shape: pl.BlockSpec(shape, lambda i, t, m: (0,) * len(shape))
    count = inbox.shape[0]
    return pl.pallas_call(
        solve_kernel,
        grid_spec=pltpu.PrefetchScalarGridSpec(
            num_scalar_prefetch=2,
            grid=(1,),
            in_specs=[
                pl.BlockSpec(memory_space=pl.ANY),
                pl.BlockSpec(memory_space=pl.ANY),
                whole(bits.shape),
                whole(inverse.shape),
                whole(own.shape),
            ],
            out_specs=[
                whole((PW, pivots)),
                whole((PW, pivots)),
                pl.BlockSpec(memory_space=pl.ANY),
            ],
            scratch_shapes=[
                pltpu.VMEM((PW, order), jnp.float32),
                pltpu.VMEM((count, SLOTS * TB, TB), jnp.bfloat16),
                pltpu.SemaphoreType.DMA((count // CHUNK + 1,)),
                pltpu.SemaphoreType.DMA,
            ],
        ),
        out_shape=[
            jax.ShapeDtypeStruct((PW, pivots), jnp.float32),
            jax.ShapeDtypeStruct((PW, pivots), jnp.bfloat16),
            jax.ShapeDtypeStruct((PW, order - pivots), jnp.float32),
        ],
        compiler_params=pltpu.CompilerParams(vmem_limit_bytes=60 * MIB),
        name="solve_rows",
    )(tags, me, front, inbox, bits, inverse, own)


def on_device(front_matrix, child_tiles, tile_route, tile_row, tile_col):
    work = front_matrix[0]
    tiles = child_tiles[0]
    count = tiles.shape[0]
    groups = lax.axis_size("group")
    fronts = lax.axis_size("front")
    devices = groups * fronts
    tail = fronts - PANELS
    me = lax.axis_index("front")
    shares = spread_pivots(work)

    target = tile_route[0, :, 0]
    destination = target // tail * fronts + PANELS + target % tail
    label = tile_row[0] * 64 + tile_col[0]
    positions = jnp.arange(count, dtype=jnp.int32)
    meets = destination[None, :] == jnp.arange(devices, dtype=jnp.int32)[:, None]
    first = jnp.min(jnp.where(meets, positions[None, :], count), axis=1)
    last = jnp.max(jnp.where(meets, positions[None, :], -1), axis=1)
    pick = jnp.stack([jnp.where(first < count, first, 0), jnp.maximum(last, 0)], axis=1)
    here = positions[None, :] == first[:, None]
    label_first = jnp.max(jnp.where(here, label[None, :], -1), axis=1)
    here = (positions[None, :] == last[:, None]) & (last != first)[:, None]
    label_last = jnp.max(jnp.where(here, label[None, :], -1), axis=1)
    lane = jnp.arange(TB, dtype=jnp.int32)[None, :]
    labels = jnp.where(lane == 0, label_first[:, None], label_last[:, None])
    labels = jnp.broadcast_to(
        labels.astype(jnp.bfloat16)[:, None, :], (devices, LABEL_ROWS, TB)
    )
    outbox = pack_tiles(pick.reshape(devices * SLOTS), tiles, labels)
    outbox, shares = lax.optimization_barrier((outbox, shares))
    inbox = lax.all_to_all(outbox, ("group", "front"), 0, 0, tiled=True)
    tags = inbox[:, SLOTS * TB, :SLOTS].astype(jnp.int32).reshape(devices * SLOTS)

    self = me.astype(jnp.int32).reshape(1)
    bits, inverse, own = factor_pivots(self, shares)
    factor, rows, rest = solve_rows(tags, self, work, inbox, bits, inverse, own)
    schur = gather_schur(rows, rest)
    return (factor[None], schur[None])


def solution(mesh):
    return jax.shard_map(
        on_device,
        mesh=mesh,
        in_specs=(
            P("group", "front", None),
            P("group", "front", None, None),
            P("group", "front", None),
            P("group", "front"),
            P("group", "front"),
        ),
        out_specs=(P("group", "front", None), P("group", "front", None)),
        check_vma=False,
    )
```

```python
import functools

import jax
import jax.numpy as jnp
from jax import lax
from jax.experimental import pallas as pl
from jax.experimental.pallas import tpu as pltpu
from jax.sharding import PartitionSpec as P

PANELS = 6
PW = 256
TB = 128
SUB = 16
SLOTS = 2
LABEL_ROWS = 16
AHEAD = 4
EARLY = 10
EACH = 1
STEPS = 22
MIB = 1 << 20


def dot_nt(a, b, precision=None):
    return lax.dot_general(
        a, b, (((1,), (1,)), ((), ())), precision=precision, preferred_element_type=jnp.float32
    )


def dot_nn(a, b, precision=None):
    return lax.dot_general(
        a, b, (((1,), (0,)), ((), ())), precision=precision, preferred_element_type=jnp.float32
    )


def halves(a):
    high = a.astype(jnp.bfloat16)
    low = (a - high.astype(jnp.float32)).astype(jnp.bfloat16)
    return high, low


def dot_tn_split(a, b):
    ah, al = halves(a)
    bh, bl = halves(b)
    left = jnp.concatenate([ah, ah, al], axis=0)
    right = jnp.concatenate([bh, bl, bh], axis=0)
    return lax.dot_general(
        left, right, (((0,), (0,)), ((), ())), preferred_element_type=jnp.float32
    )


def dot_nt_split(a, b):
    ah, al = halves(a)
    bh, bl = halves(b)
    left = jnp.concatenate([ah, ah, al], axis=1)
    right = jnp.concatenate([bh, bl, bh], axis=1)
    return dot_nt(left, right)


def dot_nn_split(a, b):
    ah, al = halves(a)
    bh, bl = halves(b)
    left = jnp.concatenate([ah, ah, al], axis=1)
    right = jnp.concatenate([bh, bl, bh], axis=0)
    return dot_nn(left, right)


def chol_inv(block):
    n = TB
    parts = SUB // 8
    lane = lax.broadcasted_iota(jnp.int32, (8, n), 1)
    sub = lax.broadcasted_iota(jnp.int32, (8, n), 0)
    rows = [block[8 * i : 8 * i + 8] for i in range(n // 8)]
    upper = []
    inverse = []
    for p in range(n // SUB):
        first = p * parts
        left = p * SUB
        panel = rows[first : first + parts]
        unit = [jnp.where(lane == sub + (left + 8 * h), 1.0, 0.0) for h in range(parts)]
        spread = [
            [jnp.broadcast_to(panel[h][:, left + j : left + j + 1], (8, n)) for h in range(parts)]
            for j in range(SUB)
        ]
        scale = [jnp.zeros((8, n), jnp.float32) for _ in range(parts)]
        for j in range(SUB):
            at, s = divmod(j, 8)
            inv = lax.rsqrt(jnp.broadcast_to(spread[j][at][s : s + 1], (8, n)))
            mult = [None] * parts
            for h in range(at, parts):
                mult[h] = spread[j][h] * inv
                if h == at:
                    mult[h] = jnp.where(sub > s, mult[h], 0.0)
            for target in [panel, unit] + spread[j + 1 :]:
                row = jnp.broadcast_to(target[at][s : s + 1], (8, n)) * inv
                for h in range(at, parts):
                    target[h] = target[h] - mult[h] * row
            scale[at] = jnp.where(sub == s, inv, scale[at])
        inside = (lane >= left) & (lane < left + SUB)
        ups = []
        full = []
        for h in range(parts):
            up = panel[h] * scale[h]
            mixed = jnp.where(inside, unit[h] * scale[h], up)
            inverse.append(jnp.where(lane < left + SUB, mixed, 0.0))
            upper.append(jnp.where(lane >= left, up, 0.0))
            ups.append(up)
            full.append(mixed)
        if left + SUB < n:
            ups = jnp.concatenate(ups, axis=0)
            full = jnp.concatenate(full, axis=0)
            change = dot_tn_split(ups[:, left + SUB :], full)
            for k, i in enumerate(range(first + parts, n // 8)):
                rows[i] = jnp.where(inside, 0.0, rows[i]) - change[8 * k : 8 * k + 8]
    return jnp.concatenate(upper, axis=0), jnp.concatenate(inverse, axis=0)


def share_segments(i):
    half_width = (PANELS + 1) * PW // 2
    group = min(i, PANELS - 1 - i)
    begin = 0 if i < PANELS // 2 else (group + 1) * PW
    end = begin + (i + 1) * PW
    found = []
    for half in range(2):
        low, high = max(begin, half * half_width), min(end, (half + 1) * half_width)
        if low < high:
            found.append((half, group, low - half * half_width, low - begin, high - low))
    return found


MESH = pl.DeviceIdType.MESH
SIDE = 4
SENDS = 64
MOVES = {"b+": (0, 3), "b-": (0, 1), "a+": (3, 0), "a-": (1, 0)}


def when(condition, action):
    if condition is None:
        action()
    else:
        pl.when(condition)(action)


class Ring:
    def __init__(self, skip):
        me = lax.axis_index("front")
        self.me = me
        self.core = me % 2
        x, y = (me // 2) % SIDE, me // (2 * SIDE)
        self.a = jnp.where(self.core == 0, y, x)
        self.b = jnp.where(self.core == 0, x, y)
        self.skip = skip
        self.sends = 0
        self.late = []
        self.peer = {"s": me + 1 - 2 * self.core}
        for name, (da, db) in MOVES.items():
            self.peer[name] = 2 * self.chip(SIDE - da, SIDE - db) + self.core

    def chip(self, da, db, other=False):
        core = 1 - self.core if other else self.core
        a, b = (self.b, self.a) if other else (self.a, self.b)
        a, b = (a + da) % SIDE, (b + db) % SIDE
        return jnp.where(core == 0, a * SIDE + b, b * SIDE + a)

    def live(self, da, db, other=False):
        return self.chip(da, db, other) * 2 >= self.skip if self.skip else None

    def greet(self):
        barrier = pltpu.get_barrier_semaphore()
        for peer in self.peer.values():
            pl.semaphore_signal(barrier, inc=1, device_id={"front": peer}, device_id_type=MESH)
        return barrier

    def gather(self, own, out, sems, after=None, taken=False):
        ring_recv, side_recv, own_recv, local_sem, send_sem = sems
        core = self.core

        def piece(da, db, s, other=False):
            half = 1 - core if other else core
            chip = self.chip(da, db, other)
            if s is None:
                return out.at[pl.ds(2 * chip, 2), half]
            return out.at[2 * chip + s, half]

        def remote(source, target, recv, to, condition):
            k = self.sends
            self.sends += 1

            def make():
                return pltpu.make_async_remote_copy(
                    src_ref=source,
                    dst_ref=target,
                    send_sem=send_sem.at[k],
                    recv_sem=recv,
                    device_id={"front": self.peer[to]},
                    device_id_type=MESH,
                )

            when(condition, lambda: make().start())
            self.late.append((condition, lambda: make().wait_send()))

        def arrive(ref, sem, condition):
            def wait():
                pltpu.make_async_remote_copy(
                    src_ref=ref,
                    dst_ref=ref,
                    send_sem=send_sem.at[0],
                    recv_sem=sem,
                    device_id={"front": self.peer["s"]},
                    device_id_type=MESH,
                ).wait_recv()

            when(condition, wait)

        def give(da, db, s, to):
            ref = piece(da, db, s)
            at = 0 if s is None else s
            if to == "s":
                recv = side_recv.at[da, db, at]
            else:
                recv = ring_recv.at[(da + MOVES[to][0]) % SIDE, (db + MOVES[to][1]) % SIDE, at]
            remote(ref, ref, recv, to, self.live(da, db))

        here = self.live(0, 0)
        mine = pltpu.make_async_copy(own(core), piece(0, 0, core), local_sem.at[0])
        rest = pltpu.make_async_copy(own(1 - core), piece(0, 0, core, True), local_sem.at[1])
        when(here, mine.start)
        when(here, rest.start)
        remote(own(1 - core), piece(0, 0, core, True), own_recv.at[0], "s", here)
        remote(own(core), piece(0, 0, core), own_recv.at[1], "s", here)
        when(here, mine.wait)
        arrive(piece(0, 0, 1 - core), own_recv.at[0], here)
        for to in MOVES:
            give(0, 0, None, to)
        steps = [
            (0, 3, None, [(0, "b+"), (None, "a+"), (None, "a-")]),
            (0, 1, None, [(1, "b-"), (None, "a+"), (None, "a-")]),
            (3, 0, None, [(0, "a+")]),
            (1, 0, None, [(1, "a-")]),
            (0, 2, 0, [(0, "a+"), (0, "a-")]),
            (0, 2, 1, [(1, "a+"), (1, "a-")]),
            (3, 3, None, [(0, "a+")]),
            (1, 3, None, [(1, "a-")]),
            (3, 1, None, [(0, "a+")]),
            (1, 1, None, [(1, "a-")]),
            (2, 0, 0, []),
            (2, 0, 1, []),
            (3, 2, 0, [(0, "a+")]),
            (1, 2, 1, [(1, "a-")]),
            (3, 2, 1, []),
            (1, 2, 0, []),
            (2, 3, 0, []),
            (2, 3, 1, []),
            (2, 1, 0, []),
            (2, 1, 1, []),
            (2, 2, 0, []),
            (2, 2, 1, []),
        ]
        def take_own():
            arrive(piece(0, 0, 1 - core, True), own_recv.at[1], here)
            when(here, rest.wait)

        def take_side(da, db):
            parts = [s for at_a, at_b, s, _ in steps if (at_a, at_b) == (da, db)]
            for s in parts:
                arrive(
                    piece(da, db, s, True), side_recv.at[da, db, s or 0], self.live(da, db, True)
                )

        for number, (da, db, s, onward) in enumerate(steps):
            arrive(piece(da, db, s), ring_recv.at[da, db, s or 0], self.live(da, db))
            for part, to in onward:
                give(da, db, part, to)
            give(da, db, s, "s")
            if after is not None:
                after(number, take_own, take_side)
        if not taken:
            take_own()
            for da, db in UNITS[1:]:
                take_side(da, db)
        for condition, wait in self.late:
            when(condition, wait)


UNITS = [
    (0, 0), (0, 3), (0, 1), (3, 0), (1, 0), (0, 2), (3, 3), (1, 3),
    (3, 1), (1, 1), (2, 0), (3, 2), (1, 2), (2, 3), (2, 1), (2, 2),
]
BATCHES = {5: (0, 6, 0, 5), 9: (6, 10, 5, 8), 11: (10, 11, 8, 10), 15: (11, 13, 10, 11), 21: (13, 16, 11, 16)}


RING_SEMS = [
    pltpu.SemaphoreType.DMA((SIDE, SIDE, 2)),
    pltpu.SemaphoreType.DMA((SIDE, SIDE, 2)),
    pltpu.SemaphoreType.DMA((2,)),
    pltpu.SemaphoreType.DMA((2,)),
    pltpu.SemaphoreType.DMA((SENDS,)),
]


def schur_kernel(rows_ref, rest_ref, out_ref, gathered, rest_sem, *sems):
    ring = Ring(PANELS)
    pl.semaphore_wait(ring.greet(), len(ring.peer))
    below = ring.me >= PANELS
    fill = pltpu.make_async_copy(rest_ref, out_ref, rest_sem)

    @pl.when(below)
    def _():
        fill.start()

    @pl.when(jnp.logical_not(below))
    def _():
        out_ref[...] = jnp.zeros_like(out_ref)

    def after(step, take_own, take_side):
        if step not in BATCHES:
            return
        own_from, own_to, side_from, side_to = BATCHES[step]
        if own_from == 0:
            take_own()

            @pl.when(below)
            def _():
                fill.wait()

        for da, db in UNITS[max(side_from, 1) : side_to]:
            take_side(da, db)

        def use(n, c):
            side = n >= own_to - own_from
            at = jnp.where(side, n - (own_to - own_from) + side_from, n + own_from)
            da = sum(jnp.where(at == i, unit[0], 0) for i, unit in enumerate(UNITS))
            db = sum(jnp.where(at == i, unit[1], 0) for i, unit in enumerate(UNITS))
            chip = jnp.where(side, ring.chip(da, db, True), ring.chip(da, db))
            half = jnp.where(side, 1 - ring.core, ring.core)

            @pl.when(below & (chip * 2 >= PANELS))
            def _():
                unit = gathered[pl.ds(chip * 2, 2), half].reshape(PW, rows_ref.shape[1])
                term = dot_nt(rows_ref[...], unit)
                for core in range(2):
                    start = (chip * 2 + core - PANELS) * PW + half * TB
                    at_columns = pl.ds(pl.multiple_of(start, TB), TB)
                    out_ref[:, at_columns] -= term[:, core * TB : (core + 1) * TB]

            return c

        lax.fori_loop(0, own_to - own_from + side_to - side_from, use, 0)

    ring.gather(lambda h: rows_ref.at[pl.ds(h * TB, TB)], gathered, sems, after, taken=True)


def gather_schur(rows, rest):
    fronts = lax.axis_size("front")
    return pl.pallas_call(
        schur_kernel,
        in_specs=[
            pl.BlockSpec(memory_space=pltpu.VMEM),
            pl.BlockSpec(memory_space=pl.ANY),
        ],
        out_specs=pl.BlockSpec(memory_space=pltpu.VMEM),
        out_shape=jax.ShapeDtypeStruct(rest.shape, jnp.float32),
        scratch_shapes=[
            pltpu.VMEM((fronts, 2, TB, rows.shape[1]), jnp.bfloat16),
            pltpu.SemaphoreType.DMA,
        ]
        + RING_SEMS,
        compiler_params=pltpu.CompilerParams(
            collective_id=1, has_side_effects=True, vmem_limit_bytes=60 * MIB
        ),
        name="gather_schur",
    )(rows, rest)


def deal_shares(ring, front_ref, share, deal_recv, deal_send, fronts):
    me = ring.me
    pieces = []
    for i in range(PANELS):
        for segment in share_segments(i):
            pieces.append((i, len(pieces)) + segment)

    def source(f, piece):
        i, _, _, _, _, column, width = piece
        return front_ref.at[pl.ds(pl.multiple_of(f * 8, 8), 8), pl.ds(column, width)]

    def target(piece):
        _, _, half, group, column, _, width = piece
        return share.at[half, pl.ds(group * 8, 8), pl.ds(column, width)]

    def far(f, piece):
        return pltpu.make_async_remote_copy(
            src_ref=source(f, piece),
            dst_ref=target(piece),
            send_sem=deal_send.at[piece[2], f],
            recv_sem=deal_recv.at[piece[1]],
            device_id={"front": f},
            device_id_type=MESH,
        )

    def near(piece):
        return pltpu.make_async_copy(source(me, piece), target(piece), deal_recv.at[piece[1]])

    def each(i, action):
        mine = [piece for piece in pieces if piece[0] == i]

        def one(f, c):
            @pl.when(f != me)
            def _():
                for piece in mine:
                    action(far(f, piece))

            return c

        lax.fori_loop(0, fronts, one, 0)
        return mine

    for i in range(PANELS):

        @pl.when(me == i)
        def _():
            for piece in each(i, lambda copy: copy.start()):
                near(piece).start()

    def wait_share():
        for piece in pieces:

            @pl.when(me == piece[0])
            def _():
                near(piece).wait()

            @pl.when(me != piece[0])
            def _():
                far(0, piece).wait_recv()

    def wait_sent():
        for i in range(PANELS):

            @pl.when(me == i)
            def _():
                each(i, lambda copy: copy.wait_send())

    return wait_share, wait_sent


def exchange_kernel(
    pick_ref, front_ref, tiles_ref, labels_ref,
    bits_ref, inverse_ref, own_ref, inbox_ref,
    work, tiles, outbox, share, shares,
    tile_sem, unpack_sem, ship_send, ship_recv, deal_recv, deal_send, *sems,
):
    devices = inbox_ref.shape[0]
    fronts = shares.shape[0]
    tail = fronts - PANELS
    ring = Ring(0)
    me = ring.me
    mine = lax.axis_index("group") * fronts + me
    fetch = pltpu.make_async_copy(tiles_ref, tiles, tile_sem)
    fetch.start()

    def where_is(device):
        return {"group": device // fronts, "front": device % fronts}

    barrier = pltpu.get_barrier_semaphore()

    def greet(k, c):
        other = where_is((mine + k) % devices)
        pl.semaphore_signal(barrier, inc=1, device_id=other, device_id_type=MESH)
        return c

    lax.fori_loop(1, devices, greet, 0)
    pl.semaphore_wait(barrier, devices - 1)
    wait_share, wait_sent = deal_shares(ring, front_ref, share, deal_recv, deal_send, fronts)

    fetch.wait()

    def pack(i, c):
        device = i // tail * fronts + PANELS + i % tail
        for s in range(SLOTS):
            outbox[device, s * TB : (s + 1) * TB] = tiles[pick_ref[device * SLOTS + s]]
        outbox[device, SLOTS * TB :] = labels_ref[device]
        return c

    lax.fori_loop(0, devices // fronts * tail, pack, 0)
    def ship(k):
        device = (mine + k * 37) % devices
        return device, pltpu.make_async_remote_copy(
            src_ref=outbox.at[device],
            dst_ref=inbox_ref.at[mine],
            send_sem=ship_send.at[k],
            recv_sem=ship_recv.at[k],
            device_id=where_is(device),
            device_id_type=MESH,
        )

    def start(k, c):
        device, copy = ship(k)
        pl.when(device % fronts >= PANELS)(copy.start)
        return c

    def left(k, c):
        device, copy = ship(k)
        pl.when(device % fronts >= PANELS)(copy.wait_send)
        return c

    def pace(k, c):
        start(k, c)
        return left(k - AHEAD, c)

    lax.fori_loop(1, 1 + AHEAD, start, 0)
    begun = 1 + AHEAD + EARLY
    lax.fori_loop(1 + AHEAD, begun, pace, 0)

    def after(step, take_own, take_side):
        lax.fori_loop(begun + step * EACH, begun + (step + 1) * EACH, pace, 0)

    wait_share()
    ring.gather(lambda h: share.at[h], shares, sems, after)
    begun = begun + STEPS * EACH

    lax.fori_loop(begun, devices, start, 0)
    keep = pltpu.make_async_copy(outbox.at[mine], inbox_ref.at[mine], ship_recv.at[0])
    below = me >= PANELS
    pl.when(below)(keep.start)

    for i in range(PANELS):
        for half, group, source, target, width in share_segments(i):
            pltpu.make_async_copy(
                shares.at[:, half, pl.ds(group * 8, 8), pl.ds(source, width)],
                work.at[pl.ds(i * fronts, fronts), :, pl.ds(target, width)],
                unpack_sem,
            ).start()
    pltpu.make_async_copy(shares, shares, unpack_sem).wait()
    factor_pivots(me, work, bits_ref, inverse_ref, own_ref)

    pl.when(below)(keep.wait)

    def landed(k, c):
        pl.when(below)(ship(k)[1].wait_recv)
        return c

    lax.fori_loop(begun - AHEAD, devices, left, 0)
    lax.fori_loop(1, devices, landed, 0)
    wait_sent()


def factor_pivots(me, work, bits_ref, inverse_ref, own_ref):
    high = lax.Precision.HIGHEST

    def cols(i):
        return pl.ds(pl.multiple_of(i * PW, PW), PW)

    def load(i, j):
        return work[pl.ds(i * 32, 32), :, cols(j)].reshape(PW, PW)

    def panel(k, carry):
        top = pl.ds(k * 32, 16)
        low = pl.ds(k * 32 + 16, 16)
        left = pl.ds(pl.multiple_of(k * PW, TB), TB)
        right = pl.ds(pl.multiple_of(k * PW + TB, TB), TB)
        u1, w1 = chol_inv(work[top, :, left].reshape(TB, TB))
        l21 = dot_nt(work[low, :, left].reshape(TB, TB), w1, high)
        u2, w2 = chol_inv(work[low, :, right].reshape(TB, TB) - dot_nt(l21, l21, high))
        w21 = -dot_nn(w2, dot_nn(l21, w1, high), high)
        work[top, :, left] = u1.T.reshape(16, 8, TB)
        work[top, :, right] = jnp.zeros((16, 8, TB), jnp.float32)
        work[low, :, left] = l21.reshape(16, 8, TB)
        work[low, :, right] = u2.T.reshape(16, 8, TB)
        inverse_ref[k, :TB, :TB] = w1
        inverse_ref[k, :TB, TB:] = jnp.zeros((TB, TB), jnp.float32)
        inverse_ref[k, TB:, :TB] = w21
        inverse_ref[k, TB:, TB:] = w2

        def below(i, c):
            solved = dot_nt_split(load(i, k), inverse_ref[k])
            work[pl.ds(i * 32, 32), :, cols(k)] = solved.reshape(32, 8, PW)
            bits_ref[cols(i), cols(k)] = solved.astype(jnp.bfloat16)
            return c

        lax.fori_loop(k + 1, PANELS, below, 0)

        def column(j, c):
            def row(i, c2):
                term = dot_nt(bits_ref[cols(i), cols(k)], bits_ref[cols(j), cols(k)])
                work[pl.ds(i * 32, 32), :, cols(j)] -= term.reshape(32, 8, PW)
                return c2

            return lax.fori_loop(j, PANELS, row, c)

        lax.fori_loop(k + 1, PANELS, column, 0)
        return carry

    lax.fori_loop(0, PANELS, panel, 0)
    me = jnp.minimum(me, PANELS - 1)

    def out(j, c):
        own_ref[:, cols(j)] = jnp.where(j <= me, load(me, j), 0.0)
        return c

    lax.fori_loop(0, PANELS, out, 0)


def exchange(pick, front, tiles, labels):
    fronts = lax.axis_size("front")
    devices = labels.shape[0]
    order = PANELS * PW
    share = (2, PANELS // 2 * (PW // fronts), (PANELS + 1) * PW // 2)
    box = (devices, SLOTS * TB + LABEL_ROWS, TB)
    return pl.pallas_call(
        exchange_kernel,
        in_specs=[
            pl.BlockSpec(memory_space=pltpu.SMEM),
            pl.BlockSpec(memory_space=pl.ANY),
            pl.BlockSpec(memory_space=pl.ANY),
            pl.BlockSpec(memory_space=pltpu.VMEM),
        ],
        out_specs=[pl.BlockSpec(memory_space=pltpu.VMEM)] * 3
        + [pl.BlockSpec(memory_space=pl.ANY)],
        out_shape=[
            jax.ShapeDtypeStruct((order, order), jnp.bfloat16),
            jax.ShapeDtypeStruct((PANELS, PW, PW), jnp.float32),
            jax.ShapeDtypeStruct((PW, order), jnp.float32),
            jax.ShapeDtypeStruct(box, jnp.bfloat16),
        ],
        scratch_shapes=[
            pltpu.VMEM((order // 8, 8, order), jnp.float32),
            pltpu.VMEM(tiles.shape, jnp.bfloat16),
            pltpu.VMEM(box, jnp.bfloat16),
            pltpu.VMEM(share, jnp.float32),
            pltpu.VMEM((fronts,) + share, jnp.float32),
            pltpu.SemaphoreType.DMA,
            pltpu.SemaphoreType.DMA,
            pltpu.SemaphoreType.DMA((devices,)),
            pltpu.SemaphoreType.DMA((devices,)),
            pltpu.SemaphoreType.DMA((9,)),
            pltpu.SemaphoreType.DMA((2, fronts)),
        ]
        + RING_SEMS,
        compiler_params=pltpu.CompilerParams(
            collective_id=2, has_side_effects=True, vmem_limit_bytes=60 * MIB
        ),
        name="exchange_and_factor",
    )(pick, front, tiles, labels)


CHUNK = 16


def solve_kernel(
    tags_ref, me_ref, front_ref, inbox_ref, bits_ref, inverse_ref, own_ref,
    factor_ref, rows_ref, rest_ref, work, landed, sems, rest_sem,
):
    pivots = PANELS * PW
    count = inbox_ref.shape[0]
    chunks = count // CHUNK
    fill = pltpu.make_async_copy(front_ref, work, sems.at[chunks])
    fill.start()

    def fetch(c):
        part = pl.ds(c * CHUNK, CHUNK)
        return pltpu.make_async_copy(
            inbox_ref.at[part, pl.ds(0, SLOTS * TB)], landed.at[part], sems.at[c]
        )

    for c in range(chunks):
        fetch(c).start()
    fill.wait()

    for c in range(chunks):
        fetch(c).wait()

        def add(i, carry):
            for s in range(SLOTS):
                code = tags_ref[i * SLOTS + s]

                @pl.when(code >= 0)
                def _():
                    place = (
                        pl.ds(pl.multiple_of((code // 64) * TB, TB), TB),
                        pl.ds(pl.multiple_of((code % 64) * TB, TB), TB),
                    )
                    work[place] += landed[i, s * TB : (s + 1) * TB].astype(jnp.float32)

            return carry

        lax.fori_loop(c * CHUNK, (c + 1) * CHUNK, add, 0)
    leave = pltpu.make_async_copy(work.at[:, pl.ds(pivots, rest_ref.shape[1])], rest_ref, rest_sem)
    leave.start()
    below = me_ref[0] >= PANELS
    for k in range(PANELS):
        at = slice(k * PW, (k + 1) * PW)
        current = work[:, at]
        if k:
            current = current - dot_nt(rows_ref[:, : k * PW], bits_ref[at, : k * PW])
        solved = dot_nt_split(current, inverse_ref[k])
        rows_ref[:, at] = solved.astype(jnp.bfloat16)
        factor_ref[:, at] = jnp.where(below, solved, own_ref[:, at])
    leave.wait()


def solve_rows(tags, me, front, inbox, bits, inverse, own):
    order = front.shape[1]
    pivots = PANELS * PW
    whole = lambda shape: pl.BlockSpec(shape, lambda i, t, m: (0,) * len(shape))
    count = inbox.shape[0]
    return pl.pallas_call(
        solve_kernel,
        grid_spec=pltpu.PrefetchScalarGridSpec(
            num_scalar_prefetch=2,
            grid=(1,),
            in_specs=[
                pl.BlockSpec(memory_space=pl.ANY),
                pl.BlockSpec(memory_space=pl.ANY),
                whole(bits.shape),
                whole(inverse.shape),
                whole(own.shape),
            ],
            out_specs=[
                whole((PW, pivots)),
                whole((PW, pivots)),
                pl.BlockSpec(memory_space=pl.ANY),
            ],
            scratch_shapes=[
                pltpu.VMEM((PW, order), jnp.float32),
                pltpu.VMEM((count, SLOTS * TB, TB), jnp.bfloat16),
                pltpu.SemaphoreType.DMA((count // CHUNK + 1,)),
                pltpu.SemaphoreType.DMA,
            ],
        ),
        out_shape=[
            jax.ShapeDtypeStruct((PW, pivots), jnp.float32),
            jax.ShapeDtypeStruct((PW, pivots), jnp.bfloat16),
            jax.ShapeDtypeStruct((PW, order - pivots), jnp.float32),
        ],
        compiler_params=pltpu.CompilerParams(vmem_limit_bytes=60 * MIB),
        name="solve_rows",
    )(tags, me, front, inbox, bits, inverse, own)


def on_device(front_matrix, child_tiles, tile_route, tile_row, tile_col):
    work = front_matrix[0]
    tiles = child_tiles[0]
    count = tiles.shape[0]
    groups = lax.axis_size("group")
    fronts = lax.axis_size("front")
    devices = groups * fronts
    tail = fronts - PANELS
    me = lax.axis_index("front")

    target = tile_route[0, :, 0]
    destination = target // tail * fronts + PANELS + target % tail
    label = tile_row[0] * 64 + tile_col[0]
    positions = jnp.arange(count, dtype=jnp.int32)
    meets = destination[None, :] == jnp.arange(devices, dtype=jnp.int32)[:, None]
    first = jnp.min(jnp.where(meets, positions[None, :], count), axis=1)
    last = jnp.max(jnp.where(meets, positions[None, :], -1), axis=1)
    pick = jnp.stack([jnp.where(first < count, first, 0), jnp.maximum(last, 0)], axis=1)
    here = positions[None, :] == first[:, None]
    label_first = jnp.max(jnp.where(here, label[None, :], -1), axis=1)
    here = (positions[None, :] == last[:, None]) & (last != first)[:, None]
    label_last = jnp.max(jnp.where(here, label[None, :], -1), axis=1)
    lane = jnp.arange(TB, dtype=jnp.int32)[None, :]
    labels = jnp.where(lane == 0, label_first[:, None], label_last[:, None])
    labels = jnp.broadcast_to(
        labels.astype(jnp.bfloat16)[:, None, :], (devices, LABEL_ROWS, TB)
    )
    bits, inverse, own, inbox = exchange(pick.reshape(devices * SLOTS), work, tiles, labels)
    tags = jnp.where(me >= PANELS, inbox[:, SLOTS * TB, :SLOTS].astype(jnp.int32), -1)
    tags = tags.reshape(devices * SLOTS)
    self = me.astype(jnp.int32).reshape(1)
    factor, rows, rest = solve_rows(tags, self, work, inbox, bits, inverse, own)
    schur = gather_schur(rows, rest)
    return (factor[None], schur[None])


def solution(mesh):
    return jax.shard_map(
        on_device,
        mesh=mesh,
        in_specs=(
            P("group", "front", None),
            P("group", "front", None, None),
            P("group", "front", None),
            P("group", "front"),
            P("group", "front"),
        ),
        out_specs=(P("group", "front", None), P("group", "front", None)),
        check_vma=False,
    )
```

```python
import functools

import jax
import jax.numpy as jnp
from jax import lax
from jax.experimental import pallas as pl
from jax.experimental.pallas import tpu as pltpu
from jax.sharding import PartitionSpec as P

PANELS = 6
PW = 256
TB = 128
SUB = 16
SLOTS = 2
AHEAD = 4
EARLY = 10
EACH = 1
STEPS = 22
MIB = 1 << 20


def dot_nt(a, b, precision=None):
    return lax.dot_general(
        a, b, (((1,), (1,)), ((), ())), precision=precision, preferred_element_type=jnp.float32
    )


def dot_nn(a, b, precision=None):
    return lax.dot_general(
        a, b, (((1,), (0,)), ((), ())), precision=precision, preferred_element_type=jnp.float32
    )


def halves(a):
    high = a.astype(jnp.bfloat16)
    low = (a - high.astype(jnp.float32)).astype(jnp.bfloat16)
    return high, low


def dot_tn_split(a, b):
    ah, al = halves(a)
    bh, bl = halves(b)
    left = jnp.concatenate([ah, ah, al], axis=0)
    right = jnp.concatenate([bh, bl, bh], axis=0)
    return lax.dot_general(
        left, right, (((0,), (0,)), ((), ())), preferred_element_type=jnp.float32
    )


def dot_nt_split(a, b):
    ah, al = halves(a)
    bh, bl = halves(b)
    left = jnp.concatenate([ah, ah, al], axis=1)
    right = jnp.concatenate([bh, bl, bh], axis=1)
    return dot_nt(left, right)


def dot_nn_split(a, b):
    ah, al = halves(a)
    bh, bl = halves(b)
    left = jnp.concatenate([ah, ah, al], axis=1)
    right = jnp.concatenate([bh, bl, bh], axis=0)
    return dot_nn(left, right)


def chol_inv(block):
    n = TB
    parts = SUB // 8
    lane = lax.broadcasted_iota(jnp.int32, (8, n), 1)
    sub = lax.broadcasted_iota(jnp.int32, (8, n), 0)
    rows = [block[8 * i : 8 * i + 8] for i in range(n // 8)]
    upper = []
    inverse = []
    for p in range(n // SUB):
        first = p * parts
        left = p * SUB
        panel = rows[first : first + parts]
        unit = [jnp.where(lane == sub + (left + 8 * h), 1.0, 0.0) for h in range(parts)]
        spread = [
            [jnp.broadcast_to(panel[h][:, left + j : left + j + 1], (8, n)) for h in range(parts)]
            for j in range(SUB)
        ]
        scale = [jnp.zeros((8, n), jnp.float32) for _ in range(parts)]
        for j in range(SUB):
            at, s = divmod(j, 8)
            inv = lax.rsqrt(jnp.broadcast_to(spread[j][at][s : s + 1], (8, n)))
            mult = [None] * parts
            for h in range(at, parts):
                mult[h] = spread[j][h] * inv
                if h == at:
                    mult[h] = jnp.where(sub > s, mult[h], 0.0)
            for target in [panel, unit] + spread[j + 1 :]:
                row = jnp.broadcast_to(target[at][s : s + 1], (8, n)) * inv
                for h in range(at, parts):
                    target[h] = target[h] - mult[h] * row
            scale[at] = jnp.where(sub == s, inv, scale[at])
        inside = (lane >= left) & (lane < left + SUB)
        ups = []
        full = []
        for h in range(parts):
            up = panel[h] * scale[h]
            mixed = jnp.where(inside, unit[h] * scale[h], up)
            inverse.append(jnp.where(lane < left + SUB, mixed, 0.0))
            upper.append(jnp.where(lane >= left, up, 0.0))
            ups.append(up)
            full.append(mixed)
        if left + SUB < n:
            ups = jnp.concatenate(ups, axis=0)
            full = jnp.concatenate(full, axis=0)
            change = dot_tn_split(ups[:, left + SUB :], full)
            for k, i in enumerate(range(first + parts, n // 8)):
                rows[i] = jnp.where(inside, 0.0, rows[i]) - change[8 * k : 8 * k + 8]
    return jnp.concatenate(upper, axis=0), jnp.concatenate(inverse, axis=0)


def share_segments(i):
    half_width = (PANELS + 1) * PW // 2
    group = min(i, PANELS - 1 - i)
    begin = 0 if i < PANELS // 2 else (group + 1) * PW
    end = begin + (i + 1) * PW
    found = []
    for half in range(2):
        low, high = max(begin, half * half_width), min(end, (half + 1) * half_width)
        if low < high:
            found.append((half, group, low - half * half_width, low - begin, high - low))
    return found


MESH = pl.DeviceIdType.MESH
SIDE = 4
SENDS = 64
MOVES = {"b+": (0, 3), "b-": (0, 1), "a+": (3, 0), "a-": (1, 0)}


def when(condition, action):
    if condition is None:
        action()
    else:
        pl.when(condition)(action)


class Ring:
    def __init__(self, skip):
        me = lax.axis_index("front")
        self.me = me
        self.core = me % 2
        x, y = (me // 2) % SIDE, me // (2 * SIDE)
        self.a = jnp.where(self.core == 0, y, x)
        self.b = jnp.where(self.core == 0, x, y)
        self.skip = skip
        self.sends = 0
        self.late = []
        self.peer = {"s": me + 1 - 2 * self.core}
        for name, (da, db) in MOVES.items():
            self.peer[name] = 2 * self.chip(SIDE - da, SIDE - db) + self.core

    def chip(self, da, db, other=False):
        core = 1 - self.core if other else self.core
        a, b = (self.b, self.a) if other else (self.a, self.b)
        a, b = (a + da) % SIDE, (b + db) % SIDE
        return jnp.where(core == 0, a * SIDE + b, b * SIDE + a)

    def live(self, da, db, other=False):
        return self.chip(da, db, other) * 2 >= self.skip if self.skip else None

    def greet(self):
        barrier = pltpu.get_barrier_semaphore()
        for peer in self.peer.values():
            pl.semaphore_signal(barrier, inc=1, device_id={"front": peer}, device_id_type=MESH)
        return barrier

    def gather(self, own, out, sems, after=None, taken=False):
        ring_recv, side_recv, own_recv, local_sem, send_sem = sems
        core = self.core

        def piece(da, db, s, other=False):
            half = 1 - core if other else core
            chip = self.chip(da, db, other)
            if s is None:
                return out.at[pl.ds(2 * chip, 2), half]
            return out.at[2 * chip + s, half]

        def remote(source, target, recv, to, condition):
            k = self.sends
            self.sends += 1

            def make():
                return pltpu.make_async_remote_copy(
                    src_ref=source,
                    dst_ref=target,
                    send_sem=send_sem.at[k],
                    recv_sem=recv,
                    device_id={"front": self.peer[to]},
                    device_id_type=MESH,
                )

            when(condition, lambda: make().start())
            self.late.append((condition, lambda: make().wait_send()))

        def arrive(ref, sem, condition):
            def wait():
                pltpu.make_async_remote_copy(
                    src_ref=ref,
                    dst_ref=ref,
                    send_sem=send_sem.at[0],
                    recv_sem=sem,
                    device_id={"front": self.peer["s"]},
                    device_id_type=MESH,
                ).wait_recv()

            when(condition, wait)

        def give(da, db, s, to):
            ref = piece(da, db, s)
            at = 0 if s is None else s
            if to == "s":
                recv = side_recv.at[da, db, at]
            else:
                recv = ring_recv.at[(da + MOVES[to][0]) % SIDE, (db + MOVES[to][1]) % SIDE, at]
            remote(ref, ref, recv, to, self.live(da, db))

        here = self.live(0, 0)
        mine = pltpu.make_async_copy(own(core), piece(0, 0, core), local_sem.at[0])
        rest = pltpu.make_async_copy(own(1 - core), piece(0, 0, core, True), local_sem.at[1])
        when(here, mine.start)
        when(here, rest.start)
        remote(own(1 - core), piece(0, 0, core, True), own_recv.at[0], "s", here)
        remote(own(core), piece(0, 0, core), own_recv.at[1], "s", here)
        when(here, mine.wait)
        arrive(piece(0, 0, 1 - core), own_recv.at[0], here)
        for to in MOVES:
            give(0, 0, None, to)
        steps = [
            (0, 3, None, [(0, "b+"), (None, "a+"), (None, "a-")]),
            (0, 1, None, [(1, "b-"), (None, "a+"), (None, "a-")]),
            (3, 0, None, [(0, "a+")]),
            (1, 0, None, [(1, "a-")]),
            (0, 2, 0, [(0, "a+"), (0, "a-")]),
            (0, 2, 1, [(1, "a+"), (1, "a-")]),
            (3, 3, None, [(0, "a+")]),
            (1, 3, None, [(1, "a-")]),
            (3, 1, None, [(0, "a+")]),
            (1, 1, None, [(1, "a-")]),
            (2, 0, 0, []),
            (2, 0, 1, []),
            (3, 2, 0, [(0, "a+")]),
            (1, 2, 1, [(1, "a-")]),
            (3, 2, 1, []),
            (1, 2, 0, []),
            (2, 3, 0, []),
            (2, 3, 1, []),
            (2, 1, 0, []),
            (2, 1, 1, []),
            (2, 2, 0, []),
            (2, 2, 1, []),
        ]
        def take_own():
            arrive(piece(0, 0, 1 - core, True), own_recv.at[1], here)
            when(here, rest.wait)

        def take_side(da, db):
            parts = [s for at_a, at_b, s, _ in steps if (at_a, at_b) == (da, db)]
            for s in parts:
                arrive(
                    piece(da, db, s, True), side_recv.at[da, db, s or 0], self.live(da, db, True)
                )

        for number, (da, db, s, onward) in enumerate(steps):
            arrive(piece(da, db, s), ring_recv.at[da, db, s or 0], self.live(da, db))
            for part, to in onward:
                give(da, db, part, to)
            give(da, db, s, "s")
            if after is not None:
                after(number, take_own, take_side)
        if not taken:
            take_own()
            for da, db in UNITS[1:]:
                take_side(da, db)
        for condition, wait in self.late:
            when(condition, wait)


UNITS = [
    (0, 0), (0, 3), (0, 1), (3, 0), (1, 0), (0, 2), (3, 3), (1, 3),
    (3, 1), (1, 1), (2, 0), (3, 2), (1, 2), (2, 3), (2, 1), (2, 2),
]
BATCHES = {5: (0, 6, 0, 5), 9: (6, 10, 5, 8), 11: (10, 11, 8, 10), 15: (11, 13, 10, 11), 21: (13, 16, 11, 16)}


RING_SEMS = [
    pltpu.SemaphoreType.DMA((SIDE, SIDE, 2)),
    pltpu.SemaphoreType.DMA((SIDE, SIDE, 2)),
    pltpu.SemaphoreType.DMA((2,)),
    pltpu.SemaphoreType.DMA((2,)),
    pltpu.SemaphoreType.DMA((SENDS,)),
]


def schur_kernel(rows_ref, rest_ref, out_ref, gathered, rest_sem, *sems):
    ring = Ring(PANELS)
    pl.semaphore_wait(ring.greet(), len(ring.peer))
    below = ring.me >= PANELS
    fill = pltpu.make_async_copy(rest_ref, out_ref, rest_sem)

    @pl.when(below)
    def _():
        fill.start()

    @pl.when(jnp.logical_not(below))
    def _():
        out_ref[...] = jnp.zeros_like(out_ref)

    def after(step, take_own, take_side):
        if step not in BATCHES:
            return
        own_from, own_to, side_from, side_to = BATCHES[step]
        if own_from == 0:
            take_own()

            @pl.when(below)
            def _():
                fill.wait()

        for da, db in UNITS[max(side_from, 1) : side_to]:
            take_side(da, db)

        def use(n, c):
            side = n >= own_to - own_from
            at = jnp.where(side, n - (own_to - own_from) + side_from, n + own_from)
            da = sum(jnp.where(at == i, unit[0], 0) for i, unit in enumerate(UNITS))
            db = sum(jnp.where(at == i, unit[1], 0) for i, unit in enumerate(UNITS))
            chip = jnp.where(side, ring.chip(da, db, True), ring.chip(da, db))
            half = jnp.where(side, 1 - ring.core, ring.core)

            @pl.when(below & (chip * 2 >= PANELS))
            def _():
                unit = gathered[pl.ds(chip * 2, 2), half].reshape(PW, rows_ref.shape[1])
                term = dot_nt(rows_ref[...], unit)
                for core in range(2):
                    start = (chip * 2 + core - PANELS) * PW + half * TB
                    at_columns = pl.ds(pl.multiple_of(start, TB), TB)
                    out_ref[:, at_columns] -= term[:, core * TB : (core + 1) * TB]

            return c

        lax.fori_loop(0, own_to - own_from + side_to - side_from, use, 0)

    ring.gather(lambda h: rows_ref.at[pl.ds(h * TB, TB)], gathered, sems, after, taken=True)


def gather_schur(rows, rest):
    fronts = lax.axis_size("front")
    return pl.pallas_call(
        schur_kernel,
        in_specs=[
            pl.BlockSpec(memory_space=pltpu.VMEM),
            pl.BlockSpec(memory_space=pl.ANY),
        ],
        out_specs=pl.BlockSpec(memory_space=pltpu.VMEM),
        out_shape=jax.ShapeDtypeStruct(rest.shape, jnp.float32),
        scratch_shapes=[
            pltpu.VMEM((fronts, 2, TB, rows.shape[1]), jnp.bfloat16),
            pltpu.SemaphoreType.DMA,
        ]
        + RING_SEMS,
        compiler_params=pltpu.CompilerParams(
            collective_id=1, has_side_effects=True, vmem_limit_bytes=40 * MIB
        ),
        name="gather_schur",
    )(rows, rest)


def deal_shares(ring, front_ref, share, deal_recv, deal_send, fronts):
    me = ring.me
    pieces = []
    for i in range(PANELS):
        for segment in share_segments(i):
            pieces.append((i, len(pieces)) + segment)

    def source(f, piece):
        i, _, _, _, _, column, width = piece
        return front_ref.at[pl.ds(pl.multiple_of(f * 8, 8), 8), pl.ds(column, width)]

    def target(piece):
        _, _, half, group, column, _, width = piece
        return share.at[half, pl.ds(group * 8, 8), pl.ds(column, width)]

    def far(f, piece):
        return pltpu.make_async_remote_copy(
            src_ref=source(f, piece),
            dst_ref=target(piece),
            send_sem=deal_send.at[piece[2], f],
            recv_sem=deal_recv.at[piece[1]],
            device_id={"front": f},
            device_id_type=MESH,
        )

    def near(piece):
        return pltpu.make_async_copy(source(me, piece), target(piece), deal_recv.at[piece[1]])

    def each(i, action):
        mine = [piece for piece in pieces if piece[0] == i]

        def one(f, c):
            @pl.when(f != me)
            def _():
                for piece in mine:
                    action(far(f, piece))

            return c

        lax.fori_loop(0, fronts, one, 0)
        return mine

    for i in range(PANELS):

        @pl.when(me == i)
        def _():
            for piece in each(i, lambda copy: copy.start()):
                near(piece).start()

    def wait_share():
        for piece in pieces:

            @pl.when(me == piece[0])
            def _():
                near(piece).wait()

            @pl.when(me != piece[0])
            def _():
                far(0, piece).wait_recv()

    def wait_sent():
        for i in range(PANELS):

            @pl.when(me == i)
            def _():
                each(i, lambda copy: copy.wait_send())

    return wait_share, wait_sent


def exchange_kernel(
    pick_ref, front_ref, tiles_ref, labels_ref,
    bits_out, inverse_out, own_out, inbox_ref, tags_ref,
    bits_ref, inverse_ref, own_ref, work, tiles, outbox, share, shares,
    tile_sem, unpack_sem, out_sems, ship_send, ship_recv, label_send, label_recv,
    deal_recv, deal_send, *sems,
):
    devices = inbox_ref.shape[0]
    fronts = shares.shape[0]
    tail = fronts - PANELS
    ring = Ring(0)
    me = ring.me
    mine = lax.axis_index("group") * fronts + me
    fetch = pltpu.make_async_copy(tiles_ref, tiles, tile_sem)
    fetch.start()

    def where_is(device):
        return {"group": device // fronts, "front": device % fronts}

    barrier = pltpu.get_barrier_semaphore()

    def greet(k, c):
        other = where_is((mine + k) % devices)
        pl.semaphore_signal(barrier, inc=1, device_id=other, device_id_type=MESH)
        return c

    lax.fori_loop(1, devices, greet, 0)
    pl.semaphore_wait(barrier, devices - 1)
    wait_share, wait_sent = deal_shares(ring, front_ref, share, deal_recv, deal_send, fronts)

    fetch.wait()

    def pack(i, c):
        device = i // tail * fronts + PANELS + i % tail
        for s in range(SLOTS):
            outbox[device, s * TB : (s + 1) * TB] = tiles[pick_ref[device * SLOTS + s]]
        return c

    lax.fori_loop(0, devices // fronts * tail, pack, 0)
    def ship(k):
        device = (mine + k * 37) % devices
        return device % fronts >= PANELS, [
            pltpu.make_async_remote_copy(
                src_ref=source.at[device],
                dst_ref=target.at[mine],
                send_sem=send_sem.at[k],
                recv_sem=recv_sem.at[k],
                device_id=where_is(device),
                device_id_type=MESH,
            )
            for source, target, send_sem, recv_sem in (
                (outbox, inbox_ref, ship_send, ship_recv),
                (labels_ref, tags_ref, label_send, label_recv),
            )
        ]

    def start(k, c):
        live, copies = ship(k)

        @pl.when(live)
        def _():
            for copy in copies:
                copy.start()

        return c

    def left(k, c):
        live, copies = ship(k)

        @pl.when(live)
        def _():
            for copy in copies:
                copy.wait_send()

        return c

    def pace(k, c):
        start(k, c)
        return left(k - AHEAD, c)

    lax.fori_loop(1, 1 + AHEAD, start, 0)
    begun = 1 + AHEAD + EARLY
    lax.fori_loop(1 + AHEAD, begun, pace, 0)

    def after(step, take_own, take_side):
        lax.fori_loop(begun + step * EACH, begun + (step + 1) * EACH, pace, 0)

    wait_share()
    ring.gather(lambda h: share.at[h], shares, sems, after)
    begun = begun + STEPS * EACH

    lax.fori_loop(begun, devices, start, 0)
    below = me >= PANELS
    keep = [
        pltpu.make_async_copy(outbox.at[mine], inbox_ref.at[mine], ship_recv.at[0]),
        pltpu.make_async_copy(labels_ref.at[mine], tags_ref.at[mine], label_recv.at[0]),
    ]

    @pl.when(below)
    def _():
        for copy in keep:
            copy.start()

    for i in range(PANELS):
        for half, group, source, target, width in share_segments(i):
            pltpu.make_async_copy(
                shares.at[:, half, pl.ds(group * 8, 8), pl.ds(source, width)],
                work.at[pl.ds(i * fronts, fronts), :, pl.ds(target, width)],
                unpack_sem,
            ).start()
    pltpu.make_async_copy(shares, shares, unpack_sem).wait()
    factor_pivots(me, work, bits_ref, inverse_ref, own_ref)

    results = [
        pltpu.make_async_copy(value, target, out_sems.at[i])
        for i, (value, target) in enumerate(
            ((bits_ref, bits_out), (inverse_ref, inverse_out), (own_ref, own_out))
        )
    ]
    for copy in results:
        copy.start()

    @pl.when(below)
    def _():
        for copy in keep:
            copy.wait()

    def landed(k, c):
        _, copies = ship(k)

        @pl.when(below)
        def _():
            for copy in copies:
                copy.wait_recv()

        return c

    lax.fori_loop(begun - AHEAD, devices, left, 0)
    lax.fori_loop(1, devices, landed, 0)
    wait_sent()
    for copy in results:
        copy.wait()


def factor_pivots(me, work, bits_ref, inverse_ref, own_ref):
    high = lax.Precision.HIGHEST

    def cols(i):
        return pl.ds(pl.multiple_of(i * PW, PW), PW)

    def load(i, j):
        return work[pl.ds(i * 32, 32), :, cols(j)].reshape(PW, PW)

    def panel(k, carry):
        top = pl.ds(k * 32, 16)
        low = pl.ds(k * 32 + 16, 16)
        left = pl.ds(pl.multiple_of(k * PW, TB), TB)
        right = pl.ds(pl.multiple_of(k * PW + TB, TB), TB)
        u1, w1 = chol_inv(work[top, :, left].reshape(TB, TB))
        l21 = dot_nt(work[low, :, left].reshape(TB, TB), w1, high)
        u2, w2 = chol_inv(work[low, :, right].reshape(TB, TB) - dot_nt(l21, l21, high))
        w21 = -dot_nn(w2, dot_nn(l21, w1, high), high)
        work[top, :, left] = u1.T.reshape(16, 8, TB)
        work[top, :, right] = jnp.zeros((16, 8, TB), jnp.float32)
        work[low, :, left] = l21.reshape(16, 8, TB)
        work[low, :, right] = u2.T.reshape(16, 8, TB)
        inverse_ref[k, :TB, :TB] = w1
        inverse_ref[k, :TB, TB:] = jnp.zeros((TB, TB), jnp.float32)
        inverse_ref[k, TB:, :TB] = w21
        inverse_ref[k, TB:, TB:] = w2

        def below(i, c):
            solved = dot_nt_split(load(i, k), inverse_ref[k])
            work[pl.ds(i * 32, 32), :, cols(k)] = solved.reshape(32, 8, PW)
            bits_ref[cols(i), cols(k)] = solved.astype(jnp.bfloat16)
            return c

        lax.fori_loop(k + 1, PANELS, below, 0)

        def column(j, c):
            def row(i, c2):
                term = dot_nt(bits_ref[cols(i), cols(k)], bits_ref[cols(j), cols(k)])
                work[pl.ds(i * 32, 32), :, cols(j)] -= term.reshape(32, 8, PW)
                return c2

            return lax.fori_loop(j, PANELS, row, c)

        lax.fori_loop(k + 1, PANELS, column, 0)
        return carry

    lax.fori_loop(0, PANELS, panel, 0)
    me = jnp.minimum(me, PANELS - 1)

    def out(j, c):
        own_ref[:, cols(j)] = jnp.where(j <= me, load(me, j), 0.0)
        return c

    lax.fori_loop(0, PANELS, out, 0)


def exchange(pick, front, tiles, labels):
    fronts = lax.axis_size("front")
    devices = labels.shape[0]
    order = PANELS * PW
    share = (2, PANELS // 2 * (PW // fronts), (PANELS + 1) * PW // 2)
    box = (devices, SLOTS * TB, TB)
    return pl.pallas_call(
        exchange_kernel,
        in_specs=[
            pl.BlockSpec(memory_space=pltpu.SMEM),
            pl.BlockSpec(memory_space=pl.ANY),
            pl.BlockSpec(memory_space=pl.ANY),
            pl.BlockSpec(memory_space=pltpu.VMEM),
        ],
        out_specs=[pl.BlockSpec(memory_space=pl.ANY)] * 5,
        out_shape=[
            jax.ShapeDtypeStruct((order, order), jnp.bfloat16),
            jax.ShapeDtypeStruct((PANELS, PW, PW), jnp.float32),
            jax.ShapeDtypeStruct((PW, order), jnp.float32),
            jax.ShapeDtypeStruct(box, jnp.bfloat16),
            jax.ShapeDtypeStruct(labels.shape, jnp.int32),
        ],
        scratch_shapes=[
            pltpu.VMEM((order, order), jnp.bfloat16),
            pltpu.VMEM((PANELS, PW, PW), jnp.float32),
            pltpu.VMEM((PW, order), jnp.float32),
            pltpu.VMEM((order // 8, 8, order), jnp.float32),
            pltpu.VMEM(tiles.shape, jnp.bfloat16),
            pltpu.VMEM(box, jnp.bfloat16),
            pltpu.VMEM(share, jnp.float32),
            pltpu.VMEM((fronts,) + share, jnp.float32),
            pltpu.SemaphoreType.DMA,
            pltpu.SemaphoreType.DMA,
            pltpu.SemaphoreType.DMA((3,)),
            pltpu.SemaphoreType.DMA((devices,)),
            pltpu.SemaphoreType.DMA((devices,)),
            pltpu.SemaphoreType.DMA((devices,)),
            pltpu.SemaphoreType.DMA((devices,)),
            pltpu.SemaphoreType.DMA((9,)),
            pltpu.SemaphoreType.DMA((2, fronts)),
        ]
        + RING_SEMS,
        compiler_params=pltpu.CompilerParams(
            collective_id=2, has_side_effects=True, vmem_limit_bytes=60 * MIB
        ),
        name="exchange_and_factor",
    )(pick, front, tiles, labels)


CHUNK = 16


def solve_kernel(
    tags_ref, me_ref, front_ref, inbox_ref, bits_in, inverse_in, own_in,
    factor_ref, rows_ref, rest_ref,
    work, landed, bits_ref, inverse_ref, own_ref, sems, rest_sem, late_sems,
):
    pivots = PANELS * PW
    count = inbox_ref.shape[0]
    chunks = count // CHUNK
    fill = pltpu.make_async_copy(front_ref, work, sems.at[chunks])
    fill.start()

    def fetch(c):
        part = pl.ds(c * CHUNK, CHUNK)
        return pltpu.make_async_copy(
            inbox_ref.at[part, pl.ds(0, SLOTS * TB)], landed.at[part], sems.at[c]
        )

    for c in range(chunks):
        fetch(c).start()
    late = [
        pltpu.make_async_copy(value, target, late_sems.at[i])
        for i, (value, target) in enumerate(
            ((bits_in, bits_ref), (inverse_in, inverse_ref), (own_in, own_ref))
        )
    ]
    for copy in late:
        copy.start()
    fill.wait()

    for c in range(chunks):
        fetch(c).wait()

        def add(i, carry):
            for s in range(SLOTS):
                code = tags_ref[i * SLOTS + s]

                @pl.when(code >= 0)
                def _():
                    place = (
                        pl.ds(pl.multiple_of((code // 64) * TB, TB), TB),
                        pl.ds(pl.multiple_of((code % 64) * TB, TB), TB),
                    )
                    work[place] += landed[i, s * TB : (s + 1) * TB].astype(jnp.float32)

            return carry

        lax.fori_loop(c * CHUNK, (c + 1) * CHUNK, add, 0)
    leave = pltpu.make_async_copy(work.at[:, pl.ds(pivots, rest_ref.shape[1])], rest_ref, rest_sem)
    leave.start()
    for copy in late:
        copy.wait()
    below = me_ref[0] >= PANELS
    for k in range(PANELS):
        at = slice(k * PW, (k + 1) * PW)
        current = work[:, at]
        if k:
            current = current - dot_nt(rows_ref[:, : k * PW], bits_ref[at, : k * PW])
        solved = dot_nt_split(current, inverse_ref[k])
        rows_ref[:, at] = solved.astype(jnp.bfloat16)
        factor_ref[:, at] = jnp.where(below, solved, own_ref[:, at])
    leave.wait()


def solve_rows(tags, me, front, inbox, bits, inverse, own):
    order = front.shape[1]
    pivots = PANELS * PW
    whole = lambda shape: pl.BlockSpec(shape, lambda i, t, m: (0,) * len(shape))
    count = inbox.shape[0]
    return pl.pallas_call(
        solve_kernel,
        grid_spec=pltpu.PrefetchScalarGridSpec(
            num_scalar_prefetch=2,
            grid=(1,),
            in_specs=[pl.BlockSpec(memory_space=pl.ANY)] * 5,
            out_specs=[
                whole((PW, pivots)),
                whole((PW, pivots)),
                pl.BlockSpec(memory_space=pl.ANY),
            ],
            scratch_shapes=[
                pltpu.VMEM((PW, order), jnp.float32),
                pltpu.VMEM((count, SLOTS * TB, TB), jnp.bfloat16),
                pltpu.VMEM(bits.shape, bits.dtype),
                pltpu.VMEM(inverse.shape, inverse.dtype),
                pltpu.VMEM(own.shape, own.dtype),
                pltpu.SemaphoreType.DMA((count // CHUNK + 1,)),
                pltpu.SemaphoreType.DMA,
                pltpu.SemaphoreType.DMA((3,)),
            ],
        ),
        out_shape=[
            jax.ShapeDtypeStruct((PW, pivots), jnp.float32),
            jax.ShapeDtypeStruct((PW, pivots), jnp.bfloat16),
            jax.ShapeDtypeStruct((PW, order - pivots), jnp.float32),
        ],
        compiler_params=pltpu.CompilerParams(vmem_limit_bytes=34 * MIB),
        name="solve_rows",
    )(tags, me, front, inbox, bits, inverse, own)


def on_device(front_matrix, child_tiles, tile_route, tile_row, tile_col):
    work = front_matrix[0]
    tiles = child_tiles[0]
    count = tiles.shape[0]
    groups = lax.axis_size("group")
    fronts = lax.axis_size("front")
    devices = groups * fronts
    tail = fronts - PANELS
    me = lax.axis_index("front")

    target = tile_route[0, :, 0]
    destination = target // tail * fronts + PANELS + target % tail
    label = tile_row[0] * 64 + tile_col[0]
    positions = jnp.arange(count, dtype=jnp.int32)
    meets = destination[None, :] == jnp.arange(devices, dtype=jnp.int32)[:, None]
    first = jnp.min(jnp.where(meets, positions[None, :], count), axis=1)
    last = jnp.max(jnp.where(meets, positions[None, :], -1), axis=1)
    pick = jnp.stack([jnp.where(first < count, first, 0), jnp.maximum(last, 0)], axis=1)
    here = positions[None, :] == first[:, None]
    label_first = jnp.max(jnp.where(here, label[None, :], -1), axis=1)
    here = (positions[None, :] == last[:, None]) & (last != first)[:, None]
    label_last = jnp.max(jnp.where(here, label[None, :], -1), axis=1)
    lane = jnp.arange(TB, dtype=jnp.int32)[None, :]
    labels = jnp.where(lane == 0, label_first[:, None], label_last[:, None])[:, None, :]
    bits, inverse, own, inbox, tags = exchange(
        pick.reshape(devices * SLOTS), work, tiles, labels
    )
    tags = jnp.where(me >= PANELS, tags[:, 0, :SLOTS], -1).reshape(devices * SLOTS)
    self = me.astype(jnp.int32).reshape(1)
    factor, rows, rest = solve_rows(tags, self, work, inbox, bits, inverse, own)
    schur = gather_schur(rows, rest)
    return (factor[None], schur[None])


def solution(mesh):
    return jax.shard_map(
        on_device,
        mesh=mesh,
        in_specs=(
            P("group", "front", None),
            P("group", "front", None, None),
            P("group", "front", None),
            P("group", "front"),
            P("group", "front"),
        ),
        out_specs=(P("group", "front", None), P("group", "front", None)),
        check_vma=False,
    )
```

```python
import functools

import jax
import jax.numpy as jnp
from jax import lax
from jax.experimental import pallas as pl
from jax.experimental.pallas import tpu as pltpu
from jax.sharding import PartitionSpec as P

PANELS = 6
PW = 256
TB = 128
SUB = 16
SLOTS = 2
AHEAD = 4
EARLY = 10
EACH = 1
STEPS = 22
MIB = 1 << 20


def dot_nt(a, b, precision=None):
    return lax.dot_general(
        a, b, (((1,), (1,)), ((), ())), precision=precision, preferred_element_type=jnp.float32
    )


def dot_nn(a, b, precision=None):
    return lax.dot_general(
        a, b, (((1,), (0,)), ((), ())), precision=precision, preferred_element_type=jnp.float32
    )


def halves(a):
    high = a.astype(jnp.bfloat16)
    low = (a - high.astype(jnp.float32)).astype(jnp.bfloat16)
    return high, low


def dot_tn_split(a, b):
    ah, al = halves(a)
    bh, bl = halves(b)
    left = jnp.concatenate([ah, ah, al], axis=0)
    right = jnp.concatenate([bh, bl, bh], axis=0)
    return lax.dot_general(
        left, right, (((0,), (0,)), ((), ())), preferred_element_type=jnp.float32
    )


def dot_nt_split(a, b):
    ah, al = halves(a)
    bh, bl = halves(b)
    left = jnp.concatenate([ah, ah, al], axis=1)
    right = jnp.concatenate([bh, bl, bh], axis=1)
    return dot_nt(left, right)


def dot_nn_split(a, b):
    ah, al = halves(a)
    bh, bl = halves(b)
    left = jnp.concatenate([ah, ah, al], axis=1)
    right = jnp.concatenate([bh, bl, bh], axis=0)
    return dot_nn(left, right)


def chol_inv(block):
    n = TB
    parts = SUB // 8
    lane = lax.broadcasted_iota(jnp.int32, (8, n), 1)
    sub = lax.broadcasted_iota(jnp.int32, (8, n), 0)
    rows = [block[8 * i : 8 * i + 8] for i in range(n // 8)]
    upper = []
    inverse = []
    for p in range(n // SUB):
        first = p * parts
        left = p * SUB
        panel = rows[first : first + parts]
        unit = [jnp.where(lane == sub + (left + 8 * h), 1.0, 0.0) for h in range(parts)]
        spread = [
            [jnp.broadcast_to(panel[h][:, left + j : left + j + 1], (8, n)) for h in range(parts)]
            for j in range(SUB)
        ]
        scale = [jnp.zeros((8, n), jnp.float32) for _ in range(parts)]
        for j in range(SUB):
            at, s = divmod(j, 8)
            inv = lax.rsqrt(jnp.broadcast_to(spread[j][at][s : s + 1], (8, n)))
            mult = [None] * parts
            for h in range(at, parts):
                mult[h] = spread[j][h] * inv
                if h == at:
                    mult[h] = jnp.where(sub > s, mult[h], 0.0)
            for target in [panel, unit] + spread[j + 1 :]:
                row = jnp.broadcast_to(target[at][s : s + 1], (8, n)) * inv
                for h in range(at, parts):
                    target[h] = target[h] - mult[h] * row
            scale[at] = jnp.where(sub == s, inv, scale[at])
        inside = (lane >= left) & (lane < left + SUB)
        ups = []
        full = []
        for h in range(parts):
            up = panel[h] * scale[h]
            mixed = jnp.where(inside, unit[h] * scale[h], up)
            inverse.append(jnp.where(lane < left + SUB, mixed, 0.0))
            upper.append(jnp.where(lane >= left, up, 0.0))
            ups.append(up)
            full.append(mixed)
        if left + SUB < n:
            ups = jnp.concatenate(ups, axis=0)
            full = jnp.concatenate(full, axis=0)
            change = dot_tn_split(ups[:, left + SUB :], full)
            for k, i in enumerate(range(first + parts, n // 8)):
                rows[i] = jnp.where(inside, 0.0, rows[i]) - change[8 * k : 8 * k + 8]
    return jnp.concatenate(upper, axis=0), jnp.concatenate(inverse, axis=0)


PLACES = {0: (1, 1, 5 * PW), 1: (0, 1, 4 * PW), 2: (0, 1, 0), 3: (1, 1, 0), 4: (1, 0, 0), 5: (0, 0, 0)}
PART = (PANELS + 1) * PW
SHARE_ROWS = 16


def sent_width(i):
    return PART if i == 4 else (i + 2) * PW


MESH = pl.DeviceIdType.MESH
SIDE = 4
SENDS = 64
MOVES = {"b+": (0, 3), "b-": (0, 1), "a+": (3, 0), "a-": (1, 0)}


def when(condition, action):
    if condition is None:
        action()
    else:
        pl.when(condition)(action)


class Ring:
    def __init__(self, skip):
        me = lax.axis_index("front")
        self.me = me
        self.core = me % 2
        x, y = (me // 2) % SIDE, me // (2 * SIDE)
        self.a = jnp.where(self.core == 0, y, x)
        self.b = jnp.where(self.core == 0, x, y)
        self.skip = skip
        self.sends = 0
        self.late = []
        self.peer = {"s": me + 1 - 2 * self.core}
        for name, (da, db) in MOVES.items():
            self.peer[name] = 2 * self.chip(SIDE - da, SIDE - db) + self.core

    def chip(self, da, db, other=False):
        core = 1 - self.core if other else self.core
        a, b = (self.b, self.a) if other else (self.a, self.b)
        a, b = (a + da) % SIDE, (b + db) % SIDE
        return jnp.where(core == 0, a * SIDE + b, b * SIDE + a)

    def live(self, da, db, other=False):
        return self.chip(da, db, other) * 2 >= self.skip if self.skip else None

    def greet(self):
        barrier = pltpu.get_barrier_semaphore()
        for peer in self.peer.values():
            pl.semaphore_signal(barrier, inc=1, device_id={"front": peer}, device_id_type=MESH)
        return barrier

    def gather(self, own, out, sems, after=None, taken=False, whole=False):
        ring_recv, side_recv, own_recv, local_sem, send_sem = sems
        core = self.core

        def piece(da, db, s, other=False):
            half = 1 - core if other else core
            chip = self.chip(da, db, other)
            if whole:
                return out.at[half, chip] if s is None else out.at[half, chip, s]
            if s is None:
                return out.at[pl.ds(2 * chip, 2), half]
            return out.at[2 * chip + s, half]

        def remote(source, target, recv, to, condition):
            k = self.sends
            self.sends += 1

            def make():
                return pltpu.make_async_remote_copy(
                    src_ref=source,
                    dst_ref=target,
                    send_sem=send_sem.at[k],
                    recv_sem=recv,
                    device_id={"front": self.peer[to]},
                    device_id_type=MESH,
                )

            when(condition, lambda: make().start())
            self.late.append((condition, lambda: make().wait_send()))

        def arrive(ref, sem, condition):
            def wait():
                pltpu.make_async_remote_copy(
                    src_ref=ref,
                    dst_ref=ref,
                    send_sem=send_sem.at[0],
                    recv_sem=sem,
                    device_id={"front": self.peer["s"]},
                    device_id_type=MESH,
                ).wait_recv()

            when(condition, wait)

        def give(da, db, s, to):
            ref = piece(da, db, s)
            at = 0 if s is None else s
            if to == "s":
                recv = side_recv.at[da, db, at]
            else:
                recv = ring_recv.at[(da + MOVES[to][0]) % SIDE, (db + MOVES[to][1]) % SIDE, at]
            remote(ref, ref, recv, to, self.live(da, db))

        here = self.live(0, 0)
        if whole:
            give(0, 0, None, "s")
        else:
            mine = pltpu.make_async_copy(own(core), piece(0, 0, core), local_sem.at[0])
            rest = pltpu.make_async_copy(own(1 - core), piece(0, 0, core, True), local_sem.at[1])
            when(here, mine.start)
            when(here, rest.start)
            remote(own(1 - core), piece(0, 0, core, True), own_recv.at[0], "s", here)
            remote(own(core), piece(0, 0, core), own_recv.at[1], "s", here)
            when(here, mine.wait)
            arrive(piece(0, 0, 1 - core), own_recv.at[0], here)
        for to in MOVES:
            give(0, 0, None, to)
        steps = [
            (0, 3, None, [(0, "b+"), (None, "a+"), (None, "a-")]),
            (0, 1, None, [(1, "b-"), (None, "a+"), (None, "a-")]),
            (3, 0, None, [(0, "a+")]),
            (1, 0, None, [(1, "a-")]),
            (0, 2, 0, [(0, "a+"), (0, "a-")]),
            (0, 2, 1, [(1, "a+"), (1, "a-")]),
            (3, 3, None, [(0, "a+")]),
            (1, 3, None, [(1, "a-")]),
            (3, 1, None, [(0, "a+")]),
            (1, 1, None, [(1, "a-")]),
            (2, 0, 0, []),
            (2, 0, 1, []),
            (3, 2, 0, [(0, "a+")]),
            (1, 2, 1, [(1, "a-")]),
            (3, 2, 1, []),
            (1, 2, 0, []),
            (2, 3, 0, []),
            (2, 3, 1, []),
            (2, 1, 0, []),
            (2, 1, 1, []),
            (2, 2, 0, []),
            (2, 2, 1, []),
        ]
        def take_own():
            if whole:
                return arrive(piece(0, 0, None, True), side_recv.at[0, 0, 0], here)
            arrive(piece(0, 0, 1 - core, True), own_recv.at[1], here)
            when(here, rest.wait)

        def take_side(da, db):
            parts = [s for at_a, at_b, s, _ in steps if (at_a, at_b) == (da, db)]
            for s in parts:
                arrive(
                    piece(da, db, s, True), side_recv.at[da, db, s or 0], self.live(da, db, True)
                )

        for number, (da, db, s, onward) in enumerate(steps):
            arrive(piece(da, db, s), ring_recv.at[da, db, s or 0], self.live(da, db))
            for part, to in onward:
                give(da, db, part, to)
            give(da, db, s, "s")
            if after is not None:
                after(number, take_own, take_side)
        if not taken:
            take_own()
            for da, db in UNITS[1:]:
                take_side(da, db)
        for condition, wait in self.late:
            when(condition, wait)


UNITS = [
    (0, 0), (0, 3), (0, 1), (3, 0), (1, 0), (0, 2), (3, 3), (1, 3),
    (3, 1), (1, 1), (2, 0), (3, 2), (1, 2), (2, 3), (2, 1), (2, 2),
]
BATCHES = {5: (0, 6, 0, 5), 9: (6, 10, 5, 8), 11: (10, 11, 8, 10), 15: (11, 13, 10, 11), 21: (13, 16, 11, 16)}


RING_SEMS = [
    pltpu.SemaphoreType.DMA((SIDE, SIDE, 2)),
    pltpu.SemaphoreType.DMA((SIDE, SIDE, 2)),
    pltpu.SemaphoreType.DMA((2,)),
    pltpu.SemaphoreType.DMA((2,)),
    pltpu.SemaphoreType.DMA((SENDS,)),
]


def schur_kernel(rows_ref, rest_ref, out_ref, gathered, rest_sem, *sems):
    ring = Ring(PANELS)
    pl.semaphore_wait(ring.greet(), len(ring.peer))
    below = ring.me >= PANELS
    fill = pltpu.make_async_copy(rest_ref, out_ref, rest_sem)

    @pl.when(below)
    def _():
        fill.start()

    @pl.when(jnp.logical_not(below))
    def _():
        out_ref[...] = jnp.zeros_like(out_ref)

    def after(step, take_own, take_side):
        if step not in BATCHES:
            return
        own_from, own_to, side_from, side_to = BATCHES[step]
        if own_from == 0:
            take_own()

            @pl.when(below)
            def _():
                fill.wait()

        for da, db in UNITS[max(side_from, 1) : side_to]:
            take_side(da, db)

        def use(n, c):
            side = n >= own_to - own_from
            at = jnp.where(side, n - (own_to - own_from) + side_from, n + own_from)
            da = sum(jnp.where(at == i, unit[0], 0) for i, unit in enumerate(UNITS))
            db = sum(jnp.where(at == i, unit[1], 0) for i, unit in enumerate(UNITS))
            chip = jnp.where(side, ring.chip(da, db, True), ring.chip(da, db))
            half = jnp.where(side, 1 - ring.core, ring.core)

            @pl.when(below & (chip * 2 >= PANELS))
            def _():
                unit = gathered[pl.ds(chip * 2, 2), half].reshape(PW, rows_ref.shape[1])
                term = dot_nt(rows_ref[...], unit)
                for core in range(2):
                    start = (chip * 2 + core - PANELS) * PW + half * TB
                    at_columns = pl.ds(pl.multiple_of(start, TB), TB)
                    out_ref[:, at_columns] -= term[:, core * TB : (core + 1) * TB]

            return c

        lax.fori_loop(0, own_to - own_from + side_to - side_from, use, 0)

    ring.gather(lambda h: rows_ref.at[pl.ds(h * TB, TB)], gathered, sems, after, taken=True)


def gather_schur(rows, rest):
    fronts = lax.axis_size("front")
    return pl.pallas_call(
        schur_kernel,
        in_specs=[
            pl.BlockSpec(memory_space=pltpu.VMEM),
            pl.BlockSpec(memory_space=pl.ANY),
        ],
        out_specs=pl.BlockSpec(memory_space=pltpu.VMEM),
        out_shape=jax.ShapeDtypeStruct(rest.shape, jnp.float32),
        scratch_shapes=[
            pltpu.VMEM((fronts, 2, TB, rows.shape[1]), jnp.bfloat16),
            pltpu.SemaphoreType.DMA,
        ]
        + RING_SEMS,
        compiler_params=pltpu.CompilerParams(
            collective_id=1, has_side_effects=True, vmem_limit_bytes=40 * MIB
        ),
        name="gather_schur",
    )(rows, rest)


def round_rows(me, staged, rounded):
    for i in range(PANELS):

        @pl.when(me == i)
        def _():
            width = (i + 1) * PW
            rounded[:, :width] = staged[:, :width].astype(jnp.bfloat16)
            diagonal = staged[:, i * PW : width]
            taken = diagonal - diagonal.astype(jnp.bfloat16).astype(jnp.float32)
            rounded[:, width : width + PW] = taken.astype(jnp.bfloat16)
            if sent_width(i) > width + PW:
                rounded[:, width + PW :] = jnp.zeros((PW, PW), jnp.bfloat16)


def deal_shares(ring, rounded, shares, deal_recv, deal_send):
    me = ring.me
    chips = shares.shape[1]

    def ends(i, chip):
        half, part, first = PLACES[i]
        rows = pl.ds(pl.multiple_of(chip * SHARE_ROWS, SHARE_ROWS), SHARE_ROWS)
        return (
            rounded.at[rows, pl.ds(0, sent_width(i))],
            shares.at[half, chip, part, :, pl.ds(first, sent_width(i))],
        )

    def far(i, chip):
        source, target = ends(i, chip)
        return pltpu.make_async_remote_copy(
            src_ref=source,
            dst_ref=target,
            send_sem=deal_send.at[chip],
            recv_sem=deal_recv.at[i],
            device_id={"front": 2 * chip + PLACES[i][0]},
            device_id_type=MESH,
        )

    def near(i):
        return pltpu.make_async_copy(*ends(i, me // 2), deal_recv.at[i])

    def each(i, action):
        def one(chip, c):
            @pl.when(2 * chip + PLACES[i][0] != me)
            def _():
                action(far(i, chip))

            return c

        lax.fori_loop(0, chips, one, 0)

    for i in range(PANELS):

        @pl.when(me == i)
        def _():
            each(i, lambda copy: copy.start())
            if PLACES[i][0] == i % 2:
                near(i).start()

    def wait_share():
        for i in range(PANELS):
            takes = ring.core == PLACES[i][0]

            @pl.when(takes & (me != i))
            def _():
                far(i, me // 2).wait_recv()

            if PLACES[i][0] == i % 2:

                @pl.when(me == i)
                def _():
                    near(i).wait()

    def wait_sent():
        for i in range(PANELS):

            @pl.when(me == i)
            def _():
                each(i, lambda copy: copy.wait_send())

    return wait_share, wait_sent


def exchange_kernel(
    pick_ref, front_ref, tiles_ref, labels_ref,
    bits_out, inverse_out, own_out, inbox_ref, tags_ref,
    bits_ref, inverse_ref, own_ref, work, tiles, outbox, staged, rounded, shares,
    tile_sem, stage_sem, out_sems, ship_send, ship_recv, label_send, label_recv,
    deal_recv, deal_send, *sems,
):
    devices = inbox_ref.shape[0]
    fronts = 2 * shares.shape[1]
    tail = fronts - PANELS
    ring = Ring(0)
    me = ring.me
    mine = lax.axis_index("group") * fronts + me
    fetch = pltpu.make_async_copy(tiles_ref, tiles, tile_sem)
    fetch.start()
    stage = pltpu.make_async_copy(front_ref.at[:, pl.ds(0, PANELS * PW)], staged, stage_sem)
    pl.when(me < PANELS)(stage.start)

    def where_is(device):
        return {"group": device // fronts, "front": device % fronts}

    barrier = pltpu.get_barrier_semaphore()

    def greet(k, c):
        other = where_is((mine + k) % devices)
        pl.semaphore_signal(barrier, inc=1, device_id=other, device_id_type=MESH)
        return c

    lax.fori_loop(1, devices, greet, 0)
    pl.when(me < PANELS)(stage.wait)
    round_rows(me, staged, rounded)
    pl.semaphore_wait(barrier, devices - 1)
    wait_share, wait_sent = deal_shares(ring, rounded, shares, deal_recv, deal_send)

    fetch.wait()

    def pack(i, c):
        device = i // tail * fronts + PANELS + i % tail
        for s in range(SLOTS):
            outbox[device, s * TB : (s + 1) * TB] = tiles[pick_ref[device * SLOTS + s]]
        return c

    lax.fori_loop(0, devices // fronts * tail, pack, 0)
    def ship(k):
        device = (mine + k * 59) % devices
        return device % fronts >= PANELS, [
            pltpu.make_async_remote_copy(
                src_ref=source.at[device],
                dst_ref=target.at[mine],
                send_sem=send_sem.at[k],
                recv_sem=recv_sem.at[k],
                device_id=where_is(device),
                device_id_type=MESH,
            )
            for source, target, send_sem, recv_sem in (
                (outbox, inbox_ref, ship_send, ship_recv),
                (labels_ref, tags_ref, label_send, label_recv),
            )
        ]

    def start(k, c):
        live, copies = ship(k)

        @pl.when(live)
        def _():
            for copy in copies:
                copy.start()

        return c

    def left(k, c):
        live, copies = ship(k)

        @pl.when(live)
        def _():
            for copy in copies:
                copy.wait_send()

        return c

    def pace(k, c):
        start(k, c)
        return left(k - AHEAD, c)

    lax.fori_loop(1, 1 + AHEAD, start, 0)
    begun = 1 + AHEAD + EARLY
    lax.fori_loop(1 + AHEAD, begun, pace, 0)

    def after(step, take_own, take_side):
        lax.fori_loop(begun + step * EACH, begun + (step + 1) * EACH, pace, 0)

    wait_share()
    ring.gather(None, shares, sems, after, whole=True)
    begun = begun + STEPS * EACH

    lax.fori_loop(begun, devices, start, 0)
    below = me >= PANELS
    keep = [
        pltpu.make_async_copy(outbox.at[mine], inbox_ref.at[mine], ship_recv.at[0]),
        pltpu.make_async_copy(labels_ref.at[mine], tags_ref.at[mine], label_recv.at[0]),
    ]

    @pl.when(below)
    def _():
        for copy in keep:
            copy.start()

    def unpack(chip, c):
        for i in range(PANELS):
            half, part, first = PLACES[i]
            width = (i + 1) * PW
            rows = pl.ds(i * fronts + 2 * chip, 2)

            def take(start, count):
                value = shares[half, chip, part, :, start : start + count].astype(jnp.float32)
                return value.reshape(2, 8, count)

            work[rows, :, :width] = take(first, width)
            work[rows, :, i * PW : width] += take(first + width, PW)
        return c

    lax.fori_loop(0, fronts // 2, unpack, 0)
    factor_pivots(me, work, bits_ref, inverse_ref, own_ref)

    results = [
        pltpu.make_async_copy(value, target, out_sems.at[i])
        for i, (value, target) in enumerate(
            ((bits_ref, bits_out), (inverse_ref, inverse_out), (own_ref, own_out))
        )
    ]
    for copy in results:
        copy.start()

    @pl.when(below)
    def _():
        for copy in keep:
            copy.wait()

    def landed(k, c):
        _, copies = ship(k)

        @pl.when(below)
        def _():
            for copy in copies:
                copy.wait_recv()

        return c

    lax.fori_loop(begun - AHEAD, devices, left, 0)
    lax.fori_loop(1, devices, landed, 0)
    wait_sent()
    for copy in results:
        copy.wait()


def factor_pivots(me, work, bits_ref, inverse_ref, own_ref):
    high = lax.Precision.HIGHEST

    def cols(i):
        return pl.ds(pl.multiple_of(i * PW, PW), PW)

    def load(i, j):
        return work[pl.ds(i * 32, 32), :, cols(j)].reshape(PW, PW)

    def panel(k, carry):
        top = pl.ds(k * 32, 16)
        low = pl.ds(k * 32 + 16, 16)
        left = pl.ds(pl.multiple_of(k * PW, TB), TB)
        right = pl.ds(pl.multiple_of(k * PW + TB, TB), TB)
        u1, w1 = chol_inv(work[top, :, left].reshape(TB, TB))
        l21 = dot_nt(work[low, :, left].reshape(TB, TB), w1, high)
        u2, w2 = chol_inv(work[low, :, right].reshape(TB, TB) - dot_nt(l21, l21, high))
        w21 = -dot_nn(w2, dot_nn(l21, w1, high), high)
        work[top, :, left] = u1.T.reshape(16, 8, TB)
        work[top, :, right] = jnp.zeros((16, 8, TB), jnp.float32)
        work[low, :, left] = l21.reshape(16, 8, TB)
        work[low, :, right] = u2.T.reshape(16, 8, TB)
        inverse_ref[k, :TB, :TB] = w1
        inverse_ref[k, :TB, TB:] = jnp.zeros((TB, TB), jnp.float32)
        inverse_ref[k, TB:, :TB] = w21
        inverse_ref[k, TB:, TB:] = w2

        def below(i, c):
            solved = dot_nt_split(load(i, k), inverse_ref[k])
            work[pl.ds(i * 32, 32), :, cols(k)] = solved.reshape(32, 8, PW)
            bits_ref[cols(i), cols(k)] = solved.astype(jnp.bfloat16)
            return c

        lax.fori_loop(k + 1, PANELS, below, 0)

        def column(j, c):
            def row(i, c2):
                term = dot_nt(bits_ref[cols(i), cols(k)], bits_ref[cols(j), cols(k)])
                work[pl.ds(i * 32, 32), :, cols(j)] -= term.reshape(32, 8, PW)
                return c2

            return lax.fori_loop(j, PANELS, row, c)

        lax.fori_loop(k + 1, PANELS, column, 0)
        return carry

    lax.fori_loop(0, PANELS, panel, 0)
    me = jnp.minimum(me, PANELS - 1)

    def out(j, c):
        own_ref[:, cols(j)] = jnp.where(j <= me, load(me, j), 0.0)
        return c

    lax.fori_loop(0, PANELS, out, 0)


def exchange(pick, front, tiles, labels):
    fronts = lax.axis_size("front")
    devices = labels.shape[0]
    order = PANELS * PW
    box = (devices, SLOTS * TB, TB)
    return pl.pallas_call(
        exchange_kernel,
        in_specs=[
            pl.BlockSpec(memory_space=pltpu.SMEM),
            pl.BlockSpec(memory_space=pl.ANY),
            pl.BlockSpec(memory_space=pl.ANY),
            pl.BlockSpec(memory_space=pltpu.VMEM),
        ],
        out_specs=[pl.BlockSpec(memory_space=pl.ANY)] * 5,
        out_shape=[
            jax.ShapeDtypeStruct((order, order), jnp.bfloat16),
            jax.ShapeDtypeStruct((PANELS, PW, PW), jnp.float32),
            jax.ShapeDtypeStruct((PW, order), jnp.float32),
            jax.ShapeDtypeStruct(box, jnp.bfloat16),
            jax.ShapeDtypeStruct(labels.shape, jnp.int32),
        ],
        scratch_shapes=[
            pltpu.VMEM((order, order), jnp.bfloat16),
            pltpu.VMEM((PANELS, PW, PW), jnp.float32),
            pltpu.VMEM((PW, order), jnp.float32),
            pltpu.VMEM((order // 8, 8, order), jnp.float32),
            pltpu.VMEM(tiles.shape, jnp.bfloat16),
            pltpu.VMEM(box, jnp.bfloat16),
            pltpu.VMEM((PW, order), jnp.float32),
            pltpu.VMEM((PW, PART), jnp.bfloat16),
            pltpu.VMEM((2, fronts // 2, 2, SHARE_ROWS, PART), jnp.bfloat16),
            pltpu.SemaphoreType.DMA,
            pltpu.SemaphoreType.DMA,
            pltpu.SemaphoreType.DMA((3,)),
            pltpu.SemaphoreType.DMA((devices,)),
            pltpu.SemaphoreType.DMA((devices,)),
            pltpu.SemaphoreType.DMA((devices,)),
            pltpu.SemaphoreType.DMA((devices,)),
            pltpu.SemaphoreType.DMA((PANELS,)),
            pltpu.SemaphoreType.DMA((fronts // 2,)),
        ]
        + RING_SEMS,
        compiler_params=pltpu.CompilerParams(
            collective_id=2, has_side_effects=True, vmem_limit_bytes=60 * MIB
        ),
        name="exchange_and_factor",
    )(pick, front, tiles, labels)


CHUNK = 16


def solve_kernel(
    tags_ref, me_ref, front_ref, inbox_ref, bits_in, inverse_in, own_in,
    factor_ref, rows_ref, rest_ref,
    work, landed, bits_ref, inverse_ref, own_ref, sems, rest_sem, late_sems,
):
    pivots = PANELS * PW
    count = inbox_ref.shape[0]
    chunks = count // CHUNK
    fill = pltpu.make_async_copy(front_ref, work, sems.at[chunks])
    fill.start()

    def fetch(c):
        part = pl.ds(c * CHUNK, CHUNK)
        return pltpu.make_async_copy(
            inbox_ref.at[part, pl.ds(0, SLOTS * TB)], landed.at[part], sems.at[c]
        )

    for c in range(chunks):
        fetch(c).start()
    late = [
        pltpu.make_async_copy(value, target, late_sems.at[i])
        for i, (value, target) in enumerate(
            ((bits_in, bits_ref), (inverse_in, inverse_ref), (own_in, own_ref))
        )
    ]
    for copy in late:
        copy.start()
    fill.wait()

    for c in range(chunks):
        fetch(c).wait()

        def add(i, carry):
            for s in range(SLOTS):
                code = tags_ref[i * SLOTS + s]

                @pl.when(code >= 0)
                def _():
                    place = (
                        pl.ds(pl.multiple_of((code // 64) * TB, TB), TB),
                        pl.ds(pl.multiple_of((code % 64) * TB, TB), TB),
                    )
                    work[place] += landed[i, s * TB : (s + 1) * TB].astype(jnp.float32)

            return carry

        lax.fori_loop(c * CHUNK, (c + 1) * CHUNK, add, 0)
    leave = pltpu.make_async_copy(work.at[:, pl.ds(pivots, rest_ref.shape[1])], rest_ref, rest_sem)
    leave.start()
    for copy in late:
        copy.wait()
    below = me_ref[0] >= PANELS
    for k in range(PANELS):
        at = slice(k * PW, (k + 1) * PW)
        current = work[:, at]
        if k:
            current = current - dot_nt(rows_ref[:, : k * PW], bits_ref[at, : k * PW])
        solved = dot_nt_split(current, inverse_ref[k])
        rows_ref[:, at] = solved.astype(jnp.bfloat16)
        factor_ref[:, at] = jnp.where(below, solved, own_ref[:, at])
    leave.wait()


def solve_rows(tags, me, front, inbox, bits, inverse, own):
    order = front.shape[1]
    pivots = PANELS * PW
    whole = lambda shape: pl.BlockSpec(shape, lambda i, t, m: (0,) * len(shape))
    count = inbox.shape[0]
    return pl.pallas_call(
        solve_kernel,
        grid_spec=pltpu.PrefetchScalarGridSpec(
            num_scalar_prefetch=2,
            grid=(1,),
            in_specs=[pl.BlockSpec(memory_space=pl.ANY)] * 5,
            out_specs=[
                whole((PW, pivots)),
                whole((PW, pivots)),
                pl.BlockSpec(memory_space=pl.ANY),
            ],
            scratch_shapes=[
                pltpu.VMEM((PW, order), jnp.float32),
                pltpu.VMEM((count, SLOTS * TB, TB), jnp.bfloat16),
                pltpu.VMEM(bits.shape, bits.dtype),
                pltpu.VMEM(inverse.shape, inverse.dtype),
                pltpu.VMEM(own.shape, own.dtype),
                pltpu.SemaphoreType.DMA((count // CHUNK + 1,)),
                pltpu.SemaphoreType.DMA,
                pltpu.SemaphoreType.DMA((3,)),
            ],
        ),
        out_shape=[
            jax.ShapeDtypeStruct((PW, pivots), jnp.float32),
            jax.ShapeDtypeStruct((PW, pivots), jnp.bfloat16),
            jax.ShapeDtypeStruct((PW, order - pivots), jnp.float32),
        ],
        compiler_params=pltpu.CompilerParams(vmem_limit_bytes=34 * MIB),
        name="solve_rows",
    )(tags, me, front, inbox, bits, inverse, own)


def on_device(front_matrix, child_tiles, tile_route, tile_row, tile_col):
    work = front_matrix[0]
    tiles = child_tiles[0]
    count = tiles.shape[0]
    groups = lax.axis_size("group")
    fronts = lax.axis_size("front")
    devices = groups * fronts
    tail = fronts - PANELS
    me = lax.axis_index("front")

    target = tile_route[0, :, 0]
    destination = target // tail * fronts + PANELS + target % tail
    label = tile_row[0] * 64 + tile_col[0]
    positions = jnp.arange(count, dtype=jnp.int32)
    meets = destination[None, :] == jnp.arange(devices, dtype=jnp.int32)[:, None]
    first = jnp.min(jnp.where(meets, positions[None, :], count), axis=1)
    last = jnp.max(jnp.where(meets, positions[None, :], -1), axis=1)
    pick = jnp.stack([jnp.where(first < count, first, 0), jnp.maximum(last, 0)], axis=1)
    here = positions[None, :] == first[:, None]
    label_first = jnp.max(jnp.where(here, label[None, :], -1), axis=1)
    here = (positions[None, :] == last[:, None]) & (last != first)[:, None]
    label_last = jnp.max(jnp.where(here, label[None, :], -1), axis=1)
    lane = jnp.arange(TB, dtype=jnp.int32)[None, :]
    labels = jnp.where(lane == 0, label_first[:, None], label_last[:, None])[:, None, :]
    bits, inverse, own, inbox, tags = exchange(
        pick.reshape(devices * SLOTS), work, tiles, labels
    )
    tags = jnp.where(me >= PANELS, tags[:, 0, :SLOTS], -1).reshape(devices * SLOTS)
    self = me.astype(jnp.int32).reshape(1)
    factor, rows, rest = solve_rows(tags, self, work, inbox, bits, inverse, own)
    schur = gather_schur(rows, rest)
    return (factor[None], schur[None])


def solution(mesh):
    return jax.shard_map(
        on_device,
        mesh=mesh,
        in_specs=(
            P("group", "front", None),
            P("group", "front", None, None),
            P("group", "front", None),
            P("group", "front"),
            P("group", "front"),
        ),
        out_specs=(P("group", "front", None), P("group", "front", None)),
        check_vma=False,
    )
```

```python
import functools

import jax
import jax.numpy as jnp
from jax import lax
from jax.experimental import pallas as pl
from jax.experimental.pallas import tpu as pltpu
from jax.sharding import PartitionSpec as P

PANELS = 6
PW = 256
TB = 128
SUB = 16
SLOTS = 2
AHEAD = 4
EARLY = 10
EACH = 1
STEPS = 22
MIB = 1 << 20


def dot_nt(a, b, precision=None):
    return lax.dot_general(
        a, b, (((1,), (1,)), ((), ())), precision=precision, preferred_element_type=jnp.float32
    )


def dot_nn(a, b, precision=None):
    return lax.dot_general(
        a, b, (((1,), (0,)), ((), ())), precision=precision, preferred_element_type=jnp.float32
    )


def halves(a):
    high = a.astype(jnp.bfloat16)
    low = (a - high.astype(jnp.float32)).astype(jnp.bfloat16)
    return high, low


def dot_tn_split(a, b):
    ah, al = halves(a)
    bh, bl = halves(b)
    left = jnp.concatenate([ah, ah, al], axis=0)
    right = jnp.concatenate([bh, bl, bh], axis=0)
    return lax.dot_general(
        left, right, (((0,), (0,)), ((), ())), preferred_element_type=jnp.float32
    )


def dot_nt_split(a, b):
    ah, al = halves(a)
    bh, bl = halves(b)
    left = jnp.concatenate([ah, ah, al], axis=1)
    right = jnp.concatenate([bh, bl, bh], axis=1)
    return dot_nt(left, right)


def dot_nn_split(a, b):
    ah, al = halves(a)
    bh, bl = halves(b)
    left = jnp.concatenate([ah, ah, al], axis=1)
    right = jnp.concatenate([bh, bl, bh], axis=0)
    return dot_nn(left, right)


def chol_inv(block):
    n = TB
    parts = SUB // 8
    lane = lax.broadcasted_iota(jnp.int32, (8, n), 1)
    sub = lax.broadcasted_iota(jnp.int32, (8, n), 0)
    rows = [block[8 * i : 8 * i + 8] for i in range(n // 8)]
    upper = []
    inverse = []
    for p in range(n // SUB):
        first = p * parts
        left = p * SUB
        panel = rows[first : first + parts]
        unit = [jnp.where(lane == sub + (left + 8 * h), 1.0, 0.0) for h in range(parts)]
        spread = [
            [jnp.broadcast_to(panel[h][:, left + j : left + j + 1], (8, n)) for h in range(parts)]
            for j in range(SUB)
        ]
        scale = [jnp.zeros((8, n), jnp.float32) for _ in range(parts)]
        for j in range(SUB):
            at, s = divmod(j, 8)
            inv = lax.rsqrt(jnp.broadcast_to(spread[j][at][s : s + 1], (8, n)))
            mult = [None] * parts
            for h in range(at, parts):
                mult[h] = spread[j][h] * inv
                if h == at:
                    mult[h] = jnp.where(sub > s, mult[h], 0.0)
            for target in [panel, unit] + spread[j + 1 :]:
                row = jnp.broadcast_to(target[at][s : s + 1], (8, n)) * inv
                for h in range(at, parts):
                    target[h] = target[h] - mult[h] * row
            scale[at] = jnp.where(sub == s, inv, scale[at])
        inside = (lane >= left) & (lane < left + SUB)
        ups = []
        full = []
        for h in range(parts):
            up = panel[h] * scale[h]
            mixed = jnp.where(inside, unit[h] * scale[h], up)
            inverse.append(jnp.where(lane < left + SUB, mixed, 0.0))
            upper.append(jnp.where(lane >= left, up, 0.0))
            ups.append(up)
            full.append(mixed)
        if left + SUB < n:
            ups = jnp.concatenate(ups, axis=0)
            full = jnp.concatenate(full, axis=0)
            change = dot_tn_split(ups[:, left + SUB :], full)
            for k, i in enumerate(range(first + parts, n // 8)):
                rows[i] = jnp.where(inside, 0.0, rows[i]) - change[8 * k : 8 * k + 8]
    return jnp.concatenate(upper, axis=0), jnp.concatenate(inverse, axis=0)


PLACES = {0: (1, 1, 5 * PW), 1: (0, 1, 4 * PW), 2: (0, 1, 0), 3: (1, 1, 0), 4: (1, 0, 0), 5: (0, 0, 0)}
PART = (PANELS + 1) * PW
SHARE_ROWS = 16


def sent_width(i):
    return PART if i == 4 else (i + 2) * PW


MESH = pl.DeviceIdType.MESH
SIDE = 4
SENDS = 64
MOVES = {"b+": (0, 3), "b-": (0, 1), "a+": (3, 0), "a-": (1, 0)}


def when(condition, action):
    if condition is None:
        action()
    else:
        pl.when(condition)(action)


class Ring:
    def __init__(self, skip):
        me = lax.axis_index("front")
        self.me = me
        self.core = me % 2
        x, y = (me // 2) % SIDE, me // (2 * SIDE)
        self.a = jnp.where(self.core == 0, y, x)
        self.b = jnp.where(self.core == 0, x, y)
        self.skip = skip
        self.sends = 0
        self.late = []
        self.peer = {"s": me + 1 - 2 * self.core}
        for name, (da, db) in MOVES.items():
            self.peer[name] = 2 * self.chip(SIDE - da, SIDE - db) + self.core

    def chip(self, da, db, other=False):
        core = 1 - self.core if other else self.core
        a, b = (self.b, self.a) if other else (self.a, self.b)
        a, b = (a + da) % SIDE, (b + db) % SIDE
        return jnp.where(core == 0, a * SIDE + b, b * SIDE + a)

    def live(self, da, db, other=False):
        return self.chip(da, db, other) * 2 >= self.skip if self.skip else None

    def greet(self):
        barrier = pltpu.get_barrier_semaphore()
        for peer in self.peer.values():
            pl.semaphore_signal(barrier, inc=1, device_id={"front": peer}, device_id_type=MESH)
        return barrier

    def gather(self, own, out, sems, after=None, taken=False, whole=False):
        ring_recv, side_recv, own_recv, local_sem, send_sem = sems
        core = self.core

        def piece(da, db, s, other=False):
            half = 1 - core if other else core
            chip = self.chip(da, db, other)
            if whole:
                return out.at[half, chip] if s is None else out.at[half, chip, s]
            if s is None:
                return out.at[pl.ds(2 * chip, 2), half]
            return out.at[2 * chip + s, half]

        def remote(source, target, recv, to, condition):
            k = self.sends
            self.sends += 1

            def make():
                return pltpu.make_async_remote_copy(
                    src_ref=source,
                    dst_ref=target,
                    send_sem=send_sem.at[k],
                    recv_sem=recv,
                    device_id={"front": self.peer[to]},
                    device_id_type=MESH,
                )

            when(condition, lambda: make().start())
            self.late.append((condition, lambda: make().wait_send()))

        def arrive(ref, sem, condition):
            def wait():
                pltpu.make_async_remote_copy(
                    src_ref=ref,
                    dst_ref=ref,
                    send_sem=send_sem.at[0],
                    recv_sem=sem,
                    device_id={"front": self.peer["s"]},
                    device_id_type=MESH,
                ).wait_recv()

            when(condition, wait)

        def give(da, db, s, to):
            ref = piece(da, db, s)
            at = 0 if s is None else s
            if to == "s":
                recv = side_recv.at[da, db, at]
            else:
                recv = ring_recv.at[(da + MOVES[to][0]) % SIDE, (db + MOVES[to][1]) % SIDE, at]
            remote(ref, ref, recv, to, self.live(da, db))

        here = self.live(0, 0)
        if whole:
            give(0, 0, None, "s")
        else:
            mine = pltpu.make_async_copy(own(core), piece(0, 0, core), local_sem.at[0])
            rest = pltpu.make_async_copy(own(1 - core), piece(0, 0, core, True), local_sem.at[1])
            when(here, mine.start)
            when(here, rest.start)
            remote(own(1 - core), piece(0, 0, core, True), own_recv.at[0], "s", here)
            remote(own(core), piece(0, 0, core), own_recv.at[1], "s", here)
            when(here, mine.wait)
            arrive(piece(0, 0, 1 - core), own_recv.at[0], here)
        for to in MOVES:
            give(0, 0, None, to)
        steps = [
            (0, 3, None, [(0, "b+"), (None, "a+"), (None, "a-")]),
            (0, 1, None, [(1, "b-"), (None, "a+"), (None, "a-")]),
            (3, 0, None, [(0, "a+")]),
            (1, 0, None, [(1, "a-")]),
            (0, 2, 0, [(0, "a+"), (0, "a-")]),
            (0, 2, 1, [(1, "a+"), (1, "a-")]),
            (3, 3, None, [(0, "a+")]),
            (1, 3, None, [(1, "a-")]),
            (3, 1, None, [(0, "a+")]),
            (1, 1, None, [(1, "a-")]),
            (2, 0, 0, []),
            (2, 0, 1, []),
            (3, 2, 0, [(0, "a+")]),
            (1, 2, 1, [(1, "a-")]),
            (3, 2, 1, []),
            (1, 2, 0, []),
            (2, 3, 0, []),
            (2, 3, 1, []),
            (2, 1, 0, []),
            (2, 1, 1, []),
            (2, 2, 0, []),
            (2, 2, 1, []),
        ]
        def take_own():
            if whole:
                return arrive(piece(0, 0, None, True), side_recv.at[0, 0, 0], here)
            arrive(piece(0, 0, 1 - core, True), own_recv.at[1], here)
            when(here, rest.wait)

        def take_side(da, db):
            parts = [s for at_a, at_b, s, _ in steps if (at_a, at_b) == (da, db)]
            for s in parts:
                arrive(
                    piece(da, db, s, True), side_recv.at[da, db, s or 0], self.live(da, db, True)
                )

        for number, (da, db, s, onward) in enumerate(steps):
            arrive(piece(da, db, s), ring_recv.at[da, db, s or 0], self.live(da, db))
            for part, to in onward:
                give(da, db, part, to)
            give(da, db, s, "s")
            if after is not None:
                after(number, take_own, take_side)
        if not taken:
            take_own()
            for da, db in UNITS[1:]:
                take_side(da, db)
        for condition, wait in self.late:
            when(condition, wait)


UNITS = [
    (0, 0), (0, 3), (0, 1), (3, 0), (1, 0), (0, 2), (3, 3), (1, 3),
    (3, 1), (1, 1), (2, 0), (3, 2), (1, 2), (2, 3), (2, 1), (2, 2),
]
BATCHES = {5: (0, 6, 0, 5), 9: (6, 10, 5, 8), 11: (10, 11, 8, 10), 15: (11, 13, 10, 11), 17: (13, 14, 11, 12), 19: (14, 15, 12, 13), 21: (15, 16, 13, 16)}


RING_SEMS = [
    pltpu.SemaphoreType.DMA((SIDE, SIDE, 2)),
    pltpu.SemaphoreType.DMA((SIDE, SIDE, 2)),
    pltpu.SemaphoreType.DMA((2,)),
    pltpu.SemaphoreType.DMA((2,)),
    pltpu.SemaphoreType.DMA((SENDS,)),
]


def schur_kernel(rows_ref, rest_ref, out_ref, gathered, rest_sem, *sems):
    ring = Ring(PANELS)
    pl.semaphore_wait(ring.greet(), len(ring.peer))
    below = ring.me >= PANELS
    fill = pltpu.make_async_copy(rest_ref, out_ref, rest_sem)

    @pl.when(below)
    def _():
        fill.start()

    @pl.when(jnp.logical_not(below))
    def _():
        out_ref[...] = jnp.zeros_like(out_ref)

    def after(step, take_own, take_side):
        if step not in BATCHES:
            return
        own_from, own_to, side_from, side_to = BATCHES[step]
        if own_from == 0:
            take_own()

            @pl.when(below)
            def _():
                fill.wait()

        for da, db in UNITS[max(side_from, 1) : side_to]:
            take_side(da, db)

        def use(n, c):
            side = n >= own_to - own_from
            at = jnp.where(side, n - (own_to - own_from) + side_from, n + own_from)
            da = sum(jnp.where(at == i, unit[0], 0) for i, unit in enumerate(UNITS))
            db = sum(jnp.where(at == i, unit[1], 0) for i, unit in enumerate(UNITS))
            chip = jnp.where(side, ring.chip(da, db, True), ring.chip(da, db))
            half = jnp.where(side, 1 - ring.core, ring.core)

            @pl.when(below & (chip * 2 >= PANELS))
            def _():
                unit = gathered[pl.ds(chip * 2, 2), half].reshape(PW, rows_ref.shape[1])
                term = dot_nt(rows_ref[...], unit)
                for core in range(2):
                    start = (chip * 2 + core - PANELS) * PW + half * TB
                    at_columns = pl.ds(pl.multiple_of(start, TB), TB)
                    out_ref[:, at_columns] -= term[:, core * TB : (core + 1) * TB]

            return c

        lax.fori_loop(0, own_to - own_from + side_to - side_from, use, 0)

    ring.gather(lambda h: rows_ref.at[pl.ds(h * TB, TB)], gathered, sems, after, taken=True)


def gather_schur(rows, rest):
    fronts = lax.axis_size("front")
    return pl.pallas_call(
        schur_kernel,
        in_specs=[
            pl.BlockSpec(memory_space=pltpu.VMEM),
            pl.BlockSpec(memory_space=pl.ANY),
        ],
        out_specs=pl.BlockSpec(memory_space=pltpu.VMEM),
        out_shape=jax.ShapeDtypeStruct(rest.shape, jnp.float32),
        scratch_shapes=[
            pltpu.VMEM((fronts, 2, TB, rows.shape[1]), jnp.bfloat16),
            pltpu.SemaphoreType.DMA,
        ]
        + RING_SEMS,
        compiler_params=pltpu.CompilerParams(
            collective_id=1, has_side_effects=True, vmem_limit_bytes=40 * MIB
        ),
        name="gather_schur",
    )(rows, rest)


def round_rows(me, staged, rounded):
    for i in range(PANELS):

        @pl.when(me == i)
        def _():
            width = (i + 1) * PW
            rounded[:, :width] = staged[:, :width].astype(jnp.bfloat16)
            diagonal = staged[:, i * PW : width]
            taken = diagonal - diagonal.astype(jnp.bfloat16).astype(jnp.float32)
            rounded[:, width : width + PW] = taken.astype(jnp.bfloat16)
            if sent_width(i) > width + PW:
                rounded[:, width + PW :] = jnp.zeros((PW, PW), jnp.bfloat16)


def deal_shares(ring, rounded, shares, deal_recv, deal_send):
    me = ring.me
    chips = shares.shape[1]

    def ends(i, chip):
        half, part, first = PLACES[i]
        rows = pl.ds(pl.multiple_of(chip * SHARE_ROWS, SHARE_ROWS), SHARE_ROWS)
        return (
            rounded.at[rows, pl.ds(0, sent_width(i))],
            shares.at[half, chip, part, :, pl.ds(first, sent_width(i))],
        )

    def far(i, chip):
        source, target = ends(i, chip)
        return pltpu.make_async_remote_copy(
            src_ref=source,
            dst_ref=target,
            send_sem=deal_send.at[chip],
            recv_sem=deal_recv.at[i],
            device_id={"front": 2 * chip + PLACES[i][0]},
            device_id_type=MESH,
        )

    def near(i):
        return pltpu.make_async_copy(*ends(i, me // 2), deal_recv.at[i])

    def each(i, action):
        def one(chip, c):
            @pl.when(2 * chip + PLACES[i][0] != me)
            def _():
                action(far(i, chip))

            return c

        lax.fori_loop(0, chips, one, 0)

    for i in range(PANELS):

        @pl.when(me == i)
        def _():
            each(i, lambda copy: copy.start())
            if PLACES[i][0] == i % 2:
                near(i).start()

    def wait_share():
        for i in range(PANELS):
            takes = ring.core == PLACES[i][0]

            @pl.when(takes & (me != i))
            def _():
                far(i, me // 2).wait_recv()

            if PLACES[i][0] == i % 2:

                @pl.when(me == i)
                def _():
                    near(i).wait()

    def wait_sent():
        for i in range(PANELS):

            @pl.when(me == i)
            def _():
                each(i, lambda copy: copy.wait_send())

    return wait_share, wait_sent


def exchange_kernel(
    pick_ref, front_ref, tiles_ref, labels_ref,
    bits_out, inverse_out, own_out, inbox_ref, tags_ref,
    bits_ref, inverse_ref, own_ref, work, tiles, outbox, staged, rounded, shares,
    tile_sem, stage_sem, out_sems, ship_send, ship_recv, label_send, label_recv,
    deal_recv, deal_send, *sems,
):
    devices = inbox_ref.shape[0]
    fronts = 2 * shares.shape[1]
    tail = fronts - PANELS
    ring = Ring(0)
    me = ring.me
    mine = lax.axis_index("group") * fronts + me
    fetch = pltpu.make_async_copy(tiles_ref, tiles, tile_sem)
    fetch.start()
    stage = pltpu.make_async_copy(front_ref.at[:, pl.ds(0, PANELS * PW)], staged, stage_sem)
    pl.when(me < PANELS)(stage.start)

    def where_is(device):
        return {"group": device // fronts, "front": device % fronts}

    barrier = pltpu.get_barrier_semaphore()

    def greet(k, c):
        other = where_is((mine + k) % devices)
        pl.semaphore_signal(barrier, inc=1, device_id=other, device_id_type=MESH)
        return c

    lax.fori_loop(1, devices, greet, 0)
    pl.when(me < PANELS)(stage.wait)
    round_rows(me, staged, rounded)
    pl.semaphore_wait(barrier, devices - 1)
    wait_share, wait_sent = deal_shares(ring, rounded, shares, deal_recv, deal_send)

    fetch.wait()

    def pack(i, c):
        device = i // tail * fronts + PANELS + i % tail
        for s in range(SLOTS):
            outbox[device, s * TB : (s + 1) * TB] = tiles[pick_ref[device * SLOTS + s]]
        return c

    lax.fori_loop(0, devices // fronts * tail, pack, 0)
    def ship(k):
        device = (mine + k * 59) % devices
        return device % fronts >= PANELS, [
            pltpu.make_async_remote_copy(
                src_ref=source.at[device],
                dst_ref=target.at[mine],
                send_sem=send_sem.at[k],
                recv_sem=recv_sem.at[k],
                device_id=where_is(device),
                device_id_type=MESH,
            )
            for source, target, send_sem, recv_sem in (
                (outbox, inbox_ref, ship_send, ship_recv),
                (labels_ref, tags_ref, label_send, label_recv),
            )
        ]

    def start(k, c):
        live, copies = ship(k)

        @pl.when(live)
        def _():
            for copy in copies:
                copy.start()

        return c

    def left(k, c):
        live, copies = ship(k)

        @pl.when(live)
        def _():
            for copy in copies:
                copy.wait_send()

        return c

    def pace(k, c):
        start(k, c)
        return left(k - AHEAD, c)

    lax.fori_loop(1, 1 + AHEAD, start, 0)
    begun = 1 + AHEAD + EARLY
    lax.fori_loop(1 + AHEAD, begun, pace, 0)

    def after(step, take_own, take_side):
        lax.fori_loop(begun + step * EACH, begun + (step + 1) * EACH, pace, 0)

    wait_share()
    ring.gather(None, shares, sems, after, whole=True)
    begun = begun + STEPS * EACH

    lax.fori_loop(begun, devices, start, 0)
    below = me >= PANELS
    keep = [
        pltpu.make_async_copy(outbox.at[mine], inbox_ref.at[mine], ship_recv.at[0]),
        pltpu.make_async_copy(labels_ref.at[mine], tags_ref.at[mine], label_recv.at[0]),
    ]

    @pl.when(below)
    def _():
        for copy in keep:
            copy.start()

    def unpack(chip, c):
        for i in range(PANELS):
            half, part, first = PLACES[i]
            width = (i + 1) * PW
            rows = pl.ds(i * fronts + 2 * chip, 2)

            def take(start, count):
                value = shares[half, chip, part, :, start : start + count].astype(jnp.float32)
                return value.reshape(2, 8, count)

            work[rows, :, :width] = take(first, width)
            work[rows, :, i * PW : width] += take(first + width, PW)
        return c

    lax.fori_loop(0, fronts // 2, unpack, 0)
    factor_pivots(me, work, bits_ref, inverse_ref, own_ref)

    results = [
        pltpu.make_async_copy(value, target, out_sems.at[i])
        for i, (value, target) in enumerate(
            ((bits_ref, bits_out), (inverse_ref, inverse_out), (own_ref, own_out))
        )
    ]
    for copy in results:
        copy.start()

    @pl.when(below)
    def _():
        for copy in keep:
            copy.wait()

    def landed(k, c):
        _, copies = ship(k)

        @pl.when(below)
        def _():
            for copy in copies:
                copy.wait_recv()

        return c

    lax.fori_loop(begun - AHEAD, devices, left, 0)
    lax.fori_loop(1, devices, landed, 0)
    wait_sent()
    for copy in results:
        copy.wait()


def factor_pivots(me, work, bits_ref, inverse_ref, own_ref):
    high = lax.Precision.HIGHEST

    def cols(i):
        return pl.ds(pl.multiple_of(i * PW, PW), PW)

    def load(i, j):
        return work[pl.ds(i * 32, 32), :, cols(j)].reshape(PW, PW)

    def panel(k, carry):
        top = pl.ds(k * 32, 16)
        low = pl.ds(k * 32 + 16, 16)
        left = pl.ds(pl.multiple_of(k * PW, TB), TB)
        right = pl.ds(pl.multiple_of(k * PW + TB, TB), TB)
        u1, w1 = chol_inv(work[top, :, left].reshape(TB, TB))
        l21 = dot_nt(work[low, :, left].reshape(TB, TB), w1, high)
        u2, w2 = chol_inv(work[low, :, right].reshape(TB, TB) - dot_nt(l21, l21, high))
        w21 = -dot_nn(w2, dot_nn(l21, w1, high), high)
        work[top, :, left] = u1.T.reshape(16, 8, TB)
        work[top, :, right] = jnp.zeros((16, 8, TB), jnp.float32)
        work[low, :, left] = l21.reshape(16, 8, TB)
        work[low, :, right] = u2.T.reshape(16, 8, TB)
        inverse_ref[k, :TB, :TB] = w1
        inverse_ref[k, :TB, TB:] = jnp.zeros((TB, TB), jnp.float32)
        inverse_ref[k, TB:, :TB] = w21
        inverse_ref[k, TB:, TB:] = w2

        def below(i, c):
            solved = dot_nt_split(load(i, k), inverse_ref[k])
            work[pl.ds(i * 32, 32), :, cols(k)] = solved.reshape(32, 8, PW)
            bits_ref[cols(i), cols(k)] = solved.astype(jnp.bfloat16)
            return c

        lax.fori_loop(k + 1, PANELS, below, 0)

        def column(j, c):
            def row(i, c2):
                term = dot_nt(bits_ref[cols(i), cols(k)], bits_ref[cols(j), cols(k)])
                work[pl.ds(i * 32, 32), :, cols(j)] -= term.reshape(32, 8, PW)
                return c2

            return lax.fori_loop(j, PANELS, row, c)

        lax.fori_loop(k + 1, PANELS, column, 0)
        return carry

    lax.fori_loop(0, PANELS, panel, 0)
    me = jnp.minimum(me, PANELS - 1)

    def out(j, c):
        own_ref[:, cols(j)] = jnp.where(j <= me, load(me, j), 0.0)
        return c

    lax.fori_loop(0, PANELS, out, 0)


def exchange(pick, front, tiles, labels):
    fronts = lax.axis_size("front")
    devices = labels.shape[0]
    order = PANELS * PW
    box = (devices, SLOTS * TB, TB)
    return pl.pallas_call(
        exchange_kernel,
        in_specs=[
            pl.BlockSpec(memory_space=pltpu.SMEM),
            pl.BlockSpec(memory_space=pl.ANY),
            pl.BlockSpec(memory_space=pl.ANY),
            pl.BlockSpec(memory_space=pltpu.VMEM),
        ],
        out_specs=[pl.BlockSpec(memory_space=pl.ANY)] * 5,
        out_shape=[
            jax.ShapeDtypeStruct((order, order), jnp.bfloat16),
            jax.ShapeDtypeStruct((PANELS, PW, PW), jnp.float32),
            jax.ShapeDtypeStruct((PW, order), jnp.float32),
            jax.ShapeDtypeStruct(box, jnp.bfloat16),
            jax.ShapeDtypeStruct(labels.shape, jnp.int32),
        ],
        scratch_shapes=[
            pltpu.VMEM((order, order), jnp.bfloat16),
            pltpu.VMEM((PANELS, PW, PW), jnp.float32),
            pltpu.VMEM((PW, order), jnp.float32),
            pltpu.VMEM((order // 8, 8, order), jnp.float32),
            pltpu.VMEM(tiles.shape, jnp.bfloat16),
            pltpu.VMEM(box, jnp.bfloat16),
            pltpu.VMEM((PW, order), jnp.float32),
            pltpu.VMEM((PW, PART), jnp.bfloat16),
            pltpu.VMEM((2, fronts // 2, 2, SHARE_ROWS, PART), jnp.bfloat16),
            pltpu.SemaphoreType.DMA,
            pltpu.SemaphoreType.DMA,
            pltpu.SemaphoreType.DMA((3,)),
            pltpu.SemaphoreType.DMA((devices,)),
            pltpu.SemaphoreType.DMA((devices,)),
            pltpu.SemaphoreType.DMA((devices,)),
            pltpu.SemaphoreType.DMA((devices,)),
            pltpu.SemaphoreType.DMA((PANELS,)),
            pltpu.SemaphoreType.DMA((fronts // 2,)),
        ]
        + RING_SEMS,
        compiler_params=pltpu.CompilerParams(
            collective_id=2, has_side_effects=True, vmem_limit_bytes=60 * MIB
        ),
        name="exchange_and_factor",
    )(pick, front, tiles, labels)


CHUNK = 16


def solve_kernel(
    tags_ref, me_ref, front_ref, inbox_ref, bits_in, inverse_in, own_in,
    factor_ref, rows_ref, rest_ref,
    work, landed, bits_ref, inverse_ref, own_ref, sems, rest_sem, late_sems,
):
    pivots = PANELS * PW
    count = inbox_ref.shape[0]
    chunks = count // CHUNK
    fill = pltpu.make_async_copy(front_ref, work, sems.at[chunks])
    fill.start()

    def fetch(c):
        part = pl.ds(c * CHUNK, CHUNK)
        return pltpu.make_async_copy(
            inbox_ref.at[part, pl.ds(0, SLOTS * TB)], landed.at[part], sems.at[c]
        )

    for c in range(chunks):
        fetch(c).start()
    late = [
        pltpu.make_async_copy(value, target, late_sems.at[i])
        for i, (value, target) in enumerate(
            ((bits_in, bits_ref), (inverse_in, inverse_ref), (own_in, own_ref))
        )
    ]
    for copy in late:
        copy.start()
    fill.wait()

    for c in range(chunks):
        fetch(c).wait()

        def add(i, carry):
            for s in range(SLOTS):
                code = tags_ref[i * SLOTS + s]

                @pl.when(code >= 0)
                def _():
                    place = (
                        pl.ds(pl.multiple_of((code // 64) * TB, TB), TB),
                        pl.ds(pl.multiple_of((code % 64) * TB, TB), TB),
                    )
                    work[place] += landed[i, s * TB : (s + 1) * TB].astype(jnp.float32)

            return carry

        lax.fori_loop(c * CHUNK, (c + 1) * CHUNK, add, 0)
    leave = pltpu.make_async_copy(work.at[:, pl.ds(pivots, rest_ref.shape[1])], rest_ref, rest_sem)
    leave.start()
    for copy in late:
        copy.wait()
    below = me_ref[0] >= PANELS
    for k in range(PANELS):
        at = slice(k * PW, (k + 1) * PW)
        current = work[:, at]
        if k:
            current = current - dot_nt(rows_ref[:, : k * PW], bits_ref[at, : k * PW])
        solved = dot_nt_split(current, inverse_ref[k])
        rows_ref[:, at] = solved.astype(jnp.bfloat16)
        factor_ref[:, at] = jnp.where(below, solved, own_ref[:, at])
    leave.wait()


def solve_rows(tags, me, front, inbox, bits, inverse, own):
    order = front.shape[1]
    pivots = PANELS * PW
    whole = lambda shape: pl.BlockSpec(shape, lambda i, t, m: (0,) * len(shape))
    count = inbox.shape[0]
    return pl.pallas_call(
        solve_kernel,
        grid_spec=pltpu.PrefetchScalarGridSpec(
            num_scalar_prefetch=2,
            grid=(1,),
            in_specs=[pl.BlockSpec(memory_space=pl.ANY)] * 5,
            out_specs=[
                whole((PW, pivots)),
                whole((PW, pivots)),
                pl.BlockSpec(memory_space=pl.ANY),
            ],
            scratch_shapes=[
                pltpu.VMEM((PW, order), jnp.float32),
                pltpu.VMEM((count, SLOTS * TB, TB), jnp.bfloat16),
                pltpu.VMEM(bits.shape, bits.dtype),
                pltpu.VMEM(inverse.shape, inverse.dtype),
                pltpu.VMEM(own.shape, own.dtype),
                pltpu.SemaphoreType.DMA((count // CHUNK + 1,)),
                pltpu.SemaphoreType.DMA,
                pltpu.SemaphoreType.DMA((3,)),
            ],
        ),
        out_shape=[
            jax.ShapeDtypeStruct((PW, pivots), jnp.float32),
            jax.ShapeDtypeStruct((PW, pivots), jnp.bfloat16),
            jax.ShapeDtypeStruct((PW, order - pivots), jnp.float32),
        ],
        compiler_params=pltpu.CompilerParams(vmem_limit_bytes=34 * MIB),
        name="solve_rows",
    )(tags, me, front, inbox, bits, inverse, own)


def on_device(front_matrix, child_tiles, tile_route, tile_row, tile_col):
    work = front_matrix[0]
    tiles = child_tiles[0]
    count = tiles.shape[0]
    groups = lax.axis_size("group")
    fronts = lax.axis_size("front")
    devices = groups * fronts
    tail = fronts - PANELS
    me = lax.axis_index("front")

    target = tile_route[0, :, 0]
    destination = target // tail * fronts + PANELS + target % tail
    label = tile_row[0] * 64 + tile_col[0]
    positions = jnp.arange(count, dtype=jnp.int32)
    meets = destination[None, :] == jnp.arange(devices, dtype=jnp.int32)[:, None]
    first = jnp.min(jnp.where(meets, positions[None, :], count), axis=1)
    last = jnp.max(jnp.where(meets, positions[None, :], -1), axis=1)
    pick = jnp.stack([jnp.where(first < count, first, 0), jnp.maximum(last, 0)], axis=1)
    here = positions[None, :] == first[:, None]
    label_first = jnp.max(jnp.where(here, label[None, :], -1), axis=1)
    here = (positions[None, :] == last[:, None]) & (last != first)[:, None]
    label_last = jnp.max(jnp.where(here, label[None, :], -1), axis=1)
    lane = jnp.arange(TB, dtype=jnp.int32)[None, :]
    labels = jnp.where(lane == 0, label_first[:, None], label_last[:, None])[:, None, :]
    bits, inverse, own, inbox, tags = exchange(
        pick.reshape(devices * SLOTS), work, tiles, labels
    )
    tags = jnp.where(me >= PANELS, tags[:, 0, :SLOTS], -1).reshape(devices * SLOTS)
    self = me.astype(jnp.int32).reshape(1)
    factor, rows, rest = solve_rows(tags, self, work, inbox, bits, inverse, own)
    schur = gather_schur(rows, rest)
    return (factor[None], schur[None])


def solution(mesh):
    return jax.shard_map(
        on_device,
        mesh=mesh,
        in_specs=(
            P("group", "front", None),
            P("group", "front", None, None),
            P("group", "front", None),
            P("group", "front"),
            P("group", "front"),
        ),
        out_specs=(P("group", "front", None), P("group", "front", None)),
        check_vma=False,
    )
```
